32 devices in a mesh: dp: 2 (over x), expert: 16 (over z, y, core).
Axes of the slice: x: 2, y: 2, z: 4, core: 2. Of those that a mesh axis runs over, the one named last changes fastest.
Arguments:
- tokens: bfloat16 [2048, 2048], P('expert'), may hold values from -6 to 6
- expert_ids: int32 [2048, 6], P('expert'), may hold values from 0 to 15, all different within a row; in each aligned block of 128 rows (0 to 127, 128 to 255, ...) at most 60 rows name the same one
- gates: float32 [2048, 6], P('expert'), may hold values from 0.05 to 0.5
- w_gate: bfloat16 [16, 2048, 1408], P('expert', None, 'dp'), may hold values from -0.125 to 0.125
- w_up: bfloat16 [16, 2048, 1408], P('expert', None, 'dp'), may hold values from -0.125 to 0.125
- w_down: bfloat16 [16, 1408, 2048], P('expert', 'dp'), may hold values from -0.15625 to 0.15625
- s_gate: bfloat16 [2048, 2816], P(None, 'dp'), may hold values from -0.125 to 0.125
- s_up: bfloat16 [2048, 2816], P(None, 'dp'), may hold values from -0.125 to 0.125
- s_down: bfloat16 [2816, 2048], P('dp'), may hold values from -0.109375 to 0.109375
- cotangent: bfloat16 [2048, 2048], P('expert'), may hold values from -6 to 6
Outputs:
- moe_out: bfloat16 [2048, 2048], P('expert')
- token_grads: bfloat16 [2048, 2048], P('expert')
- gate_grads: float32 [2048, 6], P('expert')
- grad_w_gate: bfloat16 [16, 2048, 1408], P('expert', None, 'dp')
- grad_w_up: bfloat16 [16, 2048, 1408], P('expert', None, 'dp')
- grad_w_down: bfloat16 [16, 1408, 2048], P('expert', 'dp')
- grad_s_gate: bfloat16 [2048, 2816], P('expert', 'dp')
- grad_s_up: bfloat16 [2048, 2816], P('expert', 'dp')
- grad_s_down: bfloat16 [2816, 2048], P('dp', 'expert')
The draws below stay inside these ranges and needn't reach their ends.
Inputs may be any that keep to these rules, and one draw needn't show every extreme that they name: `expert_ids`: each row names 6 different experts. In each aligned block of 128 rows (the rows of one index of the expert axis) no expert is named by more than 60 rows, and in some block one expert is named by exactly 60 rows.
All inputs are finite; a program needn't handle non-finite values.
Results may differ from the reference program's by a relative error of at most 0.02.
Values may be sent and summed in bfloat16 or wider, within the bound.
No kernel may reach another device: no remote copies, remote signals or barrier semaphores. Data moves between devices by JAX's collectives and lax.ppermute only.
A program may use at most 192 MiB of HBM per device.

```python
import math
import jax
import jax.numpy as jnp
import numpy as np
from jax import lax

D = 2048
FF = 1408
FS = 2816
TOP = 6
TOK_DEV = 128
EXPERTS = 16
TOKENS = 2048
CAP = 60
N_DP = 2
N_EXPERT = 16


def spiked(result, rng, source, target, shards_of, factor):
    def block_of(axis_at):
        return (jnp.arange(result.shape[axis_at]) // (result.shape[axis_at] // shards_of)).reshape((-1,) + (1,) * (result.ndim - 1 - axis_at))

    first = jax.random.permutation(rng, shards_of)[block_of(target)]
    other_side = (block_of(target) + shards_of // 2) % shards_of
    return jnp.where((block_of(source) == first) | (block_of(source) == other_side), factor * result, result)


def steps_of(key, dims, split, low, largest):
    def one(axis_at, parts):
        heights = jax.random.uniform(jax.random.fold_in(jax.random.fold_in(key, 6), axis_at), (parts,), jnp.float32, low / len(split), largest / len(split))
        return jnp.repeat(jnp.exp(heights), dims[axis_at] // parts).reshape((-1,) + (1,) * (len(dims) - axis_at - 1))

    factor_of = one(*split[0])
    for cut in split[1:]:
        factor_of = factor_of * one(*cut)
    return factor_of


def deal_out(key, own, number, rows, amount, top, limit, lean):
    sequence = jax.random.permutation(key, amount)
    heavy_load, common = shares(amount, rows * top, limit, lean, True), shares(amount, rows * top, limit, lean, False)
    places = jnp.arange(amount)

    def named(tallies, offset_by):
        used = int((tallies > 0).sum())
        fixed = max(1, used // 4)
        moved = fixed + (places - fixed + offset_by * (used - fixed)) % max(1, amount - fixed)
        return jnp.zeros((amount,), jnp.int32).at[sequence[jnp.where(places < fixed, places, moved)]].set(jnp.asarray(tallies, jnp.int32))

    tallies = jnp.where(number % 4 == 0, named(heavy_load, number // 4), named(common, number - number // 4 - 1))
    mixed = jax.random.permutation(jax.random.fold_in(own, 3), amount)
    source_of, sink = mixed[0:amount // 2 * 2:2], mixed[1:amount // 2 * 2:2]
    slack = jnp.minimum(tallies[source_of] - 1, limit - tallies[sink]) // 2
    slack = jnp.where((source_of == sequence[0]) | (sink == sequence[0]) | (tallies[sink] == 0), 0, jnp.maximum(slack, 0))
    moved = jax.random.randint(jax.random.fold_in(own, 4), (amount // 2,), 0, 1 << 20) % (slack + 1)
    tallies = tallies.at[source_of].add(-moved).at[sink].add(moved)
    members = jnp.searchsorted(jnp.cumsum(tallies), jnp.arange(rows * top), side="right").astype(jnp.int32)
    listing = members.reshape(top, rows).T
    listing = listing[jax.random.permutation(jax.random.fold_in(own, 1), rows)]
    offset_by = jax.random.randint(jax.random.fold_in(own, 2), (rows, 1), 0, top)
    return jnp.take_along_axis(listing, (jnp.arange(top)[None, :] + offset_by) % top, axis=1)


def shares(count, total, most, skew, full):
    portions = [(1 << 20) // math.isqrt(standing ** skew) + 1 for standing in range(1, count + 1)]
    largest = most if full else min(most, max(-(-total // count), total * portions[0] // sum(portions)))
    least = 1 if total - largest >= count - 1 else 0
    counts, rest = [largest] + [least] * (count - 1), total - largest - least * (count - 1)
    while rest > 0:
        free = [i for i in range(1, count) if counts[i] < largest] or [i for i in range(1, count) if counts[i] < most]
        pool, remaining = sum([portions[i] for i in free]), rest
        for i in free:
            extra = min(most - counts[i], max(1, remaining * portions[i] // pool), rest)
            counts[i] = counts[i] + extra
            rest = rest - extra
    return np.array(counts)


def centred(rng, dims, scale, limit, split=(), kind=jnp.bfloat16):
    values = jax.random.normal(rng, dims, jnp.float32) * scale
    if len(split) > 0:
        values = steps_of(rng, dims, split, -0.22, 0.18) * values
    return jnp.clip(values, min=-limit, max=limit).astype(kind)


def noise_with(key, extent, deviation, bound, cuts, heavy, held_as=jnp.bfloat16):
    drawn = deviation * jax.random.normal(key, extent, jnp.float32)
    if cuts:
        drawn = drawn * steps_of(key, extent, cuts, -0.22, 0.18)
    return jnp.clip(spiked(drawn, jax.random.fold_in(key, 3), *heavy), -bound, bound).astype(held_as)


def setup_inputs(seed: int = 0) -> dict:
    arg_keys = jax.random.split(jax.random.key(seed), 11)
    tokens = noise_with(arg_keys[0], (TOKENS, D), 1.0, 6.0, ((0, 16),), (0, 1, 16, 2.0))
    expert_ids_keys = jax.random.split(jax.random.fold_in(arg_keys[1], 1), TOKENS // TOK_DEV)
    expert_ids_turns = jax.random.permutation(jax.random.fold_in(arg_keys[1], 3), TOKENS // TOK_DEV)
    expert_ids = jax.vmap(lambda own, number: deal_out(jax.random.fold_in(arg_keys[1], 2), own, number, TOK_DEV, EXPERTS, TOP, CAP, 2))(expert_ids_keys, expert_ids_turns).reshape((TOKENS, TOP))
    gates = jnp.clip(jnp.exp(math.log(0.5) - 2.3025851 * jax.random.uniform(arg_keys[2], (TOKENS, TOP), jnp.float32) ** steps_of(arg_keys[2], (TOKENS, TOP), ((0, 16),), -0.2, 0.2)), 0.05, 0.5)
    w_gate = centred(arg_keys[3], (EXPERTS, D, FF), D ** -0.5, 0.125, ((0, 16), (2, 2)))
    w_up = centred(arg_keys[4], (EXPERTS, D, FF), D ** -0.5, 0.125, ((0, 16), (2, 2)))
    w_down = centred(arg_keys[5], (EXPERTS, FF, D), FF ** -0.5, 0.15625, ((0, 16), (1, 2)))
    s_gate = centred(arg_keys[6], (D, FS), D ** -0.5, 0.125, ((1, 2),))
    s_up = centred(arg_keys[7], (D, FS), D ** -0.5, 0.125, ((1, 2),))
    s_down = centred(arg_keys[8], (FS, D), FS ** -0.5, 0.109375, ((0, 2),))
    cotangent = noise_with(arg_keys[9], (TOKENS, D), 1.0, 6.0, ((0, 16),), (0, 1, 16, 2.0))
    return {"tokens": tokens, "expert_ids": expert_ids, "gates": gates, "w_gate": w_gate, "w_up": w_up, "w_down": w_down, "s_gate": s_gate, "s_up": s_up, "s_down": s_down, "cotangent": cotangent}


def contract_dims(left, right, left_dim, right_dim):
    return lax.dot_general(left, right, (((left_dim,), (right_dim,)), ((), ())), preferred_element_type=jnp.float32)


def reference(tokens, expert_ids, gates, w_gate, w_up, w_down, s_gate, s_up, s_down, cotangent):
    blocks = N_EXPERT
    pair_total = TOKENS * TOP
    slot_rows = blocks * CAP
    block_width = FF // N_DP
    flat_ids = expert_ids.reshape(blocks, TOK_DEV * TOP)
    onehot = (flat_ids[:, :, None] == jnp.arange(EXPERTS, dtype=jnp.int32)[None, None, :]).astype(jnp.int32)
    before = jnp.cumsum(onehot, axis=1) - onehot
    position = jnp.sum(before * onehot, axis=2)
    source = jnp.arange(blocks, dtype=jnp.int32)[:, None]
    dest_index = (flat_ids * slot_rows + source * CAP + position).reshape(pair_total)
    slot_table = jnp.full((EXPERTS * slot_rows,), pair_total, jnp.int32).at[dest_index].set(
        jnp.arange(pair_total, dtype=jnp.int32)).reshape(EXPERTS, slot_rows)
    zero_row = jnp.zeros((1, D), jnp.bfloat16)
    padded_tokens = jnp.concatenate([tokens, zero_row], axis=0)
    weights = gates.astype(jnp.float32)
    grad_rows = cotangent.astype(jnp.float32)
    scaled = (weights[:, :, None] * grad_rows[:, None, :]).astype(jnp.bfloat16).reshape(pair_total, D)
    padded_scaled = jnp.concatenate([scaled, zero_row], axis=0)

    def expert_step(totals, inputs):
        out_acc, dx_acc = totals
        row_index, gate_mat, up_mat, down_mat = inputs
        received = padded_tokens[row_index // TOP]
        received_grads = padded_scaled[row_index]
        gate_pre = jnp.dot(received, gate_mat, preferred_element_type=jnp.float32)
        up_pre = jnp.dot(received, up_mat, preferred_element_type=jnp.float32)
        gate_sigmoid = jax.nn.sigmoid(gate_pre)
        hidden = (gate_pre * gate_sigmoid * up_pre).astype(jnp.bfloat16)
        block_parts = jnp.einsum("rjf,jfe->rje",
                                 hidden.reshape(slot_rows, N_DP, block_width).astype(jnp.float32),
                                 down_mat.reshape(N_DP, block_width, D).astype(jnp.float32))
        rounded = lax.optimization_barrier(block_parts.astype(jnp.bfloat16))
        expert_out = jnp.sum(rounded.astype(jnp.float32), axis=1)
        hidden_grad = contract_dims(received_grads, down_mat, 1, 1)
        gate_grad_pre = (hidden_grad * up_pre * gate_sigmoid * (1.0 + gate_pre * (1.0 - gate_sigmoid))).astype(jnp.bfloat16)
        up_grad_pre = (hidden_grad * gate_pre * gate_sigmoid).astype(jnp.bfloat16)
        dx_parts = jnp.einsum("rjf,ejf->rje",
                              gate_grad_pre.reshape(slot_rows, N_DP, block_width).astype(jnp.float32),
                              gate_mat.reshape(D, N_DP, block_width).astype(jnp.float32))
        dx_parts = dx_parts + jnp.einsum("rjf,ejf->rje",
                                         up_grad_pre.reshape(slot_rows, N_DP, block_width).astype(jnp.float32),
                                         up_mat.reshape(D, N_DP, block_width).astype(jnp.float32))
        rounded_dx = lax.optimization_barrier(dx_parts.astype(jnp.bfloat16))
        expert_dx = jnp.sum(rounded_dx.astype(jnp.float32), axis=1)
        out_acc = out_acc.at[row_index].add(expert_out)
        dx_acc = dx_acc.at[row_index].add(expert_dx)
        expert_grads = (contract_dims(received, gate_grad_pre, 0, 0).astype(jnp.bfloat16),
                        contract_dims(received, up_grad_pre, 0, 0).astype(jnp.bfloat16),
                        contract_dims(hidden, received_grads, 0, 0).astype(jnp.bfloat16))
        return (out_acc, dx_acc), expert_grads

    start_totals = (jnp.zeros((pair_total + 1, D), jnp.float32), jnp.zeros((pair_total + 1, D), jnp.float32))
    (out_acc, dx_acc), expert_grads = lax.scan(expert_step, start_totals, (slot_table, w_gate, w_up, w_down))
    grad_w_gate, grad_w_up, grad_w_down = expert_grads
    pair_out = out_acc[:pair_total].reshape(TOKENS, TOP, D)

    shared_gate_pre = jnp.dot(tokens, s_gate, preferred_element_type=jnp.float32)
    shared_up_pre = jnp.dot(tokens, s_up, preferred_element_type=jnp.float32)
    shared_sigmoid = jax.nn.sigmoid(shared_gate_pre)
    shared_hidden = (shared_gate_pre * shared_sigmoid * shared_up_pre).astype(jnp.bfloat16)
    shared_out = jnp.dot(shared_hidden, s_down, preferred_element_type=jnp.float32)
    moe_out = (jnp.sum(weights[:, :, None] * pair_out, axis=1) + shared_out).astype(jnp.bfloat16)
    gate_grads = jnp.sum(grad_rows[:, None, :] * pair_out, axis=2)

    shared_hidden_grad = contract_dims(cotangent, s_down, 1, 1)
    shared_gate_grad = (shared_hidden_grad * shared_up_pre * shared_sigmoid
                        * (1.0 + shared_gate_pre * (1.0 - shared_sigmoid))).astype(jnp.bfloat16)
    shared_up_grad = (shared_hidden_grad * shared_gate_pre * shared_sigmoid).astype(jnp.bfloat16)
    shared_dx = contract_dims(shared_gate_grad, s_gate, 1, 1) + contract_dims(shared_up_grad, s_up, 1, 1)
    token_grads = (jnp.sum(dx_acc[:pair_total].reshape(TOKENS, TOP, D), axis=1) + shared_dx).astype(jnp.bfloat16)
    grad_s_gate = contract_dims(tokens, shared_gate_grad, 0, 0).astype(jnp.bfloat16)
    grad_s_up = contract_dims(tokens, shared_up_grad, 0, 0).astype(jnp.bfloat16)
    grad_s_down = contract_dims(shared_hidden, cotangent, 0, 0).astype(jnp.bfloat16)
    return (moe_out, token_grads, gate_grads, grad_w_gate, grad_w_up, grad_w_down, grad_s_gate, grad_s_up, grad_s_down)
```

```python
import jax
import jax.numpy as jnp
from jax import lax
from jax.sharding import PartitionSpec as P

F32 = jnp.float32
BF16 = jnp.bfloat16


def mm(left, right, left_dim, right_dim):
    return lax.dot_general(
        left, right, (((left_dim,), (right_dim,)), ((), ())), preferred_element_type=F32
    )


def gather_all(rows):
    dp = lax.axis_size("dp")
    share = rows.shape[0] // dp
    mine = lax.dynamic_slice_in_dim(rows, lax.axis_index("dp") * share, share, 0)
    return lax.all_gather(mine, ("expert", "dp"), axis=0, tiled=True)


def scatter_sum(partial):
    share = lax.psum_scatter(partial, ("expert", "dp"), scatter_dimension=0, tiled=True)
    return lax.all_gather(share, "dp", axis=0, tiled=True)


def routing(ids, gates, blocks, slots):
    tok = ids.shape[0] // blocks
    hit = ids == lax.axis_index("expert")
    taken = jnp.any(hit, axis=1).reshape(blocks, tok)
    gate = jnp.sum(jnp.where(hit, gates, 0.0), axis=1).reshape(blocks, tok)
    count = taken.astype(jnp.int32)
    position = jnp.cumsum(count, axis=1) - count
    position = jnp.where(taken, position, -1)
    pick = position[:, None, :] == jnp.arange(slots, dtype=jnp.int32)[None, :, None]
    slot_gate = jnp.sum(jnp.where(pick, gate[:, None, :], 0.0), axis=2)
    return pick.astype(BF16), slot_gate.reshape(blocks * slots, 1)


def take(pick, rows):
    blocks, slots, tok = pick.shape
    width = rows.shape[1]
    out = jnp.einsum(
        "bst,btd->bsd", pick, rows.reshape(blocks, tok, width), preferred_element_type=F32
    )
    return out.astype(BF16).reshape(blocks * slots, width)


def put(pick, rows):
    blocks, slots, tok = pick.shape
    width = rows.shape[1]
    out = jnp.einsum(
        "bst,bsd->btd", pick, rows.reshape(blocks, slots, width), preferred_element_type=F32
    )
    return out.reshape(blocks * tok, width)


def combine(pick, rows, left, right, pieces=4):
    blocks, slots, tok = pick.shape
    step = blocks // pieces
    rows = rows.reshape(blocks, slots, -1)
    out = []
    for i in range(pieces):
        cut = slice(i * step, (i + 1) * step)
        part = put(pick[cut], rows[cut].reshape(step * slots, -1))
        for a, b, dim in zip(left, right, (0,) if len(left) == 1 else (1, 1)):
            part = part + mm(a[i * step * tok : (i + 1) * step * tok], b, 1, dim)
        out.append(part.astype(BF16))
    return jnp.concatenate(out, axis=0)


def local(tokens, expert_ids, gates, w_gate, w_up, w_down, s_gate, s_up, s_down, cotangent):
    tok, width = tokens.shape
    top = expert_ids.shape[1]
    experts = lax.axis_size("expert")
    me = lax.axis_index("expert")
    capacity = min(tok, 5 * tok * top // (4 * experts))
    slots = -(-capacity // 16) * 16
    units = s_gate.shape[1] // experts

    info = jnp.concatenate([expert_ids.astype(F32), gates], axis=1)
    info_all = lax.all_gather(info, "expert", axis=0, tiled=True)
    x_all = gather_all(tokens)
    c_all = gather_all(cotangent)
    pick, slot_gate = routing(info_all[:, :top].astype(jnp.int32), info_all[:, top:], experts, slots)

    sg = lax.dynamic_slice_in_dim(s_gate, me * units, units, 1)
    su = lax.dynamic_slice_in_dim(s_up, me * units, units, 1)
    sd = lax.dynamic_slice_in_dim(s_down, me * units, units, 0)
    wg, wu, wd = w_gate[0], w_up[0], w_down[0]

    xr = take(pick, x_all)
    gate_pre = mm(xr, wg, 1, 0)
    up_pre = mm(xr, wu, 1, 0)
    sig = jax.nn.sigmoid(gate_pre)
    silu = gate_pre * sig
    hidden = silu * up_pre
    hidden_b = hidden.astype(BF16)
    sgate_pre = mm(x_all, sg, 1, 0)
    sup_pre = mm(x_all, su, 1, 0)
    ssig = jax.nn.sigmoid(sgate_pre)
    ssilu = sgate_pre * ssig
    shidden_b = (ssilu * sup_pre).astype(BF16)
    routed_out = (mm(hidden_b, wd, 1, 0) * slot_gate).astype(BF16)
    out_part = combine(pick, routed_out, (shidden_b,), (sd,))
    moe_out = scatter_sum(out_part)

    cr = take(pick, c_all)
    raw = mm(cr, wd, 1, 1)
    score = jnp.sum(raw * hidden_b.astype(F32), axis=1, keepdims=True)
    hgrad = raw * slot_gate
    ggp = (hgrad * up_pre * sig * (1.0 + gate_pre * (1.0 - sig))).astype(BF16)
    ugp = (hgrad * silu).astype(BF16)
    shgrad = mm(c_all, sd, 1, 1)
    sgg = (shgrad * sup_pre * ssig * (1.0 + sgate_pre * (1.0 - ssig))).astype(BF16)
    sug = (shgrad * ssilu).astype(BF16)
    routed_dx = (mm(ggp, wg, 1, 1) + mm(ugp, wu, 1, 1)).astype(BF16)
    dx_part = combine(pick, routed_dx, (sgg, sug), (sg, su))
    token_grads = scatter_sum(dx_part)

    score_tok = jnp.sum(
        pick.astype(F32) * score.reshape(experts, slots, 1), axis=1
    )
    high = score_tok.astype(BF16)
    low = (score_tok - high.astype(F32)).astype(BF16)
    grads = jnp.concatenate([mm(sgg, x_all, 0, 0), mm(sug, x_all, 0, 0), mm(shidden_b, c_all, 0, 0)], axis=0)
    grads = grads.astype(BF16).reshape(3 * units, experts, width // experts)
    block = grads.shape[2]
    lines = -(-tok // block)
    extra = jnp.stack([high, low], axis=0)
    extra = jnp.pad(extra, ((0, 0), (0, 0), (0, lines * block - tok)))
    extra = extra.reshape(2, experts, lines, block).transpose(0, 2, 1, 3)
    extra = extra.reshape(2 * lines, experts, block)
    send = jnp.concatenate([grads, extra], axis=0).transpose(1, 0, 2)
    got = lax.all_to_all(send, "expert", split_axis=0, concat_axis=0, tiled=True)
    grad_sg = got[:, :units].reshape(experts * units, -1).T
    grad_su = got[:, units : 2 * units].reshape(experts * units, -1).T
    grad_sd = got[:, 2 * units : 3 * units].reshape(experts * units, -1)
    scores = got[:, 3 * units :].reshape(experts, 2, lines * block)[:, :, :tok].astype(F32)
    scores = scores[:, 0] + scores[:, 1]
    hit = expert_ids[:, :, None] == jnp.arange(experts, dtype=jnp.int32)[None, None, :]
    mine = jnp.sum(jnp.where(hit, scores.T[:, None, :], 0.0), axis=2)
    gate_grads = lax.psum(mine, "dp")

    cs = (cr.astype(F32) * slot_gate).astype(BF16)
    grad_wg = mm(xr, ggp, 0, 0).astype(BF16)[None]
    grad_wu = mm(xr, ugp, 0, 0).astype(BF16)[None]
    grad_wd = mm(hidden_b, cs, 0, 0).astype(BF16)[None]
    return (moe_out, token_grads, gate_grads, grad_wg, grad_wu, grad_wd, grad_sg, grad_su, grad_sd)


def solution(mesh):
    row = P("expert", None)
    cols = P("expert", None, "dp")
    return jax.shard_map(
        local,
        mesh=mesh,
        in_specs=(
            row, row, row, cols, cols, P("expert", "dp", None),
            P(None, "dp"), P(None, "dp"), P("dp", None), row,
        ),
        out_specs=(
            row, row, row, cols, cols, P("expert", "dp", None),
            P("expert", "dp"), P("expert", "dp"), P("dp", "expert"),
        ),
        check_vma=False,
    )
```

```python
import jax
import jax.numpy as jnp
import numpy as np
from jax import lax
from jax.sharding import PartitionSpec as P

F32 = jnp.float32
BF16 = jnp.bfloat16


def mm(left, right, left_dim, right_dim):
    return lax.dot_general(
        left, right, (((left_dim,), (right_dim,)), ((), ())), preferred_element_type=F32
    )


def split_of(experts, dp):
    bits = experts.bit_length() - 1
    middle = (bits - 1) // 2
    return (2, 1 << middle, 1 << (bits - 1 - middle), dp)


def partner(array, sizes, dim, k):
    if dim == 3:
        axis, mask = "dp", k
    else:
        axis, mask = "expert", k * (1, 2, 2 * sizes[1])[dim]
    return lax.ppermute(array, axis, [(i, i ^ mask) for i in range(lax.axis_size(axis))])


def gather_all(rows, sizes, order):
    out = rows.reshape((1, 1, 1, 1) + rows.shape)
    for dim in order:
        out = jnp.concatenate(
            [out] + [partner(out, sizes, dim, k) for k in range(1, sizes[dim])], axis=dim
        )
    return out


def total(terms):
    out = terms[0].astype(F32)
    for term in terms[1:]:
        out = out + term.astype(F32)
    return out.astype(BF16)


def scatter_sum(partial, sizes, order):
    terms = [partial]
    for dim in order:
        cut = lambda k: [lax.slice_in_dim(t, k, k + 1, axis=dim) for t in terms]
        came = [partner(total(cut(k)), sizes, dim, k) for k in range(1, sizes[dim])]
        terms = cut(0) + came
    return total(terms).reshape(partial.shape[4:])


def both_halves(rows, sizes):
    out = [rows] + [partner(rows, sizes, 3, k) for k in range(1, sizes[3])]
    out = jnp.stack(out)
    order = jnp.arange(sizes[3]) ^ lax.axis_index("dp")
    return out[order].reshape(-1, rows.shape[1])


def routing(ids, gates, blocks, slots):
    tok = ids.shape[0] // blocks
    hit = ids == lax.axis_index("expert")
    taken = jnp.any(hit, axis=1).reshape(blocks, tok)
    gate = jnp.sum(jnp.where(hit, gates, 0.0), axis=1).reshape(blocks, tok)
    count = taken.astype(jnp.int32)
    position = jnp.cumsum(count, axis=1) - count
    position = jnp.where(taken, position, -1)
    pick = position[:, None, :] == jnp.arange(slots, dtype=jnp.int32)[None, :, None]
    slot_gate = jnp.sum(jnp.where(pick, gate[:, None, :], 0.0), axis=2)
    return pick.astype(BF16), slot_gate.reshape(blocks * slots, 1)


def take(pick, rows):
    blocks, slots, tok = pick.shape
    width = rows.shape[1]
    out = jnp.einsum(
        "bst,btd->bsd", pick, rows.reshape(blocks, tok, width), preferred_element_type=F32
    )
    return out.astype(BF16).reshape(blocks * slots, width)


def put(pick, rows):
    blocks, slots, tok = pick.shape
    width = rows.shape[1]
    out = jnp.einsum(
        "bst,bsd->btd", pick, rows.reshape(blocks, slots, width), preferred_element_type=F32
    )
    return out.reshape(blocks * tok, width)


def combine(pick, rows, left, right):
    out = put(pick, rows)
    for a, b in zip(left, right):
        out = out + mm(a, b, 1, 0)
    return out.astype(BF16)


def local(tokens, expert_ids, gates, w_gate, w_up, w_down, s_gate, s_up, s_down, cotangent):
    tok, width = tokens.shape
    top = expert_ids.shape[1]
    experts = lax.axis_size("expert")
    me = lax.axis_index("expert")
    capacity = min(tok, 5 * tok * top // (4 * experts))
    slots = -(-capacity // 16) * 16
    units = s_gate.shape[1] // experts

    info = jnp.concatenate([expert_ids.astype(F32), gates], axis=1)
    info_all = lax.all_gather(info, "expert", axis=0, tiled=True)
    dp = lax.axis_size("dp")
    my_dp = lax.axis_index("dp")
    share = tok // dp
    sizes = split_of(experts, dp)
    half = width // 2
    orders = ((2, 3, 1, 0), (2, 1, 3, 0))

    def whole(rows):
        mine = lax.dynamic_slice_in_dim(rows, my_dp * share, share, 0)
        parts = [gather_all(mine[:, i * half : (i + 1) * half], sizes, orders[i]) for i in range(2)]
        return jnp.concatenate(parts, axis=5).reshape(experts * tok, width)

    def summed(parts):
        shape = sizes + (share, half)
        out = [scatter_sum(p.reshape(shape), sizes, o[::-1]) for p, o in zip(parts, orders)]
        return both_halves(jnp.concatenate(out, axis=1), sizes)

    index = np.arange(experts).reshape(sizes[2], sizes[1], 2).transpose(2, 1, 0).reshape(-1)
    blocks_at = me ^ jnp.asarray(index, jnp.int32)
    shares_at = my_dp ^ jnp.arange(dp, dtype=jnp.int32)
    info_all = info_all.reshape(experts, dp, share, 2 * top)[blocks_at][:, shares_at]
    info_all = info_all.reshape(experts * tok, 2 * top)
    x_all = whole(tokens)
    c_all = whole(cotangent)
    pick, slot_gate = routing(info_all[:, :top].astype(jnp.int32), info_all[:, top:], experts, slots)

    sg = lax.dynamic_slice_in_dim(s_gate, me * units, units, 1)
    su = lax.dynamic_slice_in_dim(s_up, me * units, units, 1)
    sd = lax.dynamic_slice_in_dim(s_down, me * units, units, 0)
    wg, wu, wd = w_gate[0], w_up[0], w_down[0]

    xr = take(pick, x_all)
    gate_pre = mm(xr, wg, 1, 0)
    up_pre = mm(xr, wu, 1, 0)
    sig = jax.nn.sigmoid(gate_pre)
    silu = gate_pre * sig
    hidden = silu * up_pre
    hidden_b = hidden.astype(BF16)
    sgate_pre = mm(x_all, sg, 1, 0)
    sup_pre = mm(x_all, su, 1, 0)
    ssig = jax.nn.sigmoid(sgate_pre)
    ssilu = sgate_pre * ssig
    shidden_b = (ssilu * sup_pre).astype(BF16)
    out_part = []
    for i in range(2):
        cut = slice(i * half, (i + 1) * half)
        routed_out = (mm(hidden_b, wd[:, cut], 1, 0) * slot_gate).astype(BF16)
        out_part.append(combine(pick, routed_out, (shidden_b,), (sd[:, cut],)))
    moe_out = summed(out_part)

    cr = take(pick, c_all)
    raw = mm(cr, wd, 1, 1)
    score = jnp.sum(raw * hidden_b.astype(F32), axis=1, keepdims=True)
    hgrad = raw * slot_gate
    ggp = (hgrad * up_pre * sig * (1.0 + gate_pre * (1.0 - sig))).astype(BF16)
    ugp = (hgrad * silu).astype(BF16)
    shgrad = mm(c_all, sd, 1, 1)
    sgg = (shgrad * sup_pre * ssig * (1.0 + sgate_pre * (1.0 - ssig))).astype(BF16)
    sug = (shgrad * ssilu).astype(BF16)
    dx_part = []
    for i in range(2):
        cut = slice(i * half, (i + 1) * half)
        routed_dx = (mm(ggp, wg[cut], 1, 1) + mm(ugp, wu[cut], 1, 1)).astype(BF16)
        dx_part.append(combine(pick, routed_dx, (sgg, sug), (sg[cut].T, su[cut].T)))
    token_grads = summed(dx_part)

    score_tok = jnp.sum(
        pick.astype(F32) * score.reshape(experts, slots, 1), axis=1
    )
    score_tok = jnp.zeros((experts, dp, share), F32).at[blocks_at].set(score_tok.reshape(experts, dp, share))
    score_tok = score_tok[:, shares_at].reshape(experts, tok)
    high = score_tok.astype(BF16)
    low = (score_tok - high.astype(F32)).astype(BF16)
    grads = jnp.concatenate([mm(sgg, x_all, 0, 0), mm(sug, x_all, 0, 0), mm(shidden_b, c_all, 0, 0)], axis=0)
    grads = grads.astype(BF16).reshape(3 * units, experts, width // experts)
    block = grads.shape[2]
    lines = -(-tok // block)
    extra = jnp.stack([high, low], axis=0)
    extra = jnp.pad(extra, ((0, 0), (0, 0), (0, lines * block - tok)))
    extra = extra.reshape(2, experts, lines, block).transpose(0, 2, 1, 3)
    extra = extra.reshape(2 * lines, experts, block)
    send = jnp.concatenate([grads, extra], axis=0).transpose(1, 0, 2)
    got = lax.all_to_all(send, "expert", split_axis=0, concat_axis=0, tiled=True)
    grad_sg = got[:, :units].reshape(experts * units, -1).T
    grad_su = got[:, units : 2 * units].reshape(experts * units, -1).T
    grad_sd = got[:, 2 * units : 3 * units].reshape(experts * units, -1)
    scores = got[:, 3 * units :].reshape(experts, 2, lines * block)[:, :, :tok].astype(F32)
    scores = scores[:, 0] + scores[:, 1]
    hit = expert_ids[:, :, None] == jnp.arange(experts, dtype=jnp.int32)[None, None, :]
    mine = jnp.sum(jnp.where(hit, scores.T[:, None, :], 0.0), axis=2)
    gate_grads = lax.psum(mine, "dp")

    cs = (cr.astype(F32) * slot_gate).astype(BF16)
    grad_wg = mm(xr, ggp, 0, 0).astype(BF16)[None]
    grad_wu = mm(xr, ugp, 0, 0).astype(BF16)[None]
    grad_wd = mm(hidden_b, cs, 0, 0).astype(BF16)[None]
    return (moe_out, token_grads, gate_grads, grad_wg, grad_wu, grad_wd, grad_sg, grad_su, grad_sd)


def solution(mesh):
    row = P("expert", None)
    cols = P("expert", None, "dp")
    return jax.shard_map(
        local,
        mesh=mesh,
        in_specs=(
            row, row, row, cols, cols, P("expert", "dp", None),
            P(None, "dp"), P(None, "dp"), P("dp", None), row,
        ),
        out_specs=(
            row, row, row, cols, cols, P("expert", "dp", None),
            P("expert", "dp"), P("expert", "dp"), P("dp", "expert"),
        ),
        check_vma=False,
    )
```

```python
import functools

import jax
import jax.numpy as jnp
import numpy as np
from jax import lax
from jax.experimental import pallas as pl
from jax.experimental.pallas import tpu as pltpu
from jax.sharding import PartitionSpec as P

F32 = jnp.float32
BF16 = jnp.bfloat16
GROUP = 4
VMEM_LIMIT = 56 * 1024 * 1024


def mm(left, right, left_dim, right_dim):
    return lax.dot_general(
        left, right, (((left_dim,), (right_dim,)), ((), ())), preferred_element_type=F32
    )


def split_of(experts, dp):
    bits = experts.bit_length() - 1
    middle = (bits - 1) // 2
    return (2, 1 << middle, 1 << (bits - 1 - middle), dp)


def partner(array, sizes, dim, k):
    if dim == 3:
        axis, mask = "dp", k
    else:
        axis, mask = "expert", k * (1, 2, 2 * sizes[1])[dim]
    return lax.ppermute(array, axis, [(i, i ^ mask) for i in range(lax.axis_size(axis))])


def gather_dims(rows, sizes, order):
    out = rows.reshape((1, 1, 1, 1) + rows.shape)
    for dim in order:
        out = jnp.concatenate(
            [out] + [partner(out, sizes, dim, k) for k in range(1, sizes[dim])], axis=dim
        )
    return out


def total(terms):
    out = terms[0].astype(F32)
    for term in terms[1:]:
        out = out + term.astype(F32)
    return out.astype(BF16)


def scatter_sum(own, other, sizes, order):
    terms = [own, partner(other, sizes, 0, 1)]
    for dim in order:
        cut = lambda k: [lax.slice_in_dim(t, k, k + 1, axis=dim) for t in terms]
        came = [partner(total(cut(k)), sizes, dim, k) for k in range(1, sizes[dim])]
        terms = cut(0) + came
    return total(terms).reshape(own.shape[4:])


def both_halves(rows, sizes):
    out = [rows] + [partner(rows, sizes, 3, k) for k in range(1, sizes[3])]
    out = jnp.stack(out)
    order = jnp.arange(sizes[3]) ^ lax.axis_index("dp")
    return out[order].reshape(-1, rows.shape[1])


def pick_of(place_ref, gate_ref, block, slots):
    place = place_ref[0, block : block + 1, :]
    hit = lax.broadcasted_iota(jnp.int32, (slots, place.shape[1]), 0) == place
    gate = jnp.sum(jnp.where(hit, gate_ref[0, block : block + 1, :], 0.0), axis=1, keepdims=True)
    return hit, gate


def take_rows(hits, a_ref, b_ref, tok):
    rows = []
    for block, hit in enumerate(hits):
        cut = slice(block * tok, (block + 1) * tok)
        hit = hit.astype(BF16)
        rows.append(
            jnp.concatenate(
                [mm(hit, ref[cut, :], 1, 0).astype(BF16) for ref in (a_ref, b_ref)], axis=1
            )
        )
    return jnp.concatenate(rows, axis=0)


def put_rows(hits, rows, extra, a_ref, b_ref, slots, tok):
    half = a_ref.shape[1]
    for block, hit in enumerate(hits):
        cut = slice(block * tok, (block + 1) * tok)
        part = mm(hit.astype(BF16), rows[block * slots : (block + 1) * slots, :], 0, 0)
        part = part + extra[cut, :]
        a_ref[cut, :] = part[:, :half].astype(BF16)
        b_ref[cut, :] = part[:, half:].astype(BF16)


def forward_kernel(
    slots, tok, place_ref, gate_ref, xa_ref, xb_ref, wg_ref, wu_ref, wd_ref, sgu_ref, sd_ref,
    oa_ref, ob_ref, xr_ref, gp_ref, up_ref, hid_ref, spre_ref, shid_ref,
):
    picks = [pick_of(place_ref, gate_ref, i, slots) for i in range(GROUP)]
    hits = [p[0] for p in picks]
    gate = jnp.concatenate([p[1] for p in picks], axis=0)
    half = xa_ref.shape[1]
    unit = sd_ref.shape[0]
    xr = take_rows(hits, xa_ref, xb_ref, tok)
    xr_ref[...] = xr
    gp = mm(xr, wg_ref[0], 1, 0)
    up = mm(xr, wu_ref[0], 1, 0)
    gp_ref[...] = gp
    up_ref[...] = up
    hid = (gp * jax.nn.sigmoid(gp) * up).astype(BF16)
    hid_ref[...] = hid
    rows = (mm(hid, wd_ref[0], 1, 0) * gate).astype(BF16)
    spre = mm(xa_ref[...], sgu_ref[:half, :], 1, 0) + mm(xb_ref[...], sgu_ref[half:, :], 1, 0)
    spre_ref[...] = spre
    sgp, sup = spre[:, :unit], spre[:, unit:]
    shid = (sgp * jax.nn.sigmoid(sgp) * sup).astype(BF16)
    shid_ref[...] = shid
    put_rows(hits, rows, mm(shid, sd_ref[...], 1, 0), oa_ref, ob_ref, slots, tok)


def backward_kernel(
    slots, tok, place_ref, gate_ref, ca_ref, cb_ref, wg_ref, wu_ref, wd_ref, sgu_ref, sd_ref,
    gp_ref, up_ref, spre_ref,
    oa_ref, ob_ref, cs_ref, ggp_ref, ugp_ref, sgrad_ref, score_ref,
):
    picks = [pick_of(place_ref, gate_ref, i, slots) for i in range(GROUP)]
    hits = [p[0] for p in picks]
    gate = jnp.concatenate([p[1] for p in picks], axis=0)
    half = ca_ref.shape[1]
    unit = sd_ref.shape[0]
    cr = take_rows(hits, ca_ref, cb_ref, tok)
    cs_ref[...] = (cr.astype(F32) * gate).astype(BF16)
    raw = mm(cr, wd_ref[0], 1, 1)
    gp, up = gp_ref[...], up_ref[...]
    sig = jax.nn.sigmoid(gp)
    silu = gp * sig
    score = jnp.sum(raw * (silu * up).astype(BF16).astype(F32), axis=1, keepdims=True)
    for block, hit in enumerate(hits):
        part = jnp.where(hit, score[block * slots : (block + 1) * slots, :], 0.0)
        score_ref[0, block : block + 1, :] = jnp.sum(part, axis=0, keepdims=True)
    grad = raw * gate
    ggp = (grad * up * sig * (1.0 + gp * (1.0 - sig))).astype(BF16)
    ugp = (grad * silu).astype(BF16)
    ggp_ref[...] = ggp
    ugp_ref[...] = ugp
    rows = (mm(ggp, wg_ref[0], 1, 1) + mm(ugp, wu_ref[0], 1, 1)).astype(BF16)
    sgp, sup = spre_ref[:, :unit], spre_ref[:, unit:]
    ssig = jax.nn.sigmoid(sgp)
    sgrad = mm(ca_ref[...], sd_ref[:, :half], 1, 1) + mm(cb_ref[...], sd_ref[:, half:], 1, 1)
    sgg = (sgrad * sup * ssig * (1.0 + sgp * (1.0 - ssig))).astype(BF16)
    sug = (sgrad * sgp * ssig).astype(BF16)
    both = jnp.concatenate([sgg, sug], axis=1)
    sgrad_ref[...] = both
    put_rows(hits, rows, mm(both, sgu_ref[...], 1, 1), oa_ref, ob_ref, slots, tok)


def spec_rows(rows, width):
    return pl.BlockSpec((rows, width), lambda i: (i, 0))


def spec_info(tok):
    return pl.BlockSpec((1, GROUP, tok), lambda i: (i, 0, 0))


def spec_whole(array):
    return pl.BlockSpec(array.shape, lambda i: (0,) * array.ndim, pipeline_mode=pl.Buffered(1))


def cost(flops, arrays):
    return pl.CostEstimate(
        flops=int(flops),
        bytes_accessed=int(sum(np.prod(a.shape) * a.dtype.itemsize for a in arrays)),
        transcendentals=0,
    )


def params():
    return pltpu.CompilerParams(
        dimension_semantics=("arbitrary",), vmem_limit_bytes=VMEM_LIMIT
    )


def forward_half(place, gate, xa, xb, weights, slots):
    groups, _, tok = place.shape
    rows, half = xa.shape
    wg, wu, wd, sgu, sd = weights
    ff, unit = wg.shape[2], sd.shape[0]
    t, s = GROUP * tok, GROUP * slots
    out_shape = [
        jax.ShapeDtypeStruct((rows, half), BF16),
        jax.ShapeDtypeStruct((rows, half), BF16),
        jax.ShapeDtypeStruct((groups * s, 2 * half), BF16),
        jax.ShapeDtypeStruct((groups * s, ff), F32),
        jax.ShapeDtypeStruct((groups * s, ff), F32),
        jax.ShapeDtypeStruct((groups * s, ff), BF16),
        jax.ShapeDtypeStruct((rows, 2 * unit), F32),
        jax.ShapeDtypeStruct((rows, unit), BF16),
    ]
    args = (place, gate, xa, xb) + weights
    flops = 2 * groups * (3 * s * ff * 2 * half + 3 * t * unit * 2 * half + 2 * s * t * half)
    return pl.pallas_call(
        functools.partial(forward_kernel, slots, tok),
        grid=(groups,),
        in_specs=[spec_info(tok), spec_info(tok), spec_rows(t, half), spec_rows(t, half)]
        + [spec_whole(w) for w in weights],
        out_specs=[spec_rows(t, half), spec_rows(t, half), spec_rows(s, 2 * half)]
        + [spec_rows(s, ff)] * 3
        + [spec_rows(t, 2 * unit), spec_rows(t, unit)],
        out_shape=out_shape,
        compiler_params=params(),
        cost_estimate=cost(flops, list(args) + out_shape),
        name="forward_half",
    )(*args)


def backward_half(place, gate, ca, cb, weights, gp, up, spre, slots):
    groups, _, tok = place.shape
    rows, half = ca.shape
    wg, wu, wd, sgu, sd = weights
    ff, unit = wg.shape[2], sd.shape[0]
    t, s = GROUP * tok, GROUP * slots
    out_shape = [
        jax.ShapeDtypeStruct((rows, half), BF16),
        jax.ShapeDtypeStruct((rows, half), BF16),
        jax.ShapeDtypeStruct((groups * s, 2 * half), BF16),
        jax.ShapeDtypeStruct((groups * s, ff), BF16),
        jax.ShapeDtypeStruct((groups * s, ff), BF16),
        jax.ShapeDtypeStruct((rows, 2 * unit), BF16),
        jax.ShapeDtypeStruct((groups, GROUP, tok), F32),
    ]
    args = (place, gate, ca, cb) + weights + (gp, up, spre)
    flops = 2 * groups * (3 * s * ff * 2 * half + 3 * t * unit * 2 * half + 2 * s * t * half)
    return pl.pallas_call(
        functools.partial(backward_kernel, slots, tok),
        grid=(groups,),
        in_specs=[spec_info(tok), spec_info(tok), spec_rows(t, half), spec_rows(t, half)]
        + [spec_whole(w) for w in weights]
        + [spec_rows(s, ff), spec_rows(s, ff), spec_rows(t, 2 * unit)],
        out_specs=[spec_rows(t, half), spec_rows(t, half), spec_rows(s, 2 * half)]
        + [spec_rows(s, ff)] * 2
        + [spec_rows(t, 2 * unit), spec_info(tok)],
        out_shape=out_shape,
        compiler_params=params(),
        cost_estimate=cost(flops, list(args) + out_shape),
        name="backward_half",
    )(*args)


def shared_grads_kernel(
    g0_ref, g1_ref, h0_ref, h1_ref, xa0, xa1, xb0, xb1, ca0, ca1, cb0, cb1,
    ga_ref, gb_ref, da_ref, db_ref, gt_ref, ht_ref,
):
    rows = g0_ref.shape[0]

    @pl.when(pl.program_id(0) == 0)
    def _():
        gt_ref[:, :rows] = g0_ref[...].T
        gt_ref[:, rows:] = g1_ref[...].T
        ht_ref[:, :rows] = h0_ref[...].T
        ht_ref[:, rows:] = h1_ref[...].T

    for out, t_ref, one, two in (
        (ga_ref, gt_ref, xa0, xa1),
        (gb_ref, gt_ref, xb0, xb1),
        (da_ref, ht_ref, ca0, ca1),
        (db_ref, ht_ref, cb0, cb1),
    ):
        part = mm(t_ref[:, :rows], one[...], 1, 0) + mm(t_ref[:, rows:], two[...], 1, 0)
        out[...] = part.astype(BF16)


def shared_grads(grads, hiddens, xs, cs):
    rows, half = xs[0].shape
    unit2, unit = grads[0].shape[1], hiddens[0].shape[1]
    tile = min(256, half)
    col = pl.BlockSpec((rows, tile), lambda i: (0, i))
    args = (*grads, *hiddens, *xs, *cs)
    out_shape = [jax.ShapeDtypeStruct((n, half), BF16) for n in (unit2, unit2, unit, unit)]
    return pl.pallas_call(
        shared_grads_kernel,
        grid=(half // tile,),
        in_specs=[spec_whole(a) for a in (*grads, *hiddens)] + [col] * 8,
        out_specs=[pl.BlockSpec((o.shape[0], tile), lambda i: (0, i)) for o in out_shape],
        out_shape=out_shape,
        scratch_shapes=[pltpu.VMEM((unit2, 2 * rows), BF16), pltpu.VMEM((unit, 2 * rows), BF16)],
        compiler_params=params(),
        cost_estimate=cost(8 * rows * half * (unit2 + unit), list(args) + out_shape),
        name="shared_grads",
    )(*args)


def expert_grads_kernel(
    x0_ref, x1_ref, c0_ref, c1_ref, g0_ref, g1_ref, u0_ref, u1_ref, h0_ref, h1_ref,
    wg_ref, wu_ref, wd_ref, ht_ref,
):
    rows = x0_ref.shape[0]

    @pl.when(pl.program_id(0) == 0)
    def _():
        ht_ref[:, :rows] = h0_ref[...].T
        ht_ref[:, rows:] = h1_ref[...].T

    x0, x1 = x0_ref[...].T, x1_ref[...].T
    wg_ref[0] = (mm(x0, g0_ref[...], 1, 0) + mm(x1, g1_ref[...], 1, 0)).astype(BF16)
    wu_ref[0] = (mm(x0, u0_ref[...], 1, 0) + mm(x1, u1_ref[...], 1, 0)).astype(BF16)
    wd_ref[0] = (
        mm(ht_ref[:, :rows], c0_ref[...], 1, 0) + mm(ht_ref[:, rows:], c1_ref[...], 1, 0)
    ).astype(BF16)


def expert_grads(xr, cs, ggp, ugp, hid):
    rows, width = xr[0].shape
    ff = ggp[0].shape[1]
    tile = min(256, width)
    col = pl.BlockSpec((rows, tile), lambda i: (0, i))
    args = (*xr, *cs, *ggp, *ugp, *hid)
    out_shape = [
        jax.ShapeDtypeStruct((1, width, ff), BF16),
        jax.ShapeDtypeStruct((1, width, ff), BF16),
        jax.ShapeDtypeStruct((1, ff, width), BF16),
    ]
    return pl.pallas_call(
        expert_grads_kernel,
        grid=(width // tile,),
        in_specs=[col] * 4 + [spec_whole(a) for a in (*ggp, *ugp, *hid)],
        out_specs=[pl.BlockSpec((1, tile, ff), lambda i: (0, i, 0))] * 2
        + [pl.BlockSpec((1, ff, tile), lambda i: (0, 0, i))],
        out_shape=out_shape,
        scratch_shapes=[pltpu.VMEM((ff, 2 * rows), BF16)],
        compiler_params=params(),
        cost_estimate=cost(12 * rows * width * ff, list(args) + out_shape),
        name="expert_grads",
    )(*args)


def local(tokens, expert_ids, gates, w_gate, w_up, w_down, s_gate, s_up, s_down, cotangent):
    tok, width = tokens.shape
    top = expert_ids.shape[1]
    experts, dp = lax.axis_size("expert"), lax.axis_size("dp")
    me, my_dp = lax.axis_index("expert"), lax.axis_index("dp")
    capacity = min(tok, 5 * tok * top // (4 * experts))
    slots = -(-capacity // 16) * 16
    units = s_gate.shape[1] // experts
    share, half = tok // dp, width // 2
    sizes = split_of(experts, dp)
    orders = ((2, 3, 1), (2, 1, 3))
    shares_at = my_dp ^ jnp.arange(dp, dtype=jnp.int32)

    def everyone(rows):
        mine = lax.dynamic_slice_in_dim(rows, my_dp * share, share, 0)
        own = [
            gather_dims(mine[:, i * half : (i + 1) * half], sizes, orders[i]).reshape(-1, half)
            for i in range(2)
        ]
        return own, [partner(part, sizes, 0, 1) for part in own]

    xs = everyone(tokens)
    info = jnp.concatenate([expert_ids.astype(F32), gates], axis=1).T
    info = info.reshape(2 * top, dp, share)[:, shares_at].reshape(2 * top, tok)
    info = gather_dims(info, sizes, (2, 1)).reshape(experts // 2, 2 * top, tok)
    info = jnp.stack([info, partner(info, sizes, 0, 1)])
    cs_all = everyone(cotangent)

    hit = info[:, :, :top] == me.astype(F32)
    taken = jnp.any(hit, axis=2)
    gate = jnp.sum(jnp.where(hit, info[:, :, top:], 0.0), axis=2)
    before = jnp.triu(jnp.ones((tok, tok), BF16), 1)
    place = mm(taken.astype(BF16).reshape(experts, tok), before, 1, 0).astype(jnp.int32)
    place = jnp.where(taken, place.reshape(taken.shape), -1)
    place = place.reshape(2, -1, GROUP, tok)
    gate = gate.reshape(2, -1, GROUP, tok)

    pad = -units % 128
    widen = lambda m: jnp.pad(lax.dynamic_slice_in_dim(m, me * units, units, 1), ((0, 0), (0, pad)))
    sgu = jnp.concatenate([widen(s_gate), widen(s_up)], axis=1)
    sd = jnp.pad(lax.dynamic_slice_in_dim(s_down, me * units, units, 0), ((0, pad), (0, 0)))
    weights = (w_gate, w_up, w_down, sgu, sd)

    ahead = [forward_half(place[i], gate[i], *xs[i], weights, slots) for i in range(2)]
    back = [
        backward_half(place[i], gate[i], *cs_all[i], weights, ahead[i][3], ahead[i][4], ahead[i][6], slots)
        for i in range(2)
    ]

    shape = (1,) + sizes[1:] + (share, half)

    def summed(parts):
        out = [
            scatter_sum(parts[0][i].reshape(shape), parts[1][i].reshape(shape), sizes, orders[i][::-1])
            for i in range(2)
        ]
        return both_halves(jnp.concatenate(out, axis=1), sizes)

    moe_out = summed([a[:2] for a in ahead])
    token_grads = summed([b[:2] for b in back])

    ga, gb, da, db = shared_grads(
        [b[5] for b in back],
        [a[7] for a in ahead],
        [xs[0][0], xs[1][0], xs[0][1], xs[1][1]],
        [cs_all[0][0], cs_all[1][0], cs_all[0][1], cs_all[1][1]],
    )
    unit = units + pad
    both = jnp.concatenate([ga, gb], axis=1)
    grads = jnp.concatenate(
        [both[:units], both[unit : unit + units], jnp.concatenate([da, db], axis=1)[:units]], axis=0
    ).reshape(3 * units, experts, width // experts)
    index = np.arange(experts).reshape(sizes[2], sizes[1], 2).transpose(2, 1, 0).reshape(-1)
    where = jnp.asarray(np.argsort(index), jnp.int32)[me ^ jnp.arange(experts, dtype=jnp.int32)]
    score = jnp.stack([b[6] for b in back]).reshape(experts, dp, share)
    score = score[where][:, shares_at].reshape(experts, tok)
    block = grads.shape[2]
    lines = -(-tok // block)
    high = score.astype(BF16)
    low = (score - high.astype(F32)).astype(BF16)
    extra = jnp.pad(jnp.stack([high, low]), ((0, 0), (0, 0), (0, lines * block - tok)))
    extra = extra.reshape(2, experts, lines, block).transpose(0, 2, 1, 3)
    send = jnp.concatenate([grads, extra.reshape(2 * lines, experts, block)], axis=0).transpose(1, 0, 2)
    got = lax.all_to_all(send, "expert", split_axis=0, concat_axis=0, tiled=True)
    grad_sg = got[:, :units].reshape(experts * units, -1).T
    grad_su = got[:, units : 2 * units].reshape(experts * units, -1).T
    grad_sd = got[:, 2 * units : 3 * units].reshape(experts * units, -1)
    scores = got[:, 3 * units :].reshape(experts, 2, lines * block)[:, :, :tok].astype(F32)
    scores = (scores[:, 0] + scores[:, 1]).T
    named = expert_ids[:, :, None] == jnp.arange(experts, dtype=jnp.int32)[None, None, :]
    gate_part = jnp.sum(jnp.where(named, scores[:, None, :], 0.0), axis=2)
    gate_grads = gate_part
    for k in range(1, dp):
        gate_grads = gate_grads + partner(gate_part, sizes, 3, k)

    grad_wg, grad_wu, grad_wd = expert_grads(
        [a[2] for a in ahead], [b[2] for b in back], [b[3] for b in back], [b[4] for b in back],
        [a[5] for a in ahead],
    )
    return (moe_out, token_grads, gate_grads, grad_wg, grad_wu, grad_wd, grad_sg, grad_su, grad_sd)


def solution(mesh):
    row = P("expert", None)
    cols = P("expert", None, "dp")
    return jax.shard_map(
        local,
        mesh=mesh,
        in_specs=(
            row, row, row, cols, cols, P("expert", "dp", None),
            P(None, "dp"), P(None, "dp"), P("dp", None), row,
        ),
        out_specs=(
            row, row, row, cols, cols, P("expert", "dp", None),
            P("expert", "dp"), P("expert", "dp"), P("dp", "expert"),
        ),
        check_vma=False,
    )
```

```python
import functools

import jax
import jax.numpy as jnp
import numpy as np
from jax import lax
from jax.experimental import pallas as pl
from jax.experimental.pallas import tpu as pltpu
from jax.sharding import PartitionSpec as P

F32 = jnp.float32
BF16 = jnp.bfloat16
GROUP = 4
VMEM_LIMIT = 56 * 1024 * 1024


def mm(left, right, left_dim, right_dim):
    return lax.dot_general(
        left, right, (((left_dim,), (right_dim,)), ((), ())), preferred_element_type=F32
    )


def split_of(experts, dp):
    bits = experts.bit_length() - 1
    middle = (bits - 1) // 2
    return (2, 1 << middle, 1 << (bits - 1 - middle), dp)


def partner(array, sizes, dim, k):
    if dim == 3:
        axis, mask = "dp", k
    else:
        axis, mask = "expert", k * (1, 2, 2 * sizes[1])[dim]
    return lax.ppermute(array, axis, [(i, i ^ mask) for i in range(lax.axis_size(axis))])


def after(arrays, *earlier):
    return lax.optimization_barrier((arrays, earlier))[0]


def spread(out, sizes, dim, *earlier):
    came = [partner(out, sizes, dim, k) for k in range(1, sizes[dim])]
    return jnp.concatenate([out] + after(came, *earlier), axis=dim)


def total(terms):
    out = terms[0].astype(F32)
    for term in terms[1:]:
        out = out + term.astype(F32)
    return out.astype(BF16)


def fold(terms, sizes, dim, *earlier):
    cut = lambda k: [lax.slice_in_dim(t, k, k + 1, axis=dim) for t in terms]
    came = [partner(total(cut(k)), sizes, dim, k) for k in range(1, sizes[dim])]
    return cut(0) + after(came, *earlier)


def both_halves(rows, sizes):
    out = [rows] + [partner(rows, sizes, 3, k) for k in range(1, sizes[3])]
    out = jnp.stack(out)
    order = jnp.arange(sizes[3]) ^ lax.axis_index("dp")
    return out[order].reshape(-1, rows.shape[1])


def pick_of(place_ref, gate_ref, rows):
    place = place_ref[0]
    hit = lax.broadcasted_iota(jnp.int32, (rows, place.shape[1]), 0) == place
    gate = jnp.sum(jnp.where(hit, gate_ref[0], 0.0), axis=1, keepdims=True)
    return hit, hit.astype(BF16), gate


def take_rows(pick, a_ref, b_ref, rows_ref):
    rows, tokens = pick.shape
    parts = GROUP // 2
    half = a_ref.shape[1]
    for i in range(parts):
        r = slice(i * rows // parts, (i + 1) * rows // parts)
        t = slice(i * tokens // parts, (i + 1) * tokens // parts)
        rows_ref[r, :half] = mm(pick[r, t], a_ref[t, :], 1, 0).astype(BF16)
        rows_ref[r, half:] = mm(pick[r, t], b_ref[t, :], 1, 0).astype(BF16)


def put_rows(pick, rows, units, weight_ref, a_ref, b_ref):
    half = a_ref.shape[1]
    left = jnp.concatenate([pick.T, units], axis=1)
    for ref, cut in ((a_ref, slice(0, half)), (b_ref, slice(half, 2 * half))):
        right = jnp.concatenate([rows[:, cut], weight_ref[:, cut]], axis=0)
        ref[...] = mm(left, right, 1, 0).astype(BF16)


def fetch(sources, targets, sems):
    copies = [
        pltpu.make_async_copy(src.at[0], dst, sems.at[i])
        for i, (src, dst) in enumerate(zip(sources, targets))
    ]

    @pl.when(pl.program_id(0) == 0)
    def _():
        for copy in copies:
            copy.start()

    def ready(*which):
        @pl.when(pl.program_id(0) == 0)
        def _():
            for i in which:
                copies[i].wait()

    return ready


def forward_kernel(
    place_ref, gate_ref, xa_ref, xb_ref, wg_hbm, wu_hbm, wd_hbm, sgu_ref, sd_ref,
    oa_ref, ob_ref, xr_ref, gp_ref, up_ref, hid_ref, spre_ref, shid_ref,
    wg_ref, wu_ref, wd_ref, sems,
):
    ready = fetch((wg_hbm, wu_hbm, wd_hbm), (wg_ref, wu_ref, wd_ref), sems)
    hit, pick, gate = pick_of(place_ref, gate_ref, xr_ref.shape[0])
    half = xa_ref.shape[1]
    unit = sd_ref.shape[0]
    take_rows(pick, xa_ref, xb_ref, xr_ref)
    spre = mm(xa_ref[...], sgu_ref[:, :half], 1, 1) + mm(xb_ref[...], sgu_ref[:, half:], 1, 1)
    spre_ref[...] = spre
    sgp, sup = spre[:, :unit], spre[:, unit:]
    shid = (sgp * jax.nn.sigmoid(sgp) * sup).astype(BF16)
    shid_ref[...] = shid
    xr = xr_ref[...]
    ready(0, 1)
    gp = mm(xr, wg_ref[...], 1, 1)
    up = mm(xr, wu_ref[...], 1, 1)
    gp_ref[...] = gp
    up_ref[...] = up
    hid = (gp * jax.nn.sigmoid(gp) * up).astype(BF16)
    hid_ref[...] = hid
    ready(2)
    rows = (mm(hid, wd_ref[...], 1, 0) * gate).astype(BF16)
    put_rows(pick, rows, shid, sd_ref, oa_ref, ob_ref)


def backward_kernel(
    place_ref, gate_ref, ca_ref, cb_ref, wg_hbm, wu_hbm, wd_hbm, sgu_ref, sd_ref,
    gp_ref, up_ref, spre_ref,
    oa_ref, ob_ref, cs_ref, ggp_ref, ugp_ref, sgrad_ref, score_ref,
    wg_ref, wu_ref, wd_ref, sems, cr_ref,
):
    ready = fetch((wg_hbm, wu_hbm, wd_hbm), (wg_ref, wu_ref, wd_ref), sems)
    hit, pick, gate = pick_of(place_ref, gate_ref, cr_ref.shape[0])
    half = ca_ref.shape[1]
    unit = sd_ref.shape[0]
    take_rows(pick, ca_ref, cb_ref, cr_ref)
    sgp, sup = spre_ref[:, :unit], spre_ref[:, unit:]
    ssig = jax.nn.sigmoid(sgp)
    sgrad = mm(ca_ref[...], sd_ref[:, :half], 1, 1) + mm(cb_ref[...], sd_ref[:, half:], 1, 1)
    sgg = (sgrad * sup * ssig * (1.0 + sgp * (1.0 - ssig))).astype(BF16)
    sug = (sgrad * sgp * ssig).astype(BF16)
    both = jnp.concatenate([sgg, sug], axis=1)
    sgrad_ref[...] = both
    cr = cr_ref[...]
    cs_ref[...] = (cr.astype(F32) * gate).astype(BF16)
    ready(2)
    raw = mm(cr, wd_ref[...], 1, 1)
    gp, up = gp_ref[...], up_ref[...]
    sig = jax.nn.sigmoid(gp)
    silu = gp * sig
    score = jnp.sum(raw * (silu * up).astype(BF16).astype(F32), axis=1, keepdims=True)
    score_ref[0] = jnp.sum(jnp.where(hit, score, 0.0), axis=0, keepdims=True)
    grad = raw * gate
    ggp = (grad * up * sig * (1.0 + gp * (1.0 - sig))).astype(BF16)
    ugp = (grad * silu).astype(BF16)
    ggp_ref[...] = ggp
    ugp_ref[...] = ugp
    ready(0, 1)
    rows = (mm(ggp, wg_ref[...], 1, 0) + mm(ugp, wu_ref[...], 1, 0)).astype(BF16)
    put_rows(pick, rows, both, sgu_ref, oa_ref, ob_ref)


def spec_rows(rows, width):
    return pl.BlockSpec((rows, width), lambda i: (i, 0))


def spec_info(tok):
    return pl.BlockSpec((1, 1, tok), lambda i: (i, 0, 0))


def spec_whole(array):
    return pl.BlockSpec(array.shape, lambda i: (0,) * array.ndim, pipeline_mode=pl.Buffered(1))


def cost(flops, arrays):
    return pl.CostEstimate(
        flops=int(flops),
        bytes_accessed=int(sum(np.prod(a.shape) * a.dtype.itemsize for a in arrays)),
        transcendentals=0,
    )


def params():
    return pltpu.CompilerParams(
        dimension_semantics=("arbitrary",), vmem_limit_bytes=VMEM_LIMIT
    )


def half_call(name, kernel, place, gate, parts, weights, more, outs, scratch):
    groups, _, tokens = place.shape
    half = parts[0].shape[1]
    ff = weights[0].shape[1]
    hbm = pl.BlockSpec(memory_space=pl.ANY)
    by_group = lambda n: spec_rows(n.shape[0] // groups, n.shape[1])
    args = (place, gate, *parts, *weights, *more)
    rows = outs[2].shape[0]
    unit = weights[4].shape[0]
    flops = 6 * rows * ff * 2 * half + 6 * groups * tokens * unit * 2 * half
    flops += 4 * rows * tokens * half
    return pl.pallas_call(
        kernel,
        grid=(groups,),
        in_specs=[spec_info(tokens)] * 2
        + [by_group(p) for p in parts]
        + [hbm] * 3
        + [spec_whole(w) for w in weights[3:]]
        + [by_group(m) for m in more],
        out_specs=[by_group(o) if len(o.shape) == 2 else spec_info(tokens) for o in outs],
        out_shape=outs,
        scratch_shapes=[pltpu.VMEM(w.shape[1:], BF16) for w in weights[:3]]
        + [pltpu.SemaphoreType.DMA((3,))]
        + scratch,
        compiler_params=params(),
        cost_estimate=cost(4 * flops, list(args) + outs),
        name=name,
    )(*args)


def forward_half(place, gate, parts, weights, rows):
    tokens, half = parts[0].shape
    ff, unit = weights[0].shape[1], weights[4].shape[0]
    shape = jax.ShapeDtypeStruct
    outs = [
        shape((tokens, half), BF16),
        shape((tokens, half), BF16),
        shape((rows, 2 * half), BF16),
        shape((rows, ff), F32),
        shape((rows, ff), F32),
        shape((rows, ff), BF16),
        shape((tokens, 2 * unit), F32),
        shape((tokens, unit), BF16),
    ]
    return half_call("forward_half", forward_kernel, place, gate, parts, weights, (), outs, [])


def backward_half(place, gate, parts, weights, ahead, rows):
    tokens, half = parts[0].shape
    ff, unit = weights[0].shape[1], weights[4].shape[0]
    shape = jax.ShapeDtypeStruct
    outs = [
        shape((tokens, half), BF16),
        shape((tokens, half), BF16),
        shape((rows, 2 * half), BF16),
        shape((rows, ff), BF16),
        shape((rows, ff), BF16),
        shape((tokens, 2 * unit), BF16),
        shape(place.shape, F32),
    ]
    more = (ahead[3], ahead[4], ahead[6])
    scratch = [pltpu.VMEM((rows // place.shape[0], 2 * half), BF16)]
    return half_call(
        "backward_half", backward_kernel, place, gate, parts, weights, more, outs, scratch
    )


def shared_grads_kernel(
    g0_ref, g1_ref, h0_ref, h1_ref, xa0, xa1, xb0, xb1, ca0, ca1, cb0, cb1,
    ga_ref, gb_ref, da_ref, db_ref, gt_ref, ht_ref,
):
    rows = g0_ref.shape[0]

    @pl.when(pl.program_id(0) == 0)
    def _():
        gt_ref[:, :rows] = g0_ref[...].T
        gt_ref[:, rows:] = g1_ref[...].T
        ht_ref[:, :rows] = h0_ref[...].T
        ht_ref[:, rows:] = h1_ref[...].T

    for out, t_ref, one, two in (
        (ga_ref, gt_ref, xa0, xa1),
        (gb_ref, gt_ref, xb0, xb1),
        (da_ref, ht_ref, ca0, ca1),
        (db_ref, ht_ref, cb0, cb1),
    ):
        part = mm(t_ref[:, :rows], one[...], 1, 0) + mm(t_ref[:, rows:], two[...], 1, 0)
        out[...] = part.astype(BF16)


def shared_grads(grads, hiddens, xs, cs):
    rows, half = xs[0].shape
    unit2, unit = grads[0].shape[1], hiddens[0].shape[1]
    tile = min(256, half)
    col = pl.BlockSpec((rows, tile), lambda i: (0, i))
    args = (*grads, *hiddens, *xs, *cs)
    out_shape = [jax.ShapeDtypeStruct((n, half), BF16) for n in (unit2, unit2, unit, unit)]
    return pl.pallas_call(
        shared_grads_kernel,
        grid=(half // tile,),
        in_specs=[spec_whole(a) for a in (*grads, *hiddens)] + [col] * 8,
        out_specs=[pl.BlockSpec((o.shape[0], tile), lambda i: (0, i)) for o in out_shape],
        out_shape=out_shape,
        scratch_shapes=[pltpu.VMEM((unit2, 2 * rows), BF16), pltpu.VMEM((unit, 2 * rows), BF16)],
        compiler_params=params(),
        cost_estimate=cost(8 * rows * half * (unit2 + unit), list(args) + out_shape),
        name="shared_grads",
    )(*args)


def expert_grads_kernel(
    x0_ref, x1_ref, c0_ref, c1_ref, g0_ref, g1_ref, u0_ref, u1_ref, h0_ref, h1_ref,
    wg_ref, wu_ref, wd_ref, gt_ref, ut_ref, ht_ref,
):
    rows = x0_ref.shape[0]

    @pl.when(pl.program_id(0) == 0)
    def _():
        for t_ref, one, two in (
            (gt_ref, g0_ref, g1_ref), (ut_ref, u0_ref, u1_ref), (ht_ref, h0_ref, h1_ref)
        ):
            t_ref[:, :rows] = one[...].T
            t_ref[:, rows:] = two[...].T

    x = jnp.concatenate([x0_ref[...], x1_ref[...]], axis=0)
    c = jnp.concatenate([c0_ref[...], c1_ref[...]], axis=0)
    wg_ref[0] = mm(gt_ref[...], x, 1, 0).astype(BF16)
    wu_ref[0] = mm(ut_ref[...], x, 1, 0).astype(BF16)
    wd_ref[0] = mm(ht_ref[...], c, 1, 0).astype(BF16)


def expert_grads(xr, cs, ggp, ugp, hid):
    rows, width = xr[0].shape
    ff = ggp[0].shape[1]
    tile = min(256, width)
    col = pl.BlockSpec((rows, tile), lambda i: (0, i))
    args = (*xr, *cs, *ggp, *ugp, *hid)
    out_shape = [jax.ShapeDtypeStruct((1, ff, width), BF16)] * 3
    return pl.pallas_call(
        expert_grads_kernel,
        grid=(width // tile,),
        in_specs=[col] * 4 + [spec_whole(a) for a in (*ggp, *ugp, *hid)],
        out_specs=[pl.BlockSpec((1, ff, tile), lambda i: (0, 0, i))] * 3,
        out_shape=out_shape,
        scratch_shapes=[pltpu.VMEM((ff, 2 * rows), BF16)] * 3,
        compiler_params=params(),
        cost_estimate=cost(24 * rows * width * ff, list(args) + out_shape),
        name="expert_grads",
    )(*args)


def local(tokens, expert_ids, gates, w_gate, w_up, w_down, s_gate, s_up, s_down, cotangent):
    tok, width = tokens.shape
    top = expert_ids.shape[1]
    experts, dp = lax.axis_size("expert"), lax.axis_size("dp")
    me, my_dp = lax.axis_index("expert"), lax.axis_index("dp")
    capacity = min(tok, 5 * tok * top // (4 * experts))
    slots = -(-capacity // 16) * 16
    units = s_gate.shape[1] // experts
    share, half = tok // dp, width // 2
    sizes = split_of(experts, dp)
    shares_at = my_dp ^ jnp.arange(dp, dtype=jnp.int32)
    turns = ((3, 1), (1, 3))
    shape = (1,) + sizes[1:] + (share, half)
    flat = lambda parts: [p.reshape(-1, half) for p in parts]
    full = lambda parts: [p.reshape(shape) for p in parts]

    def mine(rows):
        rows = lax.dynamic_slice_in_dim(rows, my_dp * share, share, 0)
        return [rows[:, i * half : (i + 1) * half].reshape(1, 1, 1, 1, share, half) for i in range(2)]

    x1 = [spread(p, sizes, 2) for p in mine(tokens)]
    x2 = [spread(p, sizes, turn[0]) for p, turn in zip(x1, turns)]
    x3 = [spread(p, sizes, turn[1]) for p, turn in zip(x2, turns)]
    own_x = flat(x3)
    other_x = [partner(p, sizes, 0, 1) for p in own_x]
    c1 = [spread(p, sizes, 2) for p in after(mine(cotangent), x1)]

    info = jnp.concatenate([expert_ids.astype(F32), gates], axis=1).T
    info = info.reshape(2 * top, dp, share)[:, shares_at].reshape(1, 1, 1, 1, 2 * top, tok)
    info = spread(spread(after(info, x1), sizes, 2), sizes, 1).reshape(experts // 2, 2 * top, tok)
    info = jnp.stack([info, partner(info, sizes, 0, 1)])

    hit = info[:, :, :top] == me.astype(F32)
    taken = jnp.any(hit, axis=2)
    gate = jnp.sum(jnp.where(hit, info[:, :, top:], 0.0), axis=2)
    before = jnp.triu(jnp.ones((tok, tok), BF16), 1)
    place = mm(taken.astype(BF16).reshape(experts, tok), before, 1, 0).astype(jnp.int32)
    start = slots * (jnp.arange(experts // 2, dtype=jnp.int32) % GROUP)
    place = jnp.where(taken, place.reshape(taken.shape) + start[None, :, None], -1)
    place = place.reshape(2, -1, 1, GROUP * tok)
    gate = gate.reshape(2, -1, 1, GROUP * tok)

    pad = -units % 128
    widen = lambda m: jnp.pad(m, ((0, pad), (0, 0)))
    columns = lambda m: widen(lax.dynamic_slice_in_dim(m, me * units, units, 1).T)
    sgu = jnp.concatenate([columns(s_gate), columns(s_up)], axis=0)
    sd = widen(lax.dynamic_slice_in_dim(s_down, me * units, units, 0))
    weights = (w_gate.swapaxes(1, 2), w_up.swapaxes(1, 2), w_down, sgu, sd)

    rows = experts // 2 * slots
    ahead0 = forward_half(place[0], gate[0], own_x, weights, rows)
    c2 = [spread(p, sizes, turn[0], ahead0[0]) for p, turn in zip(after(c1, x3), turns)]
    ahead1 = forward_half(place[1], gate[1], other_x, weights, rows)
    c3 = [spread(p, sizes, turn[1], ahead1[0]) for p, turn in zip(c2, turns)]
    own_c = flat(c3)
    back0 = backward_half(place[0], gate[0], own_c, weights, ahead0, rows)
    other_c, out_came = after(
        ([partner(p, sizes, 0, 1) for p in own_c], [partner(p, sizes, 0, 1) for p in full(ahead1[:2])]),
        back0[0],
    )
    back1 = backward_half(place[1], gate[1], other_c, weights, ahead1, rows)

    out = [list(t) for t in zip(full(ahead0[:2]), out_came)]
    out = [fold(t, sizes, turn[1], back1[0]) for t, turn in zip(out, turns)]
    ga, gb, da, db = shared_grads(
        [back0[5], back1[5]],
        [ahead0[7], ahead1[7]],
        [own_x[0], other_x[0], own_x[1], other_x[1]],
        [own_c[0], other_c[0], own_c[1], other_c[1]],
    )
    out = [fold(t, sizes, turn[0], ga) for t, turn in zip(out, turns)]
    dx_came = after([partner(p, sizes, 0, 1) for p in full(back1[:2])], ga)
    dx = [list(t) for t in zip(full(back0[:2]), dx_came)]
    grad_wg, grad_wu, grad_wd = expert_grads(
        [ahead0[2], ahead1[2]], [back0[2], back1[2]], [back0[3], back1[3]], [back0[4], back1[4]],
        [ahead0[5], ahead1[5]],
    )
    dx = [fold(t, sizes, turn[1], grad_wg) for t, turn in zip(dx, turns)]
    out = [fold(t, sizes, 2, grad_wg) for t in out]
    moe_out = both_halves(jnp.concatenate([total(t).reshape(share, half) for t in out], axis=1), sizes)
    dx = [fold(t, sizes, turn[0]) for t, turn in zip(dx, turns)]
    dx = [fold(t, sizes, 2) for t in dx]
    token_grads = both_halves(jnp.concatenate([total(t).reshape(share, half) for t in dx], axis=1), sizes)

    unit = units + pad
    both = jnp.concatenate([ga, gb], axis=1)
    grads = jnp.concatenate(
        [both[:units], both[unit : unit + units], jnp.concatenate([da, db], axis=1)[:units]], axis=0
    ).reshape(3 * units, experts, width // experts)
    index = np.arange(experts).reshape(sizes[2], sizes[1], 2).transpose(2, 1, 0).reshape(-1)
    where = jnp.asarray(np.argsort(index), jnp.int32)[me ^ jnp.arange(experts, dtype=jnp.int32)]
    score = jnp.stack([back0[6], back1[6]]).reshape(experts, dp, share)
    score = score[where][:, shares_at].reshape(experts, tok)
    block = grads.shape[2]
    lines = -(-tok // block)
    high = score.astype(BF16)
    low = (score - high.astype(F32)).astype(BF16)
    extra = jnp.pad(jnp.stack([high, low]), ((0, 0), (0, 0), (0, lines * block - tok)))
    extra = extra.reshape(2, experts, lines, block).transpose(0, 2, 1, 3)
    send = jnp.concatenate([grads, extra.reshape(2 * lines, experts, block)], axis=0).transpose(1, 0, 2)
    got = lax.all_to_all(send, "expert", split_axis=0, concat_axis=0, tiled=True)
    grad_sg = got[:, :units].reshape(experts * units, -1).T
    grad_su = got[:, units : 2 * units].reshape(experts * units, -1).T
    grad_sd = got[:, 2 * units : 3 * units].reshape(experts * units, -1)
    scores = got[:, 3 * units :].reshape(experts, 2, lines * block)[:, :, :tok].astype(F32)
    scores = (scores[:, 0] + scores[:, 1]).T
    named = expert_ids[:, :, None] == jnp.arange(experts, dtype=jnp.int32)[None, None, :]
    gate_part = jnp.sum(jnp.where(named, scores[:, None, :], 0.0), axis=2)
    gate_grads = gate_part
    for k in range(1, dp):
        gate_grads = gate_grads + partner(gate_part, sizes, 3, k)

    grad_wg, grad_wu = grad_wg.swapaxes(1, 2), grad_wu.swapaxes(1, 2)
    return (moe_out, token_grads, gate_grads, grad_wg, grad_wu, grad_wd, grad_sg, grad_su, grad_sd)


def solution(mesh):
    row = P("expert", None)
    cols = P("expert", None, "dp")
    return jax.shard_map(
        local,
        mesh=mesh,
        in_specs=(
            row, row, row, cols, cols, P("expert", "dp", None),
            P(None, "dp"), P(None, "dp"), P("dp", None), row,
        ),
        out_specs=(
            row, row, row, cols, cols, P("expert", "dp", None),
            P("expert", "dp"), P("expert", "dp"), P("dp", "expert"),
        ),
        check_vma=False,
    )
```

```python
import functools

import jax
import jax.numpy as jnp
import numpy as np
from jax import lax
from jax.experimental import pallas as pl
from jax.experimental.pallas import tpu as pltpu
from jax.sharding import PartitionSpec as P

F32 = jnp.float32
BF16 = jnp.bfloat16
GROUP = 4
VMEM_LIMIT = 56 * 1024 * 1024


def mm(left, right, left_dim, right_dim):
    return lax.dot_general(
        left, right, (((left_dim,), (right_dim,)), ((), ())), preferred_element_type=F32
    )


def split_of(experts, dp):
    bits = experts.bit_length() - 1
    middle = (bits - 1) // 2
    return (2, 1 << middle, 1 << (bits - 1 - middle), dp)


def partner(array, sizes, dim, k):
    if dim == 3:
        axis, mask = "dp", k
    else:
        axis, mask = "expert", k * (1, 2, 2 * sizes[1])[dim]
    return lax.ppermute(array, axis, [(i, i ^ mask) for i in range(lax.axis_size(axis))])


def after(arrays, *earlier):
    return lax.optimization_barrier((arrays, earlier))[0]


def spread(out, sizes, dim, *earlier):
    came = [partner(out, sizes, dim, k) for k in range(1, sizes[dim])]
    return jnp.concatenate([out] + after(came, *earlier), axis=dim)


def total(terms):
    out = terms[0].astype(F32)
    for term in terms[1:]:
        out = out + term.astype(F32)
    return out.astype(BF16)


def parts_for(terms, sizes, dim):
    cut = lambda k: [lax.slice_in_dim(t, k, k + 1, axis=dim) for t in terms]
    return [total(cut(k)) for k in range(1, sizes[dim])], cut(0)


def fold(sent, stays, sizes, dim):
    return stays + [partner(part, sizes, dim, k + 1) for k, part in enumerate(sent)]


def both_halves(rows, sizes):
    out = [rows] + [partner(rows, sizes, 3, k) for k in range(1, sizes[3])]
    out = jnp.stack(out)
    order = jnp.arange(sizes[3]) ^ lax.axis_index("dp")
    return out[order].reshape(-1, rows.shape[1])


def pick_of(place_ref, gate_ref, rows):
    place = place_ref[0]
    hit = lax.broadcasted_iota(jnp.int32, (rows, place.shape[1]), 0) == place
    gate = jnp.sum(jnp.where(hit, gate_ref[0], 0.0), axis=1, keepdims=True)
    return hit, hit.astype(BF16), gate


def take_rows(pick, a_ref, b_ref, rows_ref):
    rows, tokens = pick.shape
    parts = GROUP // 2
    half = a_ref.shape[1]
    for i in range(parts):
        r = slice(i * rows // parts, (i + 1) * rows // parts)
        t = slice(i * tokens // parts, (i + 1) * tokens // parts)
        rows_ref[r, :half] = mm(pick[r, t], a_ref[t, :], 1, 0).astype(BF16)
        rows_ref[r, half:] = mm(pick[r, t], b_ref[t, :], 1, 0).astype(BF16)


def put_rows(pick, rows, units, weight_ref, a_ref, b_ref):
    half = a_ref.shape[1]
    left = jnp.concatenate([pick.T, units], axis=1)
    for ref, cut in ((a_ref, slice(0, half)), (b_ref, slice(half, 2 * half))):
        right = jnp.concatenate([rows[:, cut], weight_ref[:, cut]], axis=0)
        ref[...] = mm(left, right, 1, 0).astype(BF16)


def fetch(sources, targets, sems):
    copies = [
        pltpu.make_async_copy(src.at[0], dst, sems.at[i])
        for i, (src, dst) in enumerate(zip(sources, targets))
    ]

    @pl.when(pl.program_id(0) == 0)
    def _():
        for copy in copies:
            copy.start()

    def ready(*which):
        @pl.when(pl.program_id(0) == 0)
        def _():
            for i in which:
                copies[i].wait()

    return ready


def forward_kernel(
    place_ref, gate_ref, xa_ref, xb_ref, wg_hbm, wu_hbm, wd_hbm, sgu_ref, sd_ref,
    oa_ref, ob_ref, xr_ref, gp_ref, up_ref, hid_ref, spre_ref, shid_ref,
    wg_ref, wu_ref, wd_ref, sems,
):
    ready = fetch((wg_hbm, wu_hbm, wd_hbm), (wg_ref, wu_ref, wd_ref), sems)
    hit, pick, gate = pick_of(place_ref, gate_ref, xr_ref.shape[0])
    half = xa_ref.shape[1]
    unit = sd_ref.shape[0]
    take_rows(pick, xa_ref, xb_ref, xr_ref)
    spre = mm(xa_ref[...], sgu_ref[:, :half], 1, 1) + mm(xb_ref[...], sgu_ref[:, half:], 1, 1)
    spre_ref[...] = spre
    sgp, sup = spre[:, :unit], spre[:, unit:]
    shid = (sgp * jax.nn.sigmoid(sgp) * sup).astype(BF16)
    shid_ref[...] = shid
    xr = xr_ref[...]
    ready(0, 1)
    gp = mm(xr, wg_ref[...], 1, 1)
    up = mm(xr, wu_ref[...], 1, 1)
    gp_ref[...] = gp
    up_ref[...] = up
    hid = (gp * jax.nn.sigmoid(gp) * up).astype(BF16)
    hid_ref[...] = hid
    ready(2)
    rows = (mm(hid, wd_ref[...], 1, 0) * gate).astype(BF16)
    put_rows(pick, rows, shid, sd_ref, oa_ref, ob_ref)


def backward_kernel(
    place_ref, gate_ref, ca_ref, cb_ref, wg_hbm, wu_hbm, wd_hbm, sgu_ref, sd_ref,
    gp_ref, up_ref, spre_ref,
    oa_ref, ob_ref, cs_ref, ggp_ref, ugp_ref, sgrad_ref, score_ref,
    wg_ref, wu_ref, wd_ref, sems, cr_ref,
):
    ready = fetch((wg_hbm, wu_hbm, wd_hbm), (wg_ref, wu_ref, wd_ref), sems)
    hit, pick, gate = pick_of(place_ref, gate_ref, cr_ref.shape[0])
    half = ca_ref.shape[1]
    unit = sd_ref.shape[0]
    take_rows(pick, ca_ref, cb_ref, cr_ref)
    sgp, sup = spre_ref[:, :unit], spre_ref[:, unit:]
    ssig = jax.nn.sigmoid(sgp)
    sgrad = mm(ca_ref[...], sd_ref[:, :half], 1, 1) + mm(cb_ref[...], sd_ref[:, half:], 1, 1)
    sgg = (sgrad * sup * ssig * (1.0 + sgp * (1.0 - ssig))).astype(BF16)
    sug = (sgrad * sgp * ssig).astype(BF16)
    both = jnp.concatenate([sgg, sug], axis=1)
    sgrad_ref[...] = both
    cr = cr_ref[...]
    cs_ref[...] = (cr.astype(F32) * gate).astype(BF16)
    ready(2)
    raw = mm(cr, wd_ref[...], 1, 1)
    gp, up = gp_ref[...], up_ref[...]
    sig = jax.nn.sigmoid(gp)
    silu = gp * sig
    score = jnp.sum(raw * (silu * up).astype(BF16).astype(F32), axis=1, keepdims=True)
    score_ref[0] = jnp.sum(jnp.where(hit, score, 0.0), axis=0, keepdims=True)
    grad = raw * gate
    ggp = (grad * up * sig * (1.0 + gp * (1.0 - sig))).astype(BF16)
    ugp = (grad * silu).astype(BF16)
    ggp_ref[...] = ggp
    ugp_ref[...] = ugp
    ready(0, 1)
    rows = (mm(ggp, wg_ref[...], 1, 0) + mm(ugp, wu_ref[...], 1, 0)).astype(BF16)
    put_rows(pick, rows, both, sgu_ref, oa_ref, ob_ref)


def spec_rows(rows, width):
    return pl.BlockSpec((rows, width), lambda i: (i, 0))


def spec_info(tok):
    return pl.BlockSpec((1, 1, tok), lambda i: (i, 0, 0))


def spec_whole(array):
    return pl.BlockSpec(array.shape, lambda i: (0,) * array.ndim, pipeline_mode=pl.Buffered(1))


def cost(flops, arrays):
    return pl.CostEstimate(
        flops=int(flops),
        bytes_accessed=int(sum(np.prod(a.shape) * a.dtype.itemsize for a in arrays)),
        transcendentals=0,
    )


def params():
    return pltpu.CompilerParams(
        dimension_semantics=("arbitrary",), vmem_limit_bytes=VMEM_LIMIT
    )


def half_call(name, kernel, place, gate, parts, weights, more, outs, scratch):
    groups, _, tokens = place.shape
    half = parts[0].shape[1]
    ff = weights[0].shape[1]
    hbm = pl.BlockSpec(memory_space=pl.ANY)
    by_group = lambda n: spec_rows(n.shape[0] // groups, n.shape[1])
    args = (place, gate, *parts, *weights, *more)
    rows = outs[2].shape[0]
    unit = weights[4].shape[0]
    flops = 6 * rows * ff * 2 * half + 6 * groups * tokens * unit * 2 * half
    flops += 4 * rows * tokens * half
    return pl.pallas_call(
        kernel,
        grid=(groups,),
        in_specs=[spec_info(tokens)] * 2
        + [by_group(p) for p in parts]
        + [hbm] * 3
        + [spec_whole(w) for w in weights[3:]]
        + [by_group(m) for m in more],
        out_specs=[by_group(o) if len(o.shape) == 2 else spec_info(tokens) for o in outs],
        out_shape=outs,
        scratch_shapes=[pltpu.VMEM(w.shape[1:], BF16) for w in weights[:3]]
        + [pltpu.SemaphoreType.DMA((3,))]
        + scratch,
        compiler_params=params(),
        cost_estimate=cost(4 * flops, list(args) + outs),
        name=name,
    )(*args)


def forward_half(place, gate, parts, weights, rows):
    tokens, half = parts[0].shape
    ff, unit = weights[0].shape[1], weights[4].shape[0]
    shape = jax.ShapeDtypeStruct
    outs = [
        shape((tokens, half), BF16),
        shape((tokens, half), BF16),
        shape((rows, 2 * half), BF16),
        shape((rows, ff), F32),
        shape((rows, ff), F32),
        shape((rows, ff), BF16),
        shape((tokens, 2 * unit), F32),
        shape((tokens, unit), BF16),
    ]
    return half_call("forward_half", forward_kernel, place, gate, parts, weights, (), outs, [])


def backward_half(place, gate, parts, weights, ahead, rows):
    tokens, half = parts[0].shape
    ff, unit = weights[0].shape[1], weights[4].shape[0]
    shape = jax.ShapeDtypeStruct
    outs = [
        shape((tokens, half), BF16),
        shape((tokens, half), BF16),
        shape((rows, 2 * half), BF16),
        shape((rows, ff), BF16),
        shape((rows, ff), BF16),
        shape((tokens, 2 * unit), BF16),
        shape(place.shape, F32),
    ]
    more = (ahead[3], ahead[4], ahead[6])
    scratch = [pltpu.VMEM((rows // place.shape[0], 2 * half), BF16)]
    return half_call(
        "backward_half", backward_kernel, place, gate, parts, weights, more, outs, scratch
    )


def shared_grads_kernel(
    g0_ref, g1_ref, h0_ref, h1_ref, xa0, xa1, xb0, xb1, ca0, ca1, cb0, cb1,
    ga_ref, gb_ref, da_ref, db_ref, gt_ref, ht_ref,
):
    rows = g0_ref.shape[0]

    @pl.when(pl.program_id(0) == 0)
    def _():
        gt_ref[:, :rows] = g0_ref[...].T
        gt_ref[:, rows:] = g1_ref[...].T
        ht_ref[:, :rows] = h0_ref[...].T
        ht_ref[:, rows:] = h1_ref[...].T

    for out, t_ref, one, two in (
        (ga_ref, gt_ref, xa0, xa1),
        (gb_ref, gt_ref, xb0, xb1),
        (da_ref, ht_ref, ca0, ca1),
        (db_ref, ht_ref, cb0, cb1),
    ):
        part = mm(t_ref[:, :rows], one[...], 1, 0) + mm(t_ref[:, rows:], two[...], 1, 0)
        out[...] = part.astype(BF16)


def shared_grads(grads, hiddens, xs, cs):
    rows, half = xs[0].shape
    unit2, unit = grads[0].shape[1], hiddens[0].shape[1]
    tile = min(256, half)
    col = pl.BlockSpec((rows, tile), lambda i: (0, i))
    args = (*grads, *hiddens, *xs, *cs)
    out_shape = [jax.ShapeDtypeStruct((n, half), BF16) for n in (unit2, unit2, unit, unit)]
    return pl.pallas_call(
        shared_grads_kernel,
        grid=(half // tile,),
        in_specs=[spec_whole(a) for a in (*grads, *hiddens)] + [col] * 8,
        out_specs=[pl.BlockSpec((o.shape[0], tile), lambda i: (0, i)) for o in out_shape],
        out_shape=out_shape,
        scratch_shapes=[pltpu.VMEM((unit2, 2 * rows), BF16), pltpu.VMEM((unit, 2 * rows), BF16)],
        compiler_params=params(),
        cost_estimate=cost(8 * rows * half * (unit2 + unit), list(args) + out_shape),
        name="shared_grads",
    )(*args)


def expert_grads_kernel(
    x0_ref, x1_ref, c0_ref, c1_ref, g0_ref, g1_ref, u0_ref, u1_ref, h0_ref, h1_ref,
    wg_ref, wu_ref, wd_ref, gt_ref, ut_ref, ht_ref,
):
    rows = x0_ref.shape[0]

    @pl.when(pl.program_id(0) == 0)
    def _():
        for t_ref, one, two in (
            (gt_ref, g0_ref, g1_ref), (ut_ref, u0_ref, u1_ref), (ht_ref, h0_ref, h1_ref)
        ):
            t_ref[:, :rows] = one[...].T
            t_ref[:, rows:] = two[...].T

    x = jnp.concatenate([x0_ref[...], x1_ref[...]], axis=0)
    c = jnp.concatenate([c0_ref[...], c1_ref[...]], axis=0)
    wg_ref[0] = mm(gt_ref[...], x, 1, 0).astype(BF16)
    wu_ref[0] = mm(ut_ref[...], x, 1, 0).astype(BF16)
    wd_ref[0] = mm(ht_ref[...], c, 1, 0).astype(BF16)


def expert_grads(xr, cs, ggp, ugp, hid):
    rows, width = xr[0].shape
    ff = ggp[0].shape[1]
    tile = min(256, width)
    col = pl.BlockSpec((rows, tile), lambda i: (0, i))
    args = (*xr, *cs, *ggp, *ugp, *hid)
    out_shape = [jax.ShapeDtypeStruct((1, ff, width), BF16)] * 3
    return pl.pallas_call(
        expert_grads_kernel,
        grid=(width // tile,),
        in_specs=[col] * 4 + [spec_whole(a) for a in (*ggp, *ugp, *hid)],
        out_specs=[pl.BlockSpec((1, ff, tile), lambda i: (0, 0, i))] * 3,
        out_shape=out_shape,
        scratch_shapes=[pltpu.VMEM((ff, 2 * rows), BF16)] * 3,
        compiler_params=params(),
        cost_estimate=cost(24 * rows * width * ff, list(args) + out_shape),
        name="expert_grads",
    )(*args)


def local(tokens, expert_ids, gates, w_gate, w_up, w_down, s_gate, s_up, s_down, cotangent):
    tok, width = tokens.shape
    top = expert_ids.shape[1]
    experts, dp = lax.axis_size("expert"), lax.axis_size("dp")
    me, my_dp = lax.axis_index("expert"), lax.axis_index("dp")
    capacity = min(tok, 5 * tok * top // (4 * experts))
    slots = -(-capacity // 16) * 16
    units = s_gate.shape[1] // experts
    share, half = tok // dp, width // 2
    sizes = split_of(experts, dp)
    shares_at = my_dp ^ jnp.arange(dp, dtype=jnp.int32)
    turns = ((3, 1), (1, 3))
    shape = (1,) + sizes[1:] + (share, half)
    flat = lambda parts: [p.reshape(-1, half) for p in parts]
    full = lambda parts: [p.reshape(shape) for p in parts]

    def mine(rows):
        rows = lax.dynamic_slice_in_dim(rows, my_dp * share, share, 0)
        return [rows[:, i * half : (i + 1) * half].reshape(1, 1, 1, 1, share, half) for i in range(2)]

    halves = lambda rows: [rows[..., i * half : (i + 1) * half] for i in range(2)]
    mine = lambda rows: lax.dynamic_slice_in_dim(rows, my_dp * share, share, 0)[None, None, None, None]
    x0 = mine(tokens)
    x1 = spread(x0, sizes, 2)
    x2 = [spread(p, sizes, turn[0]) for p, turn in zip(halves(x1), turns)]
    c1 = spread(after(mine(cotangent), x1), sizes, 2, x2)
    x3 = [spread(p, sizes, turn[1]) for p, turn in zip(x2, turns)]
    own_x = flat(x3)
    other_x = [partner(p, sizes, 0, 1) for p in own_x]

    info = jnp.concatenate([after(expert_ids, x0).astype(F32), gates], axis=1).T
    info = info.reshape(2 * top, dp, share)[:, shares_at].reshape(1, 1, 1, 1, 2 * top, tok)
    info = spread(info, sizes, 2, x1)
    info = spread(info, sizes, 1, x2).reshape(experts // 2, 2 * top, tok)
    info = jnp.stack([info, partner(info, sizes, 0, 1)])

    hit = info[:, :, :top] == me.astype(F32)
    taken = jnp.any(hit, axis=2)
    gate = jnp.sum(jnp.where(hit, info[:, :, top:], 0.0), axis=2)
    before = jnp.triu(jnp.ones((tok, tok), BF16), 1)
    place = mm(taken.astype(BF16).reshape(experts, tok), before, 1, 0).astype(jnp.int32)
    start = slots * (jnp.arange(experts // 2, dtype=jnp.int32) % GROUP)
    place = jnp.where(taken, place.reshape(taken.shape) + start[None, :, None], -1)
    place = place.reshape(2, -1, 1, GROUP * tok)
    gate = gate.reshape(2, -1, 1, GROUP * tok)

    pad = -units % 128
    first = after(me * units, x1)
    widen = lambda m: jnp.pad(m, ((0, pad), (0, 0)))
    columns = lambda m: widen(lax.dynamic_slice_in_dim(m, first, units, 1).T)
    sgu = jnp.concatenate([columns(s_gate), columns(s_up)], axis=0)
    sd = widen(lax.dynamic_slice_in_dim(s_down, first, units, 0))
    weights = (w_gate.swapaxes(1, 2), w_up.swapaxes(1, 2), w_down, sgu, sd)

    rows = experts // 2 * slots
    c2 = [spread(p, sizes, turn[0]) for p, turn in zip(halves(after(c1, x3)), turns)]
    ahead0 = forward_half(after(place[0], c2), gate[0], own_x, weights, rows)
    ahead1 = forward_half(place[1], gate[1], after(other_x, ahead0[0]), weights, rows)
    c3 = [spread(p, sizes, turn[1], ahead1[0]) for p, turn in zip(c2, turns)]
    own_c = flat(c3)
    back0 = backward_half(place[0], gate[0], own_c, weights, ahead0, rows)
    out_came = after([partner(p, sizes, 0, 1) for p in full(ahead1[:2])], back0[0])
    out = [list(t) for t in zip(full(ahead0[:2]), out_came)]
    out = [parts_for(t, sizes, turn[1]) for t, turn in zip(out, turns)]
    other_c = after([partner(p, sizes, 0, 1) for p in own_c], back0[0])
    back1 = backward_half(
        after(place[1], [sent for sent, _ in out]), gate[1], other_c, weights, ahead1, rows
    )

    out = [fold(*t, sizes, turn[1]) for t, turn in zip(out, turns)]
    out = [parts_for(after(t, back1[0]), sizes, turn[0]) for t, turn in zip(out, turns)]
    out_sent = [sent for sent, _ in out]
    ga, gb, da, db = shared_grads(
        after([back0[5], back1[5]], [sent for sent, _ in out]),
        [ahead0[7], ahead1[7]],
        [own_x[0], other_x[0], own_x[1], other_x[1]],
        [own_c[0], other_c[0], own_c[1], other_c[1]],
    )
    dx_came = after([partner(p, sizes, 0, 1) for p in full(after(back1[:2], out_sent))], ga)
    dx = [list(t) for t in zip(full(back0[:2]), dx_came)]
    dx = [parts_for(t, sizes, turn[1]) for t, turn in zip(dx, turns)]
    out = [fold(*t, sizes, turn[0]) for t, turn in zip(out, turns)]
    out = after(out, [sent for sent, _ in dx])
    out = [jnp.concatenate(p, axis=5) for p in zip(*out)]
    out = parts_for(out, sizes, 2)
    ga, gb, da, db = after((ga, gb, da, db), out[0])
    unit = units + pad
    both = jnp.concatenate([ga, gb], axis=1)
    grads = jnp.concatenate(
        [both[:units], both[unit : unit + units], jnp.concatenate([da, db], axis=1)[:units]], axis=0
    ).reshape(3 * units, experts, width // experts)
    index = np.arange(experts).reshape(sizes[2], sizes[1], 2).transpose(2, 1, 0).reshape(-1)
    where = jnp.asarray(np.argsort(index), jnp.int32)[me ^ jnp.arange(experts, dtype=jnp.int32)]
    score = jnp.stack(after([back0[6], back1[6]], ga)).reshape(experts, dp, share)
    score = score[where][:, shares_at].reshape(experts, tok)
    block = grads.shape[2]
    lines = -(-tok // block)
    high = score.astype(BF16)
    low = (score - high.astype(F32)).astype(BF16)
    extra = jnp.pad(jnp.stack([high, low]), ((0, 0), (0, 0), (0, lines * block - tok)))
    extra = extra.reshape(2, experts, lines, block).transpose(0, 2, 1, 3)
    send = jnp.concatenate([grads, extra.reshape(2 * lines, experts, block)], axis=0).transpose(1, 0, 2)
    got = lax.all_to_all(send, "expert", split_axis=0, concat_axis=0, tiled=True)
    grad_sg = got[:, :units].reshape(experts * units, -1).T
    grad_su = got[:, units : 2 * units].reshape(experts * units, -1).T
    grad_sd = got[:, 2 * units : 3 * units].reshape(experts * units, -1)
    scores = got[:, 3 * units :].reshape(experts, 2, lines * block)[:, :, :tok].astype(F32)
    scores = (scores[:, 0] + scores[:, 1]).T
    named = expert_ids[:, :, None] == jnp.arange(experts, dtype=jnp.int32)[None, None, :]
    gate_part = jnp.sum(jnp.where(named, scores[:, None, :], 0.0), axis=2)
    gate_grads = gate_part
    for k in range(1, dp):
        gate_grads = gate_grads + partner(gate_part, sizes, 3, k)

    grad_wg, grad_wu, grad_wd = expert_grads(
        [ahead0[2], ahead1[2]],
        after([back0[2], back1[2]], send),
        [back0[3], back1[3]],
        [back0[4], back1[4]],
        [ahead0[5], ahead1[5]],
    )
    out, dx = after(
        (fold(*out, sizes, 2), [fold(*t, sizes, turn[1]) for t, turn in zip(dx, turns)]), grad_wg
    )
    dx = [parts_for(t, sizes, turn[0]) for t, turn in zip(dx, turns)]
    out = after(out, [sent for sent, _ in dx])
    moe_out = both_halves(total(out).reshape(share, width), sizes)
    dx = [fold(*t, sizes, turn[0]) for t, turn in zip(dx, turns)]
    dx = [jnp.concatenate(p, axis=5) for p in zip(*dx)]
    dx = fold(*parts_for(dx, sizes, 2), sizes, 2)
    token_grads = both_halves(total(dx).reshape(share, width), sizes)
    grad_wg, grad_wu = grad_wg.swapaxes(1, 2), grad_wu.swapaxes(1, 2)
    return (moe_out, token_grads, gate_grads, grad_wg, grad_wu, grad_wd, grad_sg, grad_su, grad_sd)


def solution(mesh):
    row = P("expert", None)
    cols = P("expert", None, "dp")
    return jax.shard_map(
        local,
        mesh=mesh,
        in_specs=(
            row, row, row, cols, cols, P("expert", "dp", None),
            P(None, "dp"), P(None, "dp"), P("dp", None), row,
        ),
        out_specs=(
            row, row, row, cols, cols, P("expert", "dp", None),
            P("expert", "dp"), P("expert", "dp"), P("dp", "expert"),
        ),
        check_vma=False,
    )
```

```python
import functools

import jax
import jax.numpy as jnp
import numpy as np
from jax import lax
from jax.experimental import pallas as pl
from jax.experimental.pallas import tpu as pltpu
from jax.sharding import PartitionSpec as P

F32 = jnp.float32
BF16 = jnp.bfloat16
GROUP = 4
FACTS = 128
VMEM_LIMIT = 56 * 1024 * 1024


def mm(left, right, left_dim, right_dim):
    return lax.dot_general(
        left, right, (((left_dim,), (right_dim,)), ((), ())), preferred_element_type=F32
    )


def split_of(experts, dp):
    bits = experts.bit_length() - 1
    middle = (bits - 1) // 2
    return (2, 1 << middle, 1 << (bits - 1 - middle), dp)


def partner(array, sizes, dim, k):
    if dim == 3:
        axis, mask = "dp", k
    else:
        axis, mask = "expert", k * (1, 2, 2 * sizes[1])[dim]
    return lax.ppermute(array, axis, [(i, i ^ mask) for i in range(lax.axis_size(axis))])


def after(arrays, *earlier):
    return lax.optimization_barrier((arrays, earlier))[0]


def spread(out, sizes, dim, *earlier):
    came = [partner(out, sizes, dim, k) for k in range(1, sizes[dim])]
    return jnp.concatenate([out] + after(came, *earlier), axis=dim)


def total(terms):
    out = terms[0].astype(F32)
    for term in terms[1:]:
        out = out + term.astype(F32)
    return out.astype(BF16)


def parts_for(terms, sizes, dim):
    cut = lambda k: [lax.slice_in_dim(t, k, k + 1, axis=dim) for t in terms]
    stays = cut(0)
    if sizes[dim] > 2:
        stays = lax.optimization_barrier(stays)
    return [total(cut(k)) for k in range(1, sizes[dim])], stays


def fold(sent, stays, sizes, dim, *earlier):
    return stays + after([partner(part, sizes, dim, k + 1) for k, part in enumerate(sent)], *earlier)


def both_halves(rows, sizes):
    out = [rows] + [partner(rows, sizes, 3, k) for k in range(1, sizes[3])]
    out = jnp.stack(out)
    order = jnp.arange(sizes[3]) ^ lax.axis_index("dp")
    return out[order].reshape(-1, rows.shape[1])


def pick_of(place_ref, gate_ref, rows):
    place = place_ref[0]
    hit = lax.broadcasted_iota(jnp.int32, (rows, place.shape[1]), 0) == place
    gate = jnp.sum(jnp.where(hit, gate_ref[0], 0.0), axis=1, keepdims=True)
    return hit, hit.astype(BF16), gate


def take_rows(pick, a_ref, b_ref, rows_ref):
    rows, tokens = pick.shape
    parts = GROUP // 2
    half = a_ref.shape[1]
    for i in range(parts):
        r = slice(i * rows // parts, (i + 1) * rows // parts)
        t = slice(i * tokens // parts, (i + 1) * tokens // parts)
        rows_ref[r, :half] = mm(pick[r, t], a_ref[t, :], 1, 0).astype(BF16)
        rows_ref[r, half:] = mm(pick[r, t], b_ref[t, :], 1, 0).astype(BF16)


def put_rows(pick, rows, units, weight_ref, a_ref, b_ref):
    half = a_ref.shape[1]
    left = jnp.concatenate([pick.T, units], axis=1)
    for ref, cut in ((a_ref, slice(0, half)), (b_ref, slice(half, 2 * half))):
        right = jnp.concatenate([rows[:, cut], weight_ref[:, cut]], axis=0)
        ref[...] = mm(left, right, 1, 0).astype(BF16)


def fetch(sources, targets, sems):
    copies = [
        pltpu.make_async_copy(src.at[0], dst, sems.at[i])
        for i, (src, dst) in enumerate(zip(sources, targets))
    ]

    @pl.when(pl.program_id(0) == 0)
    def _():
        for copy in copies:
            copy.start()

    def ready(*which):
        @pl.when(pl.program_id(0) == 0)
        def _():
            for i in which:
                copies[i].wait()

    return ready


def forward_kernel(
    place_ref, gate_ref, xa_ref, xb_ref, wg_hbm, wu_hbm, wd_hbm, sgu_ref, sd_ref,
    oa_ref, ob_ref, xr_ref, gp_ref, up_ref, hid_ref, spre_ref, shid_ref,
    wg_ref, wu_ref, wd_ref, sems,
):
    ready = fetch((wg_hbm, wu_hbm, wd_hbm), (wg_ref, wu_ref, wd_ref), sems)
    hit, pick, gate = pick_of(place_ref, gate_ref, xr_ref.shape[0])
    half = xa_ref.shape[1]
    unit = sd_ref.shape[0]
    take_rows(pick, xa_ref, xb_ref, xr_ref)
    spre = mm(xa_ref[...], sgu_ref[:, :half], 1, 1) + mm(xb_ref[...], sgu_ref[:, half:], 1, 1)
    spre_ref[...] = spre
    sgp, sup = spre[:, :unit], spre[:, unit:]
    shid = (sgp * jax.nn.sigmoid(sgp) * sup).astype(BF16)
    shid_ref[...] = shid
    xr = xr_ref[...]
    ready(0, 1)
    gp = mm(xr, wg_ref[...], 1, 1)
    up = mm(xr, wu_ref[...], 1, 1)
    gp_ref[...] = gp
    up_ref[...] = up
    hid = (gp * jax.nn.sigmoid(gp) * up).astype(BF16)
    hid_ref[...] = hid
    ready(2)
    rows = (mm(hid, wd_ref[...], 1, 0) * gate).astype(BF16)
    put_rows(pick, rows, shid, sd_ref, oa_ref, ob_ref)


def backward_kernel(
    place_ref, gate_ref, ca_ref, cb_ref, wg_hbm, wu_hbm, wd_hbm, sgu_ref, sd_ref,
    gp_ref, up_ref, spre_ref,
    oa_ref, ob_ref, cs_ref, ggp_ref, ugp_ref, sgrad_ref, score_ref,
    wg_ref, wu_ref, wd_ref, sems, cr_ref,
):
    ready = fetch((wg_hbm, wu_hbm, wd_hbm), (wg_ref, wu_ref, wd_ref), sems)
    hit, pick, gate = pick_of(place_ref, gate_ref, cr_ref.shape[0])
    half = ca_ref.shape[1]
    unit = sd_ref.shape[0]
    take_rows(pick, ca_ref, cb_ref, cr_ref)
    sgp, sup = spre_ref[:, :unit], spre_ref[:, unit:]
    ssig = jax.nn.sigmoid(sgp)
    sgrad = mm(ca_ref[...], sd_ref[:, :half], 1, 1) + mm(cb_ref[...], sd_ref[:, half:], 1, 1)
    sgg = (sgrad * sup * ssig * (1.0 + sgp * (1.0 - ssig))).astype(BF16)
    sug = (sgrad * sgp * ssig).astype(BF16)
    both = jnp.concatenate([sgg, sug], axis=1)
    sgrad_ref[...] = both
    cr = cr_ref[...]
    cs_ref[...] = (cr.astype(F32) * gate).astype(BF16)
    ready(2)
    raw = mm(cr, wd_ref[...], 1, 1)
    gp, up = gp_ref[...], up_ref[...]
    sig = jax.nn.sigmoid(gp)
    silu = gp * sig
    score = jnp.sum(raw * (silu * up).astype(BF16).astype(F32), axis=1, keepdims=True)
    score_ref[0] = jnp.sum(jnp.where(hit, score, 0.0), axis=0, keepdims=True)
    grad = raw * gate
    ggp = (grad * up * sig * (1.0 + gp * (1.0 - sig))).astype(BF16)
    ugp = (grad * silu).astype(BF16)
    ggp_ref[...] = ggp
    ugp_ref[...] = ugp
    ready(0, 1)
    rows = (mm(ggp, wg_ref[...], 1, 0) + mm(ugp, wu_ref[...], 1, 0)).astype(BF16)
    put_rows(pick, rows, both, sgu_ref, oa_ref, ob_ref)


def spec_rows(rows, width):
    return pl.BlockSpec((rows, width), lambda i: (i, 0))


def spec_info(tok):
    return pl.BlockSpec((1, 1, tok), lambda i: (i, 0, 0))


def spec_whole(array):
    return pl.BlockSpec(array.shape, lambda i: (0,) * array.ndim, pipeline_mode=pl.Buffered(1))


def cost(flops, arrays):
    return pl.CostEstimate(
        flops=int(flops),
        bytes_accessed=int(sum(np.prod(a.shape) * a.dtype.itemsize for a in arrays)),
        transcendentals=0,
    )


def params():
    return pltpu.CompilerParams(
        dimension_semantics=("arbitrary",), vmem_limit_bytes=VMEM_LIMIT
    )


def half_call(name, kernel, place, gate, parts, weights, more, outs, scratch):
    groups, _, tokens = place.shape
    half = parts[1].shape[1]
    ff = weights[0].shape[1]
    hbm = pl.BlockSpec(memory_space=pl.ANY)
    by_group = lambda n: spec_rows(n.shape[0] // groups, n.shape[1])
    args = (place, gate, *parts, *weights, *more)
    rows = outs[2].shape[0]
    unit = weights[4].shape[0]
    flops = 6 * rows * ff * 2 * half + 6 * groups * tokens * unit * 2 * half
    flops += 4 * rows * tokens * half
    return pl.pallas_call(
        kernel,
        grid=(groups,),
        in_specs=[spec_info(tokens)] * 2
        + [spec_rows(p.shape[0] // groups, half) for p in parts]
        + [hbm] * 3
        + [spec_whole(w) for w in weights[3:]]
        + [by_group(m) for m in more],
        out_specs=[by_group(o) if len(o.shape) == 2 else spec_info(tokens) for o in outs],
        out_shape=outs,
        scratch_shapes=[pltpu.VMEM(w.shape[1:], BF16) for w in weights[:3]]
        + [pltpu.SemaphoreType.DMA((3,))]
        + scratch,
        compiler_params=params(),
        cost_estimate=cost(4 * flops, list(args) + outs),
        name=name,
    )(*args)


def forward_half(place, gate, parts, weights, rows):
    tokens, half = parts[1].shape
    ff, unit = weights[0].shape[1], weights[4].shape[0]
    shape = jax.ShapeDtypeStruct
    outs = [
        shape((tokens, half), BF16),
        shape((tokens, half), BF16),
        shape((rows, 2 * half), BF16),
        shape((rows, ff), F32),
        shape((rows, ff), F32),
        shape((rows, ff), BF16),
        shape((tokens, 2 * unit), F32),
        shape((tokens, unit), BF16),
    ]
    return half_call("forward_half", forward_kernel, place, gate, parts, weights, (), outs, [])


def backward_half(place, gate, parts, weights, ahead, rows):
    tokens, half = parts[1].shape
    ff, unit = weights[0].shape[1], weights[4].shape[0]
    shape = jax.ShapeDtypeStruct
    outs = [
        shape((tokens, half), BF16),
        shape((tokens, half), BF16),
        shape((rows, 2 * half), BF16),
        shape((rows, ff), BF16),
        shape((rows, ff), BF16),
        shape((tokens, 2 * unit), BF16),
        shape(place.shape, F32),
    ]
    more = (ahead[3], ahead[4], ahead[6])
    scratch = [pltpu.VMEM((rows // place.shape[0], 2 * half), BF16)]
    return half_call(
        "backward_half", backward_kernel, place, gate, parts, weights, more, outs, scratch
    )


def shared_grads_kernel(
    g0_ref, g1_ref, h0_ref, h1_ref, xa0, xa1, xb0, xb1, ca0, ca1, cb0, cb1,
    ga_ref, gb_ref, da_ref, db_ref, gt_ref, ht_ref,
):
    rows = g0_ref.shape[0]

    @pl.when(pl.program_id(0) == 0)
    def _():
        gt_ref[:, :rows] = g0_ref[...].T
        gt_ref[:, rows:] = g1_ref[...].T
        ht_ref[:, :rows] = h0_ref[...].T
        ht_ref[:, rows:] = h1_ref[...].T

    for out, t_ref, one, two in (
        (ga_ref, gt_ref, xa0, xa1),
        (gb_ref, gt_ref, xb0, xb1),
        (da_ref, ht_ref, ca0, ca1),
        (db_ref, ht_ref, cb0, cb1),
    ):
        part = mm(t_ref[:, :rows], one[...], 1, 0) + mm(t_ref[:, rows:], two[...], 1, 0)
        out[...] = part.astype(BF16)


def shared_grads(grads, hiddens, xs, cs):
    rows, half = xs[2].shape
    unit2, unit = grads[0].shape[1], hiddens[0].shape[1]
    tile = min(256, half)
    col = pl.BlockSpec((rows, tile), lambda i: (0, i))
    args = (*grads, *hiddens, *xs, *cs)
    out_shape = [jax.ShapeDtypeStruct((n, half), BF16) for n in (unit2, unit2, unit, unit)]
    return pl.pallas_call(
        shared_grads_kernel,
        grid=(half // tile,),
        in_specs=[spec_whole(a) for a in (*grads, *hiddens)] + [col] * 8,
        out_specs=[pl.BlockSpec((o.shape[0], tile), lambda i: (0, i)) for o in out_shape],
        out_shape=out_shape,
        scratch_shapes=[pltpu.VMEM((unit2, 2 * rows), BF16), pltpu.VMEM((unit, 2 * rows), BF16)],
        compiler_params=params(),
        cost_estimate=cost(8 * rows * half * (unit2 + unit), list(args) + out_shape),
        name="shared_grads",
    )(*args)


def expert_grads_kernel(
    x0_ref, x1_ref, c0_ref, c1_ref, g0_ref, g1_ref, u0_ref, u1_ref, h0_ref, h1_ref,
    wg_ref, wu_ref, wd_ref, gt_ref, ut_ref, ht_ref,
):
    rows = x0_ref.shape[0]

    @pl.when(pl.program_id(0) == 0)
    def _():
        for t_ref, one, two in (
            (gt_ref, g0_ref, g1_ref), (ut_ref, u0_ref, u1_ref), (ht_ref, h0_ref, h1_ref)
        ):
            t_ref[:, :rows] = one[...].T
            t_ref[:, rows:] = two[...].T

    x = jnp.concatenate([x0_ref[...], x1_ref[...]], axis=0)
    c = jnp.concatenate([c0_ref[...], c1_ref[...]], axis=0)
    wg_ref[0] = mm(gt_ref[...], x, 1, 0).astype(BF16)
    wu_ref[0] = mm(ut_ref[...], x, 1, 0).astype(BF16)
    wd_ref[0] = mm(ht_ref[...], c, 1, 0).astype(BF16)


def expert_grads(xr, cs, ggp, ugp, hid):
    rows, width = xr[0].shape
    ff = ggp[0].shape[1]
    tile = min(256, width)
    col = pl.BlockSpec((rows, tile), lambda i: (0, i))
    args = (*xr, *cs, *ggp, *ugp, *hid)
    out_shape = [jax.ShapeDtypeStruct((1, ff, width), BF16)] * 3
    return pl.pallas_call(
        expert_grads_kernel,
        grid=(width // tile,),
        in_specs=[col] * 4 + [spec_whole(a) for a in (*ggp, *ugp, *hid)],
        out_specs=[pl.BlockSpec((1, ff, tile), lambda i: (0, 0, i))] * 3,
        out_shape=out_shape,
        scratch_shapes=[pltpu.VMEM((ff, 2 * rows), BF16)] * 3,
        compiler_params=params(),
        cost_estimate=cost(24 * rows * width * ff, list(args) + out_shape),
        name="expert_grads",
    )(*args)


def local(tokens, expert_ids, gates, w_gate, w_up, w_down, s_gate, s_up, s_down, cotangent):
    tok, width = tokens.shape
    top = expert_ids.shape[1]
    experts, dp = lax.axis_size("expert"), lax.axis_size("dp")
    me, my_dp = lax.axis_index("expert"), lax.axis_index("dp")
    capacity = min(tok, 5 * tok * top // (4 * experts))
    slots = -(-capacity // 16) * 16
    units = s_gate.shape[1] // experts
    share, half = tok // dp, width // 2
    sizes = split_of(experts, dp)
    shares_at = my_dp ^ jnp.arange(dp, dtype=jnp.int32)
    turns = ((3, 1), (1, 3))
    shape = (1,) + sizes[1:] + (share, half)
    flat = lambda parts: [p.reshape(-1, p.shape[5]) for p in parts]
    full = lambda parts: [p.reshape(shape) for p in parts]

    def mine(rows):
        rows = lax.dynamic_slice_in_dim(rows, my_dp * share, share, 0)
        return [rows[:, i * half : (i + 1) * half].reshape(1, 1, 1, 1, share, half) for i in range(2)]

    halves = lambda rows: [rows[..., i * half : (i + 1) * half] for i in range(2)]
    mine = lambda rows: lax.dynamic_slice_in_dim(rows, my_dp * share, share, 0)[None, None, None, None]
    high = lax.reduce_precision(gates, 8, 7)
    facts = jnp.concatenate([expert_ids.astype(F32), high, gates - high], axis=1).astype(BF16)
    facts = jnp.pad(facts, ((0, 0), (0, FACTS - facts.shape[1])))
    x0 = mine(jnp.concatenate([tokens[:, :half], facts, tokens[:, half:]], axis=1))
    x1 = spread(x0, sizes, 2)
    x1 = (x1[..., : half + FACTS], x1[..., half + FACTS :])
    x2 = [spread(p, sizes, turn[0]) for p, turn in zip(x1, turns)]
    c1 = spread(after(mine(cotangent), x1), sizes, 2, x2)
    x3 = [spread(p, sizes, turn[1]) for p, turn in zip(x2, turns)]
    own_x = flat(x3)
    other_x = [partner(p, sizes, 0, 1) for p in own_x]

    before = jnp.triu(jnp.ones((tok, tok), BF16), 1)
    start = slots * (jnp.arange(experts // 2, dtype=jnp.int32) % GROUP)

    def routing(part):
        known = part[:, half : half + 3 * top].astype(F32).T.reshape(3, top, experts // 2, tok)
        hit = known[0] == me.astype(F32)
        taken = jnp.any(hit, axis=0)
        gate = jnp.sum(jnp.where(hit, known[1] + known[2], 0.0), axis=0)
        place = mm(taken.astype(BF16), before, 1, 0).astype(jnp.int32) + start[:, None]
        place = jnp.where(taken, place, -1)
        return place.reshape(-1, 1, GROUP * tok), gate.reshape(-1, 1, GROUP * tok)

    place, gate = zip(routing(own_x[0]), routing(other_x[0]))

    pad = -units % 128
    first = after(me * units, x1)
    widen = lambda m: jnp.pad(m, ((0, pad), (0, 0)))
    columns = lambda m: widen(lax.dynamic_slice_in_dim(m, first, units, 1).T)
    sgu = jnp.concatenate([columns(s_gate), columns(s_up)], axis=0)
    sd = widen(lax.dynamic_slice_in_dim(s_down, first, units, 0))
    weights = (w_gate.swapaxes(1, 2), w_up.swapaxes(1, 2), w_down, sgu, sd)

    rows = experts // 2 * slots
    c2 = [spread(p, sizes, turn[0]) for p, turn in zip(after(halves(c1), x3), turns)]
    ahead0 = forward_half(after(place[0], c2), gate[0], own_x, weights, rows)
    ahead1 = forward_half(place[1], gate[1], after(other_x, ahead0[0]), weights, rows)
    c3 = [spread(p, sizes, turn[1], ahead1[0]) for p, turn in zip(c2, turns)]
    own_c = flat(c3)
    back0 = backward_half(place[0], gate[0], own_c, weights, ahead0, rows)
    out_came = after([partner(p, sizes, 0, 1) for p in full(ahead1[:2])], back0[0])
    out = [list(t) for t in zip(full(ahead0[:2]), out_came)]
    out = [parts_for(t, sizes, turn[1]) for t, turn in zip(out, turns)]
    other_c = after([partner(p, sizes, 0, 1) for p in own_c], back0[0])
    back1 = backward_half(
        after(place[1], [sent for sent, _ in out]), gate[1], other_c, weights, ahead1, rows
    )

    out = [fold(*t, sizes, turn[1], back1[0]) for t, turn in zip(out, turns)]
    out = [parts_for(t, sizes, turn[0]) for t, turn in zip(out, turns)]
    out_sent = [sent for sent, _ in out]
    ga, gb, da, db = shared_grads(
        after([back0[5], back1[5]], out_sent),
        [ahead0[7], ahead1[7]],
        [own_x[0], other_x[0], own_x[1], other_x[1]],
        [own_c[0], other_c[0], own_c[1], other_c[1]],
    )
    dx_came = after([partner(p, sizes, 0, 1) for p in full(after(back1[:2], out_sent))], ga)
    dx = [list(t) for t in zip(full(back0[:2]), dx_came)]
    dx = [parts_for(t, sizes, turn[1]) for t, turn in zip(dx, turns)]
    dx_sent = [sent for sent, _ in dx]
    out = [fold(*t, sizes, turn[0], dx_sent) for t, turn in zip(out, turns)]
    out = [jnp.concatenate(p, axis=5) for p in zip(*out)]
    out = parts_for(out, sizes, 2)
    ga, gb, da, db = after((ga, gb, da, db), out[0])
    unit = units + pad
    both = jnp.concatenate([ga, gb], axis=1)
    grads = jnp.concatenate(
        [both[:units], both[unit : unit + units], jnp.concatenate([da, db], axis=1)[:units]], axis=0
    ).reshape(3 * units, experts, width // experts)
    index = np.arange(experts).reshape(sizes[2], sizes[1], 2).transpose(2, 1, 0).reshape(-1)
    where = jnp.asarray(np.argsort(index), jnp.int32)[me ^ jnp.arange(experts, dtype=jnp.int32)]
    score = jnp.stack(after([back0[6], back1[6]], ga)).reshape(experts, dp, share)
    score = score[where][:, shares_at].reshape(experts, tok)
    block = grads.shape[2]
    lines = -(-tok // block)
    high = lax.reduce_precision(score, 8, 7)
    extra = jnp.pad(jnp.stack([high, score - high]).astype(BF16), ((0, 0), (0, 0), (0, lines * block - tok)))
    extra = extra.reshape(2, experts, lines, block).transpose(0, 2, 1, 3)
    send = jnp.concatenate([grads, extra.reshape(2 * lines, experts, block)], axis=0).transpose(1, 0, 2)
    dx = [fold(*t, sizes, turn[1], send) for t, turn in zip(dx, turns)]
    dx = [parts_for(t, sizes, turn[0]) for t, turn in zip(dx, turns)]
    dx_sent = [sent for sent, _ in dx]
    got = lax.all_to_all(send, "expert", split_axis=0, concat_axis=0, tiled=True)
    got, out_came = after((got, fold(out[0], [], sizes, 2)), dx_sent)
    out = out[1] + out_came
    moe_out = both_halves(total(out).reshape(share, width), sizes)
    grad_sg = got[:, :units].reshape(experts * units, -1).T
    grad_su = got[:, units : 2 * units].reshape(experts * units, -1).T
    grad_sd = got[:, 2 * units : 3 * units].reshape(experts * units, -1)
    scores = got[:, 3 * units :].reshape(experts, 2, lines * block)[:, :, :tok].astype(F32)
    scores = (scores[:, 0] + scores[:, 1]).T
    named = expert_ids[:, :, None] == jnp.arange(experts, dtype=jnp.int32)[None, None, :]
    gate_part = jnp.sum(jnp.where(named, scores[:, None, :], 0.0), axis=2)
    gate_grads = gate_part
    for k in range(1, dp):
        gate_grads = gate_grads + partner(gate_part, sizes, 3, k)

    dx = [fold(*t, sizes, turn[0]) for t, turn in zip(dx, turns)]
    dx = [jnp.concatenate(p, axis=5) for p in zip(*dx)]
    dx = parts_for(dx, sizes, 2)
    grad_wg, grad_wu, grad_wd = expert_grads(
        [ahead0[2], ahead1[2]],
        after([back0[2], back1[2]], dx[0]),
        [back0[3], back1[3]],
        [back0[4], back1[4]],
        [ahead0[5], ahead1[5]],
    )
    token_grads = both_halves(total(fold(*dx, sizes, 2, grad_wg)).reshape(share, width), sizes)
    grad_wg, grad_wu = grad_wg.swapaxes(1, 2), grad_wu.swapaxes(1, 2)
    return (moe_out, token_grads, gate_grads, grad_wg, grad_wu, grad_wd, grad_sg, grad_su, grad_sd)


def solution(mesh):
    row = P("expert", None)
    cols = P("expert", None, "dp")
    return jax.shard_map(
        local,
        mesh=mesh,
        in_specs=(
            row, row, row, cols, cols, P("expert", "dp", None),
            P(None, "dp"), P(None, "dp"), P("dp", None), row,
        ),
        out_specs=(
            row, row, row, cols, cols, P("expert", "dp", None),
            P("expert", "dp"), P("expert", "dp"), P("dp", "expert"),
        ),
        check_vma=False,
    )
```

```python
import functools

import jax
import jax.numpy as jnp
import numpy as np
from jax import lax
from jax.experimental import pallas as pl
from jax.experimental.pallas import tpu as pltpu
from jax.sharding import PartitionSpec as P

F32 = jnp.float32
BF16 = jnp.bfloat16
GROUP = 8
SUB = 4
FACTS = 128
VMEM_LIMIT = 56 * 1024 * 1024


def mm(left, right, left_dim, right_dim):
    return lax.dot_general(
        left, right, (((left_dim,), (right_dim,)), ((), ())), preferred_element_type=F32
    )


def split_of(experts, dp):
    bits = experts.bit_length() - 1
    middle = (bits - 1) // 2
    return (2, 1 << middle, 1 << (bits - 1 - middle), dp)


def partner(array, sizes, dim, k):
    if dim == 3:
        axis, mask = "dp", k
    else:
        axis, mask = "expert", k * (1, 2, 2 * sizes[1])[dim]
    return lax.ppermute(array, axis, [(i, i ^ mask) for i in range(lax.axis_size(axis))])


def after(arrays, *earlier):
    return lax.optimization_barrier((arrays, earlier))[0]


def spread(out, sizes, dim, *earlier):
    came = [partner(out, sizes, dim, k) for k in range(1, sizes[dim])]
    return jnp.concatenate([out] + after(came, *earlier), axis=dim)


def total(terms):
    out = terms[0].astype(F32)
    for term in terms[1:]:
        out = out + term.astype(F32)
    return out.astype(BF16)


def parts_for(terms, sizes, dim):
    cut = lambda k: [lax.slice_in_dim(t, k, k + 1, axis=dim) for t in terms]
    stays = cut(0)
    if sizes[dim] > 2:
        stays = lax.optimization_barrier(stays)
    return [total(cut(k)) for k in range(1, sizes[dim])], stays


def fold(sent, stays, sizes, dim, *earlier):
    return stays + after([partner(part, sizes, dim, k + 1) for k, part in enumerate(sent)], *earlier)


def both_halves(rows, sizes):
    out = [rows] + [partner(rows, sizes, 3, k) for k in range(1, sizes[3])]
    out = jnp.stack(out)
    order = jnp.arange(sizes[3]) ^ lax.axis_index("dp")
    return out[order].reshape(-1, rows.shape[1])


def picks_of(place_ref, gate_ref, rows):
    parts = GROUP // SUB
    tokens = place_ref.shape[2] // parts
    hits, gates = [], []
    for i in range(parts):
        cut = slice(i * tokens, (i + 1) * tokens)
        place = place_ref[0, :, cut] - i * (rows // parts)
        hit = lax.broadcasted_iota(jnp.int32, (rows // parts, tokens), 0) == place
        hits.append(hit)
        gates.append(jnp.sum(jnp.where(hit, gate_ref[0, :, cut], 0.0), axis=1, keepdims=True))
    return hits, [hit.astype(BF16) for hit in hits], jnp.concatenate(gates, axis=0)


def take_rows(picks, a_ref, b_ref, rows_ref):
    half = a_ref.shape[1]
    rows, tokens = 2 * picks[0].shape[0] // SUB, 2 * picks[0].shape[1] // SUB
    for i in range(GROUP // 2):
        pick, j = picks[2 * i // SUB], i % (SUB // 2)
        pick = pick[j * rows : (j + 1) * rows, j * tokens : (j + 1) * tokens]
        r, t = slice(i * rows, (i + 1) * rows), slice(i * tokens, (i + 1) * tokens)
        rows_ref[r, :half] = mm(pick, a_ref[t, :], 1, 0).astype(BF16)
        rows_ref[r, half:] = mm(pick, b_ref[t, :], 1, 0).astype(BF16)


def put_rows(picks, rows, units, weight_ref, cut, out_ref):
    n, tokens = picks[0].shape
    for i, pick in enumerate(picks):
        t = slice(i * tokens, (i + 1) * tokens)
        left = jnp.concatenate([pick.T, units[t, :]], axis=1)
        right = jnp.concatenate([rows[i * n : (i + 1) * n, cut], weight_ref[:, cut]], axis=0)
        out_ref[t, :] = mm(left, right, 1, 0).astype(BF16)


def store(source, target, sem):
    n = source.shape[0]
    at = pl.multiple_of(pl.program_id(0) * n, n)
    copy = pltpu.make_async_copy(source, target.at[pl.ds(at, n)], sem)
    copy.start()
    return copy


def fetch(sources, targets, sems):
    copies = [
        pltpu.make_async_copy(src.at[0], dst, sems.at[i])
        for i, (src, dst) in enumerate(zip(sources, targets))
    ]

    @pl.when(pl.program_id(0) == 0)
    def _():
        for copy in copies:
            copy.start()

    def ready(*which):
        @pl.when(pl.program_id(0) == 0)
        def _():
            for i in which:
                copies[i].wait()

    return ready


def forward_kernel(
    place_ref, gate_ref, xa_ref, xb_ref, wg_hbm, wu_hbm, wd_hbm, sgu_ref, sd_ref,
    oa_hbm, ob_hbm, xr_hbm, gp_hbm, up_hbm, hid_hbm, spre_ref, shid_ref,
    wg_ref, wu_ref, wd_ref, sems, oa_ref, ob_ref, xr_ref, gp_ref, up_ref, hid_ref, out_sems,
):
    ready = fetch((wg_hbm, wu_hbm, wd_hbm), (wg_ref, wu_ref, wd_ref), sems)
    hits, picks, gate = picks_of(place_ref, gate_ref, xr_ref.shape[0])
    half = xa_ref.shape[1]
    unit = sd_ref.shape[0]
    take_rows(picks, xa_ref, xb_ref, xr_ref)
    stores = [store(xr_ref, xr_hbm, out_sems.at[0])]
    spre = mm(xa_ref[...], sgu_ref[:, :half], 1, 1) + mm(xb_ref[...], sgu_ref[:, half:], 1, 1)
    spre_ref[...] = spre
    sgp, sup = spre[:, :unit], spre[:, unit:]
    shid = (sgp * jax.nn.sigmoid(sgp) * sup).astype(BF16)
    shid_ref[...] = shid
    xr = xr_ref[...]
    ready(0, 1)
    gp = mm(xr, wg_ref[...], 1, 1)
    gp_ref[...] = gp
    stores.append(store(gp_ref, gp_hbm, out_sems.at[1]))
    up = mm(xr, wu_ref[...], 1, 1)
    up_ref[...] = up
    stores.append(store(up_ref, up_hbm, out_sems.at[2]))
    hid = (gp * jax.nn.sigmoid(gp) * up).astype(BF16)
    hid_ref[...] = hid
    stores.append(store(hid_ref, hid_hbm, out_sems.at[3]))
    ready(2)
    rows = (mm(hid, wd_ref[...], 1, 0) * gate).astype(BF16)
    put_rows(picks, rows, shid, sd_ref, slice(0, half), oa_ref)
    stores.append(store(oa_ref, oa_hbm, out_sems.at[4]))
    put_rows(picks, rows, shid, sd_ref, slice(half, 2 * half), ob_ref)
    stores.append(store(ob_ref, ob_hbm, out_sems.at[5]))
    for copy in stores:
        copy.wait()


def backward_kernel(
    place_ref, gate_ref, ca_ref, cb_ref, wg_hbm, wu_hbm, wd_hbm, sgu_ref, sd_ref,
    gp_ref, up_ref, spre_ref,
    oa_hbm, ob_hbm, cs_hbm, ggp_hbm, ugp_hbm, sgrad_ref, score_ref,
    wg_ref, wu_ref, wd_ref, sems, oa_ref, ob_ref, cs_ref, ggp_ref, ugp_ref, cr_ref, out_sems,
):
    ready = fetch((wg_hbm, wu_hbm, wd_hbm), (wg_ref, wu_ref, wd_ref), sems)
    hits, picks, gate = picks_of(place_ref, gate_ref, cr_ref.shape[0])
    half = ca_ref.shape[1]
    unit = sd_ref.shape[0]
    take_rows(picks, ca_ref, cb_ref, cr_ref)
    sgp, sup = spre_ref[:, :unit], spre_ref[:, unit:]
    ssig = jax.nn.sigmoid(sgp)
    sgrad = mm(ca_ref[...], sd_ref[:, :half], 1, 1) + mm(cb_ref[...], sd_ref[:, half:], 1, 1)
    sgg = (sgrad * sup * ssig * (1.0 + sgp * (1.0 - ssig))).astype(BF16)
    sug = (sgrad * sgp * ssig).astype(BF16)
    both = jnp.concatenate([sgg, sug], axis=1)
    sgrad_ref[...] = both
    cr = cr_ref[...]
    cs_ref[...] = (cr.astype(F32) * gate).astype(BF16)
    stores = [store(cs_ref, cs_hbm, out_sems.at[0])]
    ready(2)
    raw = mm(cr, wd_ref[...], 1, 1)
    gp, up = gp_ref[...], up_ref[...]
    sig = jax.nn.sigmoid(gp)
    silu = gp * sig
    score = jnp.sum(raw * (silu * up).astype(BF16).astype(F32), axis=1, keepdims=True)
    n, tokens = hits[0].shape
    for i, hit in enumerate(hits):
        part = jnp.where(hit, score[i * n : (i + 1) * n, :], 0.0)
        score_ref[0, :, i * tokens : (i + 1) * tokens] = jnp.sum(part, axis=0, keepdims=True)
    grad = raw * gate
    ggp = (grad * up * sig * (1.0 + gp * (1.0 - sig))).astype(BF16)
    ugp = (grad * silu).astype(BF16)
    ggp_ref[...] = ggp
    stores.append(store(ggp_ref, ggp_hbm, out_sems.at[1]))
    ugp_ref[...] = ugp
    stores.append(store(ugp_ref, ugp_hbm, out_sems.at[2]))
    ready(0, 1)
    rows = (mm(ggp, wg_ref[...], 1, 0) + mm(ugp, wu_ref[...], 1, 0)).astype(BF16)
    put_rows(picks, rows, both, sgu_ref, slice(0, half), oa_ref)
    stores.append(store(oa_ref, oa_hbm, out_sems.at[3]))
    put_rows(picks, rows, both, sgu_ref, slice(half, 2 * half), ob_ref)
    stores.append(store(ob_ref, ob_hbm, out_sems.at[4]))
    for copy in stores:
        copy.wait()


def spec_rows(rows, width):
    return pl.BlockSpec((rows, width), lambda i: (i, 0))


def spec_info(tok):
    return pl.BlockSpec((1, 1, tok), lambda i: (i, 0, 0))


def spec_whole(array):
    return pl.BlockSpec(array.shape, lambda i: (0,) * array.ndim, pipeline_mode=pl.Buffered(1))


def cost(flops, arrays):
    return pl.CostEstimate(
        flops=int(flops),
        bytes_accessed=int(sum(np.prod(a.shape) * a.dtype.itemsize for a in arrays)),
        transcendentals=0,
    )


def params():
    return pltpu.CompilerParams(
        dimension_semantics=("arbitrary",), vmem_limit_bytes=VMEM_LIMIT
    )


def half_call(name, kernel, place, gate, parts, weights, more, outs, own, scratch):
    groups, _, tokens = place.shape
    half = parts[1].shape[1]
    ff = weights[0].shape[1]
    hbm = pl.BlockSpec(memory_space=pl.ANY)
    once = dict(pipeline_mode=pl.Buffered(1)) if groups == 1 else {}
    by_group = lambda n: pl.BlockSpec((n.shape[0] // groups, n.shape[1]), lambda i: (i, 0), **once)
    args = (place, gate, *parts, *weights, *more)
    rows = outs[2].shape[0]
    unit = weights[4].shape[0]
    flops = 6 * rows * ff * 2 * half + 6 * groups * tokens * unit * 2 * half
    flops += 4 * rows * tokens * half
    return pl.pallas_call(
        kernel,
        grid=(groups,),
        in_specs=[spec_info(tokens)] * 2
        + [pl.BlockSpec((tokens, half), lambda i: (i, 0), **once)] * 2
        + [hbm] * 3
        + [spec_whole(w) for w in weights[3:]]
        + [by_group(m) for m in more],
        out_specs=[hbm] * own
        + [by_group(o) if len(o.shape) == 2 else spec_info(tokens) for o in outs[own:]],
        out_shape=outs,
        scratch_shapes=[pltpu.VMEM(w.shape[1:], BF16) for w in weights[:3]]
        + [pltpu.SemaphoreType.DMA((3,))]
        + [pltpu.VMEM((o.shape[0] // groups, o.shape[1]), o.dtype) for o in outs[:own]]
        + scratch
        + [pltpu.SemaphoreType.DMA((own,))],
        compiler_params=params(),
        cost_estimate=cost(4 * flops, list(args) + outs),
        name=name,
    )(*args)


def forward_half(place, gate, parts, weights, rows):
    tokens, half = parts[1].shape
    ff, unit = weights[0].shape[1], weights[4].shape[0]
    shape = jax.ShapeDtypeStruct
    outs = [
        shape((tokens, half), BF16),
        shape((tokens, half), BF16),
        shape((rows, 2 * half), BF16),
        shape((rows, ff), F32),
        shape((rows, ff), F32),
        shape((rows, ff), BF16),
        shape((tokens, 2 * unit), F32),
        shape((tokens, unit), BF16),
    ]
    return half_call("forward_half", forward_kernel, place, gate, parts, weights, (), outs, 6, [])


def backward_half(place, gate, parts, weights, ahead, rows):
    tokens, half = parts[1].shape
    ff, unit = weights[0].shape[1], weights[4].shape[0]
    shape = jax.ShapeDtypeStruct
    outs = [
        shape((tokens, half), BF16),
        shape((tokens, half), BF16),
        shape((rows, 2 * half), BF16),
        shape((rows, ff), BF16),
        shape((rows, ff), BF16),
        shape((tokens, 2 * unit), BF16),
        shape(place.shape, F32),
    ]
    more = (ahead[3], ahead[4], ahead[6])
    scratch = [pltpu.VMEM((rows // place.shape[0], 2 * half), BF16)]
    return half_call(
        "backward_half", backward_kernel, place, gate, parts, weights, more, outs, 5, scratch
    )


def shared_grads_kernel(
    g0_ref, g1_ref, h0_ref, h1_ref, xa0, xa1, xb0, xb1, ca0, ca1, cb0, cb1,
    ga_ref, gb_ref, da_ref, db_ref, gt_ref, ht_ref,
):
    rows = g0_ref.shape[0]

    @pl.when(pl.program_id(0) == 0)
    def _():
        gt_ref[:, :rows] = g0_ref[...].T
        gt_ref[:, rows:] = g1_ref[...].T
        ht_ref[:, :rows] = h0_ref[...].T
        ht_ref[:, rows:] = h1_ref[...].T

    for out, t_ref, one, two in (
        (ga_ref, gt_ref, xa0, xa1),
        (gb_ref, gt_ref, xb0, xb1),
        (da_ref, ht_ref, ca0, ca1),
        (db_ref, ht_ref, cb0, cb1),
    ):
        part = mm(t_ref[:, :rows], one[...], 1, 0) + mm(t_ref[:, rows:], two[...], 1, 0)
        out[...] = part.astype(BF16)


def shared_grads(grads, hiddens, xs, cs):
    rows, half = xs[2].shape
    unit2, unit = grads[0].shape[1], hiddens[0].shape[1]
    tile = min(256, half)
    col = pl.BlockSpec((rows, tile), lambda i: (0, i))
    args = (*grads, *hiddens, *xs, *cs)
    out_shape = [jax.ShapeDtypeStruct((n, half), BF16) for n in (unit2, unit2, unit, unit)]
    return pl.pallas_call(
        shared_grads_kernel,
        grid=(half // tile,),
        in_specs=[spec_whole(a) for a in (*grads, *hiddens)] + [col] * 8,
        out_specs=[pl.BlockSpec((o.shape[0], tile), lambda i: (0, i)) for o in out_shape],
        out_shape=out_shape,
        scratch_shapes=[pltpu.VMEM((unit2, 2 * rows), BF16), pltpu.VMEM((unit, 2 * rows), BF16)],
        compiler_params=params(),
        cost_estimate=cost(8 * rows * half * (unit2 + unit), list(args) + out_shape),
        name="shared_grads",
    )(*args)


def expert_grads_kernel(
    x0_ref, x1_ref, c0_ref, c1_ref, g0_ref, g1_ref, u0_ref, u1_ref, h0_ref, h1_ref,
    wg_ref, wu_ref, wd_ref, gt_ref, ut_ref, ht_ref,
):
    rows = x0_ref.shape[0]

    @pl.when(pl.program_id(0) == 0)
    def _():
        for t_ref, one, two in (
            (gt_ref, g0_ref, g1_ref), (ut_ref, u0_ref, u1_ref), (ht_ref, h0_ref, h1_ref)
        ):
            t_ref[:, :rows] = one[...].T
            t_ref[:, rows:] = two[...].T

    x = jnp.concatenate([x0_ref[...], x1_ref[...]], axis=0)
    c = jnp.concatenate([c0_ref[...], c1_ref[...]], axis=0)
    wg_ref[0] = mm(gt_ref[...], x, 1, 0).astype(BF16)
    wu_ref[0] = mm(ut_ref[...], x, 1, 0).astype(BF16)
    wd_ref[0] = mm(ht_ref[...], c, 1, 0).astype(BF16)


def expert_grads(xr, cs, ggp, ugp, hid):
    rows, width = xr[0].shape
    ff = ggp[0].shape[1]
    tile = min(256, width)
    col = pl.BlockSpec((rows, tile), lambda i: (0, i))
    args = (*xr, *cs, *ggp, *ugp, *hid)
    out_shape = [jax.ShapeDtypeStruct((1, ff, width), BF16)] * 3
    return pl.pallas_call(
        expert_grads_kernel,
        grid=(width // tile,),
        in_specs=[col] * 4 + [spec_whole(a) for a in (*ggp, *ugp, *hid)],
        out_specs=[pl.BlockSpec((1, ff, tile), lambda i: (0, 0, i))] * 3,
        out_shape=out_shape,
        scratch_shapes=[pltpu.VMEM((ff, 2 * rows), BF16)] * 3,
        compiler_params=params(),
        cost_estimate=cost(24 * rows * width * ff, list(args) + out_shape),
        name="expert_grads",
    )(*args)


def local(tokens, expert_ids, gates, w_gate, w_up, w_down, s_gate, s_up, s_down, cotangent):
    tok, width = tokens.shape
    top = expert_ids.shape[1]
    experts, dp = lax.axis_size("expert"), lax.axis_size("dp")
    me, my_dp = lax.axis_index("expert"), lax.axis_index("dp")
    capacity = min(tok, 5 * tok * top // (4 * experts))
    slots = -(-capacity // 16) * 16
    units = s_gate.shape[1] // experts
    share, half = tok // dp, width // 2
    sizes = split_of(experts, dp)
    shares_at = my_dp ^ jnp.arange(dp, dtype=jnp.int32)
    turns = ((3, 1), (1, 3))
    shape = (1,) + sizes[1:] + (share, half)
    flat = lambda parts: [p.reshape(-1, p.shape[5]) for p in parts]
    full = lambda parts: [p.reshape(shape) for p in parts]

    def mine(rows):
        rows = lax.dynamic_slice_in_dim(rows, my_dp * share, share, 0)
        return [rows[:, i * half : (i + 1) * half].reshape(1, 1, 1, 1, share, half) for i in range(2)]

    halves = lambda rows: [rows[..., i * half : (i + 1) * half] for i in range(2)]
    mine = lambda rows: lax.dynamic_slice_in_dim(rows, my_dp * share, share, 0)[None, None, None, None]
    high = lax.reduce_precision(gates, 8, 7)
    facts = jnp.concatenate([expert_ids.astype(F32), high, gates - high], axis=1).astype(BF16)
    facts = jnp.pad(facts, ((0, 0), (0, FACTS - facts.shape[1])))
    x0 = mine(jnp.concatenate([tokens[:, :half], facts, tokens[:, half:]], axis=1))
    x1 = spread(x0, sizes, 2)
    x1 = (x1[..., : half + FACTS], x1[..., half + FACTS :])
    x2 = [spread(p, sizes, turn[0]) for p, turn in zip(x1, turns)]
    c1 = spread(after(mine(cotangent), x1), sizes, 2, x2)
    x3 = [spread(p, sizes, turn[1]) for p, turn in zip(x2, turns)]
    own_x = flat(x3)
    other_x = [partner(p, sizes, 0, 1) for p in own_x]

    before = jnp.triu(jnp.ones((tok, tok), BF16), 1)
    start = slots * (jnp.arange(experts // 2, dtype=jnp.int32) % GROUP)

    def routing(part):
        known = part[:, half : half + 3 * top].astype(F32).T.reshape(3, top, experts // 2, tok)
        hit = known[0] == me.astype(F32)
        taken = jnp.any(hit, axis=0)
        gate = jnp.sum(jnp.where(hit, known[1] + known[2], 0.0), axis=0)
        place = mm(taken.astype(BF16), before, 1, 0).astype(jnp.int32) + start[:, None]
        place = jnp.where(taken, place, -1)
        return place.reshape(-1, 1, GROUP * tok), gate.reshape(-1, 1, GROUP * tok)

    place, gate = zip(routing(own_x[0]), routing(other_x[0]))

    pad = -units % 128
    first = after(me * units, x1)
    widen = lambda m: jnp.pad(m, ((0, pad), (0, 0)))
    columns = lambda m: widen(lax.dynamic_slice_in_dim(m, first, units, 1).T)
    sgu = jnp.concatenate([columns(s_gate), columns(s_up)], axis=0)
    sd = widen(lax.dynamic_slice_in_dim(s_down, first, units, 0))
    weights = (w_gate.swapaxes(1, 2), w_up.swapaxes(1, 2), w_down, sgu, sd)

    rows = experts // 2 * slots
    c2 = [spread(p, sizes, turn[0]) for p, turn in zip(after(halves(c1), x3), turns)]
    ahead0 = forward_half(after(place[0], c2), gate[0], own_x, weights, rows)
    ahead1 = forward_half(place[1], gate[1], after(other_x, ahead0[0]), weights, rows)
    c3 = [spread(p, sizes, turn[1], ahead1[0]) for p, turn in zip(c2, turns)]
    own_c = flat(c3)
    back0 = backward_half(place[0], gate[0], own_c, weights, ahead0, rows)
    out_came = after([partner(p, sizes, 0, 1) for p in full(ahead1[:2])], back0[0])
    out = [list(t) for t in zip(full(ahead0[:2]), out_came)]
    out = [parts_for(t, sizes, turn[1]) for t, turn in zip(out, turns)]
    other_c = after([partner(p, sizes, 0, 1) for p in own_c], back0[0])
    back1 = backward_half(
        after(place[1], [sent for sent, _ in out]), gate[1], other_c, weights, ahead1, rows
    )

    out = [fold(*t, sizes, turn[1], back1[0]) for t, turn in zip(out, turns)]
    out_came = [t[-1] for t in out]
    out = [parts_for(t, sizes, turn[0]) for t, turn in zip(out, turns)]
    out_sent = [sent for sent, _ in out]
    ga, gb, da, db = shared_grads(
        after([back0[5], back1[5]], out_sent),
        [ahead0[7], ahead1[7]],
        [own_x[0], other_x[0], own_x[1], other_x[1]],
        [own_c[0], other_c[0], own_c[1], other_c[1]],
    )
    ahead_of_dx = out_came if dp == 2 else out_sent
    dx_came = after([partner(p, sizes, 0, 1) for p in full(after(back1[:2], ahead_of_dx))], ga)
    dx = [list(t) for t in zip(full(back0[:2]), dx_came)]
    dx = [parts_for(t, sizes, turn[1]) for t, turn in zip(dx, turns)]
    dx_sent = [sent for sent, _ in dx]
    out = [fold(*t, sizes, turn[0], dx_sent) for t, turn in zip(out, turns)]
    out = [jnp.concatenate(p, axis=5) for p in zip(*out)]
    out = parts_for(out, sizes, 2)
    ga, gb, da, db = after((ga, gb, da, db), out[0])
    unit = units + pad
    both = jnp.concatenate([ga, gb], axis=1)
    grads = jnp.concatenate(
        [both[:units], both[unit : unit + units], jnp.concatenate([da, db], axis=1)[:units]], axis=0
    ).reshape(3 * units, experts, width // experts)
    index = np.arange(experts).reshape(sizes[2], sizes[1], 2).transpose(2, 1, 0).reshape(-1)
    where = jnp.asarray(np.argsort(index), jnp.int32)[me ^ jnp.arange(experts, dtype=jnp.int32)]
    score = jnp.stack(after([back0[6], back1[6]], ga)).reshape(experts, dp, share)
    score = score[where][:, shares_at].reshape(experts, tok)
    block = grads.shape[2]
    lines = -(-tok // block)
    high = lax.reduce_precision(score, 8, 7)
    extra = jnp.pad(jnp.stack([high, score - high]).astype(BF16), ((0, 0), (0, 0), (0, lines * block - tok)))
    extra = extra.reshape(2, experts, lines, block).transpose(0, 2, 1, 3)
    send = jnp.concatenate([grads, extra.reshape(2 * lines, experts, block)], axis=0).transpose(1, 0, 2)
    got = lax.all_to_all(send, "expert", split_axis=0, concat_axis=0, tiled=True)
    dx = [fold(*t, sizes, turn[1], got) for t, turn in zip(dx, turns)]
    dx = [parts_for(t, sizes, turn[0]) for t, turn in zip(dx, turns)]
    dx_sent = [sent for sent, _ in dx]
    got, out_came = after((got, fold(out[0], [], sizes, 2)), dx_sent)
    out = out[1] + out_came
    moe_out = both_halves(total(out).reshape(share, width), sizes)
    grad_sg = got[:, :units].reshape(experts * units, -1).T
    grad_su = got[:, units : 2 * units].reshape(experts * units, -1).T
    grad_sd = got[:, 2 * units : 3 * units].reshape(experts * units, -1)
    scores = got[:, 3 * units :].reshape(experts, 2, lines * block)[:, :, :tok].astype(F32)
    scores = (scores[:, 0] + scores[:, 1]).T
    named = expert_ids[:, :, None] == jnp.arange(experts, dtype=jnp.int32)[None, None, :]
    gate_part = jnp.sum(jnp.where(named, scores[:, None, :], 0.0), axis=2)
    gate_grads = gate_part
    for k in range(1, dp):
        gate_grads = gate_grads + partner(gate_part, sizes, 3, k)

    dx = [fold(*t, sizes, turn[0]) for t, turn in zip(dx, turns)]
    dx = [jnp.concatenate(p, axis=5) for p in zip(*dx)]
    dx = parts_for(dx, sizes, 2)
    grad_wg, grad_wu, grad_wd = expert_grads(
        [ahead0[2], ahead1[2]],
        after([back0[2], back1[2]], dx[0]),
        [back0[3], back1[3]],
        [back0[4], back1[4]],
        [ahead0[5], ahead1[5]],
    )
    token_grads = both_halves(total(fold(*dx, sizes, 2, grad_wg)).reshape(share, width), sizes)
    grad_wg, grad_wu = grad_wg.swapaxes(1, 2), grad_wu.swapaxes(1, 2)
    return (moe_out, token_grads, gate_grads, grad_wg, grad_wu, grad_wd, grad_sg, grad_su, grad_sd)


def solution(mesh):
    row = P("expert", None)
    cols = P("expert", None, "dp")
    return jax.shard_map(
        local,
        mesh=mesh,
        in_specs=(
            row, row, row, cols, cols, P("expert", "dp", None),
            P(None, "dp"), P(None, "dp"), P("dp", None), row,
        ),
        out_specs=(
            row, row, row, cols, cols, P("expert", "dp", None),
            P("expert", "dp"), P("expert", "dp"), P("dp", "expert"),
        ),
        check_vma=False,
    )
```

```python
import functools

import jax
import jax.numpy as jnp
import numpy as np
from jax import lax
from jax.experimental import pallas as pl
from jax.experimental.pallas import tpu as pltpu
from jax.sharding import PartitionSpec as P

F32 = jnp.float32
BF16 = jnp.bfloat16
GROUP = 8
SUB = 4
FACTS = 128
VMEM_LIMIT = 56 * 1024 * 1024


def mm(left, right, left_dim, right_dim):
    return lax.dot_general(
        left, right, (((left_dim,), (right_dim,)), ((), ())), preferred_element_type=F32
    )


def split_of(experts, dp):
    bits = experts.bit_length() - 1
    middle = (bits - 1) // 2
    return (2, 1 << middle, 1 << (bits - 1 - middle), dp)


def partner(array, sizes, dim, k):
    if dim == 3:
        axis, mask = "dp", k
    else:
        axis, mask = "expert", k * (1, 2, 2 * sizes[1])[dim]
    return lax.ppermute(array, axis, [(i, i ^ mask) for i in range(lax.axis_size(axis))])


def after(arrays, *earlier):
    return lax.optimization_barrier((arrays, earlier))[0]


def spread(out, sizes, dim, *earlier):
    came = [partner(out, sizes, dim, k) for k in range(1, sizes[dim])]
    return jnp.concatenate([out] + after(came, *earlier), axis=dim)


def total(terms):
    out = terms[0].astype(F32)
    for term in terms[1:]:
        out = out + term.astype(F32)
    return out.astype(BF16)


def parts_for(terms, sizes, dim):
    cut = lambda k: total([lax.slice_in_dim(t, k, k + 1, axis=dim) for t in terms])
    return [cut(k) for k in range(1, sizes[dim])], [cut(0)]


def fold(sent, stays, sizes, dim, *earlier):
    return stays + after([partner(part, sizes, dim, k + 1) for k, part in enumerate(sent)], *earlier)


def both_halves(rows, sizes):
    out = [rows] + [partner(rows, sizes, 3, k) for k in range(1, sizes[3])]
    out = jnp.stack(out)
    order = jnp.arange(sizes[3]) ^ lax.axis_index("dp")
    return out[order].reshape(-1, rows.shape[1])


def picks_of(place_ref, gate_ref, rows):
    parts = GROUP // SUB
    tokens = place_ref.shape[2] // parts
    hits, gates = [], []
    for i in range(parts):
        cut = slice(i * tokens, (i + 1) * tokens)
        place = place_ref[0, :, cut] - i * (rows // parts)
        hit = lax.broadcasted_iota(jnp.int32, (rows // parts, tokens), 0) == place
        hits.append(hit)
        gates.append(jnp.sum(jnp.where(hit, gate_ref[0, :, cut], 0.0), axis=1, keepdims=True))
    return hits, [hit.astype(BF16) for hit in hits], jnp.concatenate(gates, axis=0)


def take_rows(picks, a_ref, b_ref, rows_ref):
    half = a_ref.shape[1]
    rows, tokens = 2 * picks[0].shape[0] // SUB, 2 * picks[0].shape[1] // SUB
    for i in range(GROUP // 2):
        pick, j = picks[2 * i // SUB], i % (SUB // 2)
        pick = pick[j * rows : (j + 1) * rows, j * tokens : (j + 1) * tokens]
        r, t = slice(i * rows, (i + 1) * rows), slice(i * tokens, (i + 1) * tokens)
        rows_ref[r, :half] = mm(pick, a_ref[t, :], 1, 0).astype(BF16)
        rows_ref[r, half:] = mm(pick, b_ref[t, :], 1, 0).astype(BF16)


def put_rows(picks, rows, units, weight_ref, cut, out_ref):
    n, tokens = picks[0].shape
    for i, pick in enumerate(picks):
        t = slice(i * tokens, (i + 1) * tokens)
        left = jnp.concatenate([pick.T, units[t, :]], axis=1)
        right = jnp.concatenate([rows[i * n : (i + 1) * n, cut], weight_ref[:, cut]], axis=0)
        out_ref[t, :] = mm(left, right, 1, 0).astype(BF16)


def store(source, target, sem):
    n = source.shape[0]
    at = pl.multiple_of(pl.program_id(0) * n, n)
    copy = pltpu.make_async_copy(source, target.at[pl.ds(at, n)], sem)
    copy.start()
    return copy


def fetch(sources, targets, sems):
    copies = [
        pltpu.make_async_copy(src.at[0], dst, sems.at[i])
        for i, (src, dst) in enumerate(zip(sources, targets))
    ]

    @pl.when(pl.program_id(0) == 0)
    def _():
        for copy in copies:
            copy.start()

    def ready(*which):
        @pl.when(pl.program_id(0) == 0)
        def _():
            for i in which:
                copies[i].wait()

    return ready


def forward_kernel(
    place_ref, gate_ref, xa_ref, xb_ref, wg_hbm, wu_hbm, wd_hbm, sgu_ref, sd_ref,
    oa_hbm, ob_hbm, xr_hbm, gp_hbm, up_hbm, hid_hbm, spre_ref, shid_ref,
    wg_ref, wu_ref, wd_ref, sems, oa_ref, ob_ref, xr_ref, gp_ref, up_ref, hid_ref, out_sems,
):
    ready = fetch((wg_hbm, wu_hbm, wd_hbm), (wg_ref, wu_ref, wd_ref), sems)
    hits, picks, gate = picks_of(place_ref, gate_ref, xr_ref.shape[0])
    half = xa_ref.shape[1]
    unit = sd_ref.shape[0]
    take_rows(picks, xa_ref, xb_ref, xr_ref)
    stores = [store(xr_ref, xr_hbm, out_sems.at[0])]
    spre = mm(xa_ref[...], sgu_ref[:, :half], 1, 1) + mm(xb_ref[...], sgu_ref[:, half:], 1, 1)
    spre_ref[...] = spre
    sgp, sup = spre[:, :unit], spre[:, unit:]
    shid = (sgp * jax.nn.sigmoid(sgp) * sup).astype(BF16)
    shid_ref[...] = shid
    xr = xr_ref[...]
    ready(0, 1)
    gp = mm(xr, wg_ref[...], 1, 1)
    gp_ref[...] = gp
    stores.append(store(gp_ref, gp_hbm, out_sems.at[1]))
    up = mm(xr, wu_ref[...], 1, 1)
    up_ref[...] = up
    stores.append(store(up_ref, up_hbm, out_sems.at[2]))
    hid = (gp * jax.nn.sigmoid(gp) * up).astype(BF16)
    hid_ref[...] = hid
    stores.append(store(hid_ref, hid_hbm, out_sems.at[3]))
    ready(2)
    rows = (mm(hid, wd_ref[...], 1, 0) * gate).astype(BF16)
    put_rows(picks, rows, shid, sd_ref, slice(0, half), oa_ref)
    stores.append(store(oa_ref, oa_hbm, out_sems.at[4]))
    put_rows(picks, rows, shid, sd_ref, slice(half, 2 * half), ob_ref)
    stores.append(store(ob_ref, ob_hbm, out_sems.at[5]))
    for copy in stores:
        copy.wait()


def shared_back(spre, c_parts, sd_ref):
    unit, half = sd_ref.shape[0], c_parts[0].shape[1]
    sgp, sup = spre[:, :unit], spre[:, unit:]
    ssig = jax.nn.sigmoid(sgp)
    sgrad = mm(c_parts[0][...], sd_ref[:, :half], 1, 1) + mm(c_parts[1][...], sd_ref[:, half:], 1, 1)
    sgg = (sgrad * sup * ssig * (1.0 + sgp * (1.0 - ssig))).astype(BF16)
    sug = (sgrad * sgp * ssig).astype(BF16)
    return jnp.concatenate([sgg, sug], axis=1)


def shared_back_kernel(ca_ref, cb_ref, spre_ref, sd_ref, out_ref):
    out_ref[...] = shared_back(spre_ref[...], (ca_ref, cb_ref), sd_ref)


def shared_back_half(parts, spre, sd):
    rows, half = parts[0].shape
    tile = min(512, rows)
    out_shape = jax.ShapeDtypeStruct(spre.shape, BF16)
    args = (*parts, spre, sd)
    return pl.pallas_call(
        shared_back_kernel,
        grid=(rows // tile,),
        in_specs=[spec_rows(tile, half)] * 2 + [spec_rows(tile, spre.shape[1]), spec_whole(sd)],
        out_specs=spec_rows(tile, spre.shape[1]),
        out_shape=out_shape,
        compiler_params=params(),
        cost_estimate=cost(16 * rows * half * sd.shape[0], list(args) + [out_shape]),
        name="shared_back",
    )(*args)


def backward_kernel(
    given, place_ref, gate_ref, ca_ref, cb_ref, wg_hbm, wu_hbm, wd_hbm, sgu_ref, sd_ref,
    gp_ref, up_ref, spre_ref,
    oa_hbm, ob_hbm, cs_hbm, ggp_hbm, ugp_hbm, sgrad_ref, score_ref,
    wg_ref, wu_ref, wd_ref, sems, oa_ref, ob_ref, cs_ref, ggp_ref, ugp_ref, cr_ref, out_sems,
):
    ready = fetch((wg_hbm, wu_hbm, wd_hbm), (wg_ref, wu_ref, wd_ref), sems)
    hits, picks, gate = picks_of(place_ref, gate_ref, cr_ref.shape[0])
    half = ca_ref.shape[1]
    take_rows(picks, ca_ref, cb_ref, cr_ref)
    both = spre_ref[...] if given else shared_back(spre_ref[...], (ca_ref, cb_ref), sd_ref)
    sgrad_ref[...] = both
    cr = cr_ref[...]
    cs_ref[...] = (cr.astype(F32) * gate).astype(BF16)
    stores = [store(cs_ref, cs_hbm, out_sems.at[0])]
    ready(2)
    raw = mm(cr, wd_ref[...], 1, 1)
    gp, up = gp_ref[...], up_ref[...]
    sig = jax.nn.sigmoid(gp)
    silu = gp * sig
    score = jnp.sum(raw * (silu * up).astype(BF16).astype(F32), axis=1, keepdims=True)
    n, tokens = hits[0].shape
    for i, hit in enumerate(hits):
        part = jnp.where(hit, score[i * n : (i + 1) * n, :], 0.0)
        score_ref[0, :, i * tokens : (i + 1) * tokens] = jnp.sum(part, axis=0, keepdims=True)
    grad = raw * gate
    ggp = (grad * up * sig * (1.0 + gp * (1.0 - sig))).astype(BF16)
    ugp = (grad * silu).astype(BF16)
    ggp_ref[...] = ggp
    stores.append(store(ggp_ref, ggp_hbm, out_sems.at[1]))
    ugp_ref[...] = ugp
    stores.append(store(ugp_ref, ugp_hbm, out_sems.at[2]))
    ready(0, 1)
    rows = (mm(ggp, wg_ref[...], 1, 0) + mm(ugp, wu_ref[...], 1, 0)).astype(BF16)
    put_rows(picks, rows, both, sgu_ref, slice(0, half), oa_ref)
    stores.append(store(oa_ref, oa_hbm, out_sems.at[3]))
    put_rows(picks, rows, both, sgu_ref, slice(half, 2 * half), ob_ref)
    stores.append(store(ob_ref, ob_hbm, out_sems.at[4]))
    for copy in stores:
        copy.wait()


def spec_rows(rows, width):
    return pl.BlockSpec((rows, width), lambda i: (i, 0))


def spec_info(tok):
    return pl.BlockSpec((1, 1, tok), lambda i: (i, 0, 0))


def spec_whole(array):
    return pl.BlockSpec(array.shape, lambda i: (0,) * array.ndim, pipeline_mode=pl.Buffered(1))


def cost(flops, arrays):
    return pl.CostEstimate(
        flops=int(flops),
        bytes_accessed=int(sum(np.prod(a.shape) * a.dtype.itemsize for a in arrays)),
        transcendentals=0,
    )


def params():
    return pltpu.CompilerParams(
        dimension_semantics=("arbitrary",), vmem_limit_bytes=VMEM_LIMIT
    )


def half_call(name, kernel, place, gate, parts, weights, more, outs, own, scratch):
    groups, _, tokens = place.shape
    half = parts[1].shape[1]
    ff = weights[0].shape[1]
    hbm = pl.BlockSpec(memory_space=pl.ANY)
    once = dict(pipeline_mode=pl.Buffered(1)) if groups == 1 else {}
    by_group = lambda n: pl.BlockSpec((n.shape[0] // groups, n.shape[1]), lambda i: (i, 0), **once)
    args = (place, gate, *parts, *weights, *more)
    rows = outs[2].shape[0]
    unit = weights[4].shape[0]
    flops = 6 * rows * ff * 2 * half + 6 * groups * tokens * unit * 2 * half
    flops += 4 * rows * tokens * half
    return pl.pallas_call(
        kernel,
        grid=(groups,),
        in_specs=[spec_info(tokens)] * 2
        + [pl.BlockSpec((tokens, half), lambda i: (i, 0), **once)] * 2
        + [hbm] * 3
        + [spec_whole(w) for w in weights[3:]]
        + [by_group(m) for m in more],
        out_specs=[hbm] * own
        + [by_group(o) if len(o.shape) == 2 else spec_info(tokens) for o in outs[own:]],
        out_shape=outs,
        scratch_shapes=[pltpu.VMEM(w.shape[1:], BF16) for w in weights[:3]]
        + [pltpu.SemaphoreType.DMA((3,))]
        + [pltpu.VMEM((o.shape[0] // groups, o.shape[1]), o.dtype) for o in outs[:own]]
        + scratch
        + [pltpu.SemaphoreType.DMA((own,))],
        compiler_params=params(),
        cost_estimate=cost(4 * flops, list(args) + outs),
        name=name,
    )(*args)


def forward_half(place, gate, parts, weights, rows):
    tokens, half = parts[1].shape
    ff, unit = weights[0].shape[1], weights[4].shape[0]
    shape = jax.ShapeDtypeStruct
    outs = [
        shape((tokens, half), BF16),
        shape((tokens, half), BF16),
        shape((rows, 2 * half), BF16),
        shape((rows, ff), F32),
        shape((rows, ff), F32),
        shape((rows, ff), BF16),
        shape((tokens, 2 * unit), F32),
        shape((tokens, unit), BF16),
    ]
    return half_call("forward_half", forward_kernel, place, gate, parts, weights, (), outs, 6, [])


def backward_half(place, gate, parts, weights, ahead, rows, both=None):
    tokens, half = parts[1].shape
    ff, unit = weights[0].shape[1], weights[4].shape[0]
    shape = jax.ShapeDtypeStruct
    outs = [
        shape((tokens, half), BF16),
        shape((tokens, half), BF16),
        shape((rows, 2 * half), BF16),
        shape((rows, ff), BF16),
        shape((rows, ff), BF16),
        shape((tokens, 2 * unit), BF16),
        shape(place.shape, F32),
    ]
    more = (ahead[3], ahead[4], ahead[6] if both is None else both)
    kernel = functools.partial(backward_kernel, both is not None)
    scratch = [pltpu.VMEM((rows // place.shape[0], 2 * half), BF16)]
    return half_call(
        "backward_half", kernel, place, gate, parts, weights, more, outs, 5, scratch
    )


def shared_grads_kernel(
    g0_ref, g1_ref, h0_ref, h1_ref, xa0, xa1, xb0, xb1, ca0, ca1, cb0, cb1,
    ga_ref, gb_ref, da_ref, db_ref, gt_ref, ht_ref,
):
    rows = g0_ref.shape[0]

    @pl.when(pl.program_id(0) == 0)
    def _():
        gt_ref[:, :rows] = g0_ref[...].T
        gt_ref[:, rows:] = g1_ref[...].T
        ht_ref[:, :rows] = h0_ref[...].T
        ht_ref[:, rows:] = h1_ref[...].T

    for out, t_ref, one, two in (
        (ga_ref, gt_ref, xa0, xa1),
        (gb_ref, gt_ref, xb0, xb1),
        (da_ref, ht_ref, ca0, ca1),
        (db_ref, ht_ref, cb0, cb1),
    ):
        part = mm(t_ref[:, :rows], one[...], 1, 0) + mm(t_ref[:, rows:], two[...], 1, 0)
        out[...] = part.astype(BF16)


def shared_grads(grads, hiddens, xs, cs):
    rows, half = xs[2].shape
    unit2, unit = grads[0].shape[1], hiddens[0].shape[1]
    tile = min(256, half)
    col = pl.BlockSpec((rows, tile), lambda i: (0, i))
    args = (*grads, *hiddens, *xs, *cs)
    out_shape = [jax.ShapeDtypeStruct((n, half), BF16) for n in (unit2, unit2, unit, unit)]
    return pl.pallas_call(
        shared_grads_kernel,
        grid=(half // tile,),
        in_specs=[spec_whole(a) for a in (*grads, *hiddens)] + [col] * 8,
        out_specs=[pl.BlockSpec((o.shape[0], tile), lambda i: (0, i)) for o in out_shape],
        out_shape=out_shape,
        scratch_shapes=[pltpu.VMEM((unit2, 2 * rows), BF16), pltpu.VMEM((unit, 2 * rows), BF16)],
        compiler_params=params(),
        cost_estimate=cost(8 * rows * half * (unit2 + unit), list(args) + out_shape),
        name="shared_grads",
    )(*args)


def expert_grads_kernel(
    x0_ref, x1_ref, c0_ref, c1_ref, g0_ref, g1_ref, u0_ref, u1_ref, h0_ref, h1_ref,
    wg_ref, wu_ref, wd_ref, gt_ref, ut_ref, ht_ref,
):
    rows = x0_ref.shape[0]

    @pl.when(pl.program_id(0) == 0)
    def _():
        for t_ref, one, two in (
            (gt_ref, g0_ref, g1_ref), (ut_ref, u0_ref, u1_ref), (ht_ref, h0_ref, h1_ref)
        ):
            t_ref[:, :rows] = one[...].T
            t_ref[:, rows:] = two[...].T

    x = jnp.concatenate([x0_ref[...], x1_ref[...]], axis=0)
    c = jnp.concatenate([c0_ref[...], c1_ref[...]], axis=0)
    wg_ref[0] = mm(gt_ref[...], x, 1, 0).astype(BF16)
    wu_ref[0] = mm(ut_ref[...], x, 1, 0).astype(BF16)
    wd_ref[0] = mm(ht_ref[...], c, 1, 0).astype(BF16)


def expert_grads(xr, cs, ggp, ugp, hid):
    rows, width = xr[0].shape
    ff = ggp[0].shape[1]
    tile = min(256, width)
    col = pl.BlockSpec((rows, tile), lambda i: (0, i))
    args = (*xr, *cs, *ggp, *ugp, *hid)
    out_shape = [jax.ShapeDtypeStruct((1, ff, width), BF16)] * 3
    return pl.pallas_call(
        expert_grads_kernel,
        grid=(width // tile,),
        in_specs=[col] * 4 + [spec_whole(a) for a in (*ggp, *ugp, *hid)],
        out_specs=[pl.BlockSpec((1, ff, tile), lambda i: (0, 0, i))] * 3,
        out_shape=out_shape,
        scratch_shapes=[pltpu.VMEM((ff, 2 * rows), BF16)] * 3,
        compiler_params=params(),
        cost_estimate=cost(24 * rows * width * ff, list(args) + out_shape),
        name="expert_grads",
    )(*args)


def local(tokens, expert_ids, gates, w_gate, w_up, w_down, s_gate, s_up, s_down, cotangent):
    tok, width = tokens.shape
    top = expert_ids.shape[1]
    experts, dp = lax.axis_size("expert"), lax.axis_size("dp")
    me, my_dp = lax.axis_index("expert"), lax.axis_index("dp")
    capacity = min(tok, 5 * tok * top // (4 * experts))
    slots = -(-capacity // 16) * 16
    units = s_gate.shape[1] // experts
    share, half = tok // dp, width // 2
    sizes = split_of(experts, dp)
    shares_at = my_dp ^ jnp.arange(dp, dtype=jnp.int32)
    turns = ((3, 1), (1, 3))
    shape = (1,) + sizes[1:] + (share, half)
    flat = lambda parts: [p.reshape(-1, p.shape[5]) for p in parts]
    full = lambda parts: [p.reshape(shape) for p in parts]

    def mine(rows):
        rows = lax.dynamic_slice_in_dim(rows, my_dp * share, share, 0)
        return [rows[:, i * half : (i + 1) * half].reshape(1, 1, 1, 1, share, half) for i in range(2)]

    halves = lambda rows: [rows[..., i * half : (i + 1) * half] for i in range(2)]
    mine = lambda rows: lax.dynamic_slice_in_dim(rows, my_dp * share, share, 0)[None, None, None, None]
    high = lax.reduce_precision(gates, 8, 7)
    facts = jnp.concatenate([expert_ids.astype(F32), high, gates - high], axis=1).astype(BF16)
    facts = jnp.pad(facts, ((0, 0), (0, FACTS - facts.shape[1])))
    x0 = mine(jnp.concatenate([tokens[:, :half], facts, tokens[:, half:]], axis=1))
    x1 = spread(x0, sizes, 2)
    x1 = (x1[..., : half + FACTS], x1[..., half + FACTS :])
    x2 = [spread(p, sizes, turn[0]) for p, turn in zip(x1, turns)]
    c1 = spread(after(mine(cotangent), x1), sizes, 2, x2)
    x3 = [spread(p, sizes, turn[1]) for p, turn in zip(x2, turns)]
    own_x = flat(x3)
    other_x = [partner(p, sizes, 0, 1) for p in own_x]

    before = jnp.triu(jnp.ones((tok, tok), BF16), 1)
    start = slots * (jnp.arange(experts // 2, dtype=jnp.int32) % GROUP)

    def routing(part):
        known = part[:, half : half + 3 * top].astype(F32).T.reshape(3, top, experts // 2, tok)
        hit = known[0] == me.astype(F32)
        taken = jnp.any(hit, axis=0)
        gate = jnp.sum(jnp.where(hit, known[1] + known[2], 0.0), axis=0)
        place = mm(taken.astype(BF16), before, 1, 0).astype(jnp.int32) + start[:, None]
        place = jnp.where(taken, place, -1)
        return place.reshape(-1, 1, GROUP * tok), gate.reshape(-1, 1, GROUP * tok)

    place, gate = zip(routing(own_x[0]), routing(other_x[0]))

    pad = -units % 128
    first = after(me * units, x1)
    widen = lambda m: jnp.pad(m, ((0, pad), (0, 0)))
    columns = lambda m: widen(lax.dynamic_slice_in_dim(m, first, units, 1).T)
    sgu = jnp.concatenate([columns(s_gate), columns(s_up)], axis=0)
    sd = widen(lax.dynamic_slice_in_dim(s_down, first, units, 0))
    weights = (w_gate.swapaxes(1, 2), w_up.swapaxes(1, 2), w_down, sgu, sd)

    rows = experts // 2 * slots
    c2 = [spread(p, sizes, turn[0]) for p, turn in zip(after(halves(c1), x3), turns)]
    ahead0 = forward_half(after(place[0], c2), gate[0], own_x, weights, rows)
    ahead1 = forward_half(place[1], gate[1], after(other_x, ahead0[0]), weights, rows)
    c3 = [spread(p, sizes, turn[1], ahead1[0]) for p, turn in zip(c2, turns)]
    own_c = flat(c3)
    back0 = backward_half(place[0], gate[0], own_c, weights, ahead0, rows)
    out_came = after([partner(p, sizes, 0, 1) for p in full(ahead1[:2])], back0[0])
    out = [list(t) for t in zip(full(ahead0[:2]), out_came)]
    out = [parts_for(t, sizes, turn[1]) for t, turn in zip(out, turns)]
    other_c = after([partner(p, sizes, 0, 1) for p in own_c], back0[0])

    both1 = shared_back_half(after(other_c, [sent for sent, _ in out]), ahead1[6], sd)
    ga, gb, da, db = shared_grads(
        [back0[5], both1],
        [ahead0[7], ahead1[7]],
        [own_x[0], other_x[0], own_x[1], other_x[1]],
        [own_c[0], other_c[0], own_c[1], other_c[1]],
    )
    out = [fold(*t, sizes, turn[1], ga) for t, turn in zip(out, turns)]
    out = [parts_for(t, sizes, turn[0]) for t, turn in zip(out, turns)]
    unit = units + pad
    both = jnp.concatenate([ga, gb], axis=1)
    grads = jnp.concatenate(
        [both[:units], both[unit : unit + units], jnp.concatenate([da, db], axis=1)[:units]], axis=0
    )
    send = grads.reshape(3 * units, experts, width // experts).transpose(1, 0, 2)
    got = lax.all_to_all(send, "expert", split_axis=0, concat_axis=0, tiled=True)
    back1 = backward_half(
        after(place[1], send, [sent for sent, _ in out]), gate[1], other_c, weights, ahead1, rows, both1
    )

    out = [fold(*t, sizes, turn[0], back1[0]) for t, turn in zip(out, turns)]
    back1_out, got = after((back1[:2], got), [t[-1] for t in out])
    dx_came = [partner(p, sizes, 0, 1) for p in full(after(back1_out, got))]
    out = [jnp.concatenate(p, axis=5) for p in zip(*out)]
    out = parts_for(out, sizes, 2)
    dx = [list(t) for t in zip(full(back0[:2]), after(dx_came, out[0]))]
    dx = [parts_for(t, sizes, turn[1]) for t, turn in zip(dx, turns)]
    dx_sent = [sent for sent, _ in dx]

    index = np.arange(experts).reshape(sizes[2], sizes[1], 2).transpose(2, 1, 0).reshape(-1)
    where = jnp.asarray(np.argsort(index), jnp.int32)[me ^ jnp.arange(experts, dtype=jnp.int32)]
    score = jnp.stack(after([back0[6], back1[6]], dx_sent)).reshape(experts, dp, share)
    score = score[where][:, shares_at].reshape(experts, tok)
    scores = lax.all_to_all(score, "expert", split_axis=0, concat_axis=0, tiled=True).T
    named = expert_ids[:, :, None] == jnp.arange(experts, dtype=jnp.int32)[None, None, :]
    gate_part = jnp.sum(jnp.where(named, scores[:, None, :], 0.0), axis=2)
    gate_grads = gate_part
    for k in range(1, dp):
        gate_grads = gate_grads + partner(gate_part, sizes, 3, k)

    got = after(got, dx_sent)
    grad_sg = got[:, :units].reshape(experts * units, -1).T
    grad_su = got[:, units : 2 * units].reshape(experts * units, -1).T
    grad_sd = got[:, 2 * units :].reshape(experts * units, -1)
    out = fold(*out, sizes, 2, dx_sent)
    dx = [fold(*t, sizes, turn[1], out[1:], grad_sd) for t, turn in zip(dx, turns)]
    dx = [parts_for(t, sizes, turn[0]) for t, turn in zip(dx, turns)]
    dx_sent = [sent for sent, _ in dx]
    moe_out = both_halves(total(after(out, dx_sent)).reshape(share, width), sizes)
    dx = [fold(*t, sizes, turn[0]) for t, turn in zip(dx, turns)]
    dx = [jnp.concatenate(p, axis=5) for p in zip(*dx)]
    dx = parts_for(dx, sizes, 2)
    grad_wg, grad_wu, grad_wd = expert_grads(
        [ahead0[2], ahead1[2]],
        after([back0[2], back1[2]], dx[0]),
        [back0[3], back1[3]],
        [back0[4], back1[4]],
        [ahead0[5], ahead1[5]],
    )
    token_grads = both_halves(total(fold(*dx, sizes, 2, grad_wg)).reshape(share, width), sizes)
    grad_wg, grad_wu = grad_wg.swapaxes(1, 2), grad_wu.swapaxes(1, 2)
    return (moe_out, token_grads, gate_grads, grad_wg, grad_wu, grad_wd, grad_sg, grad_su, grad_sd)


def solution(mesh):
    row = P("expert", None)
    cols = P("expert", None, "dp")
    return jax.shard_map(
        local,
        mesh=mesh,
        in_specs=(
            row, row, row, cols, cols, P("expert", "dp", None),
            P(None, "dp"), P(None, "dp"), P("dp", None), row,
        ),
        out_specs=(
            row, row, row, cols, cols, P("expert", "dp", None),
            P("expert", "dp"), P("expert", "dp"), P("dp", "expert"),
        ),
        check_vma=False,
    )
```

```python
import functools

import jax
import jax.numpy as jnp
import numpy as np
from jax import lax
from jax.experimental import pallas as pl
from jax.experimental.pallas import tpu as pltpu
from jax.sharding import PartitionSpec as P

F32 = jnp.float32
BF16 = jnp.bfloat16
GROUP = 8
SUB = 4
FACTS = 128
VMEM_LIMIT = 56 * 1024 * 1024


def mm(left, right, left_dim, right_dim):
    return lax.dot_general(
        left, right, (((left_dim,), (right_dim,)), ((), ())), preferred_element_type=F32
    )


def split_of(experts, dp):
    bits = experts.bit_length() - 1
    middle = (bits - 1) // 2
    return (2, 1 << middle, 1 << (bits - 1 - middle), dp)


def partner(array, sizes, dim, k):
    if dim == 3:
        axis, mask = "dp", k
    else:
        axis, mask = "expert", k * (1, 2, 2 * sizes[1])[dim]
    return lax.ppermute(array, axis, [(i, i ^ mask) for i in range(lax.axis_size(axis))])


def after(arrays, *earlier):
    return lax.optimization_barrier((arrays, earlier))[0]


def spread(out, sizes, dim, *earlier):
    came = [partner(out, sizes, dim, k) for k in range(1, sizes[dim])]
    return jnp.concatenate([out] + after(came, *earlier), axis=dim)


def total(terms):
    out = terms[0].astype(F32)
    for term in terms[1:]:
        out = out + term.astype(F32)
    return out.astype(BF16)


def parts_for(terms, sizes, dim):
    cut = lambda k: total([lax.slice_in_dim(t, k, k + 1, axis=dim) for t in terms])
    return [cut(k) for k in range(1, sizes[dim])], [cut(0)]


def fold(sent, stays, sizes, dim, *earlier):
    return stays + after([partner(part, sizes, dim, k + 1) for k, part in enumerate(sent)], *earlier)


def both_halves(rows, sizes):
    out = [rows] + [partner(rows, sizes, 3, k) for k in range(1, sizes[3])]
    out = jnp.stack(out)
    order = jnp.arange(sizes[3]) ^ lax.axis_index("dp")
    return out[order].reshape(-1, rows.shape[1])


def picks_of(place_ref, gate_ref, rows):
    parts = GROUP // SUB
    tokens = place_ref.shape[2] // parts
    hits, gates = [], []
    for i in range(parts):
        cut = slice(i * tokens, (i + 1) * tokens)
        place = place_ref[0, :, cut] - i * (rows // parts)
        hit = lax.broadcasted_iota(jnp.int32, (rows // parts, tokens), 0) == place
        hits.append(hit)
        gates.append(jnp.sum(jnp.where(hit, gate_ref[0, :, cut], 0.0), axis=1, keepdims=True))
    return hits, [hit.astype(BF16) for hit in hits], jnp.concatenate(gates, axis=0)


def take_rows(picks, a_ref, b_ref, rows_ref):
    half = a_ref.shape[1]
    rows, tokens = 2 * picks[0].shape[0] // SUB, 2 * picks[0].shape[1] // SUB
    for i in range(GROUP // 2):
        pick, j = picks[2 * i // SUB], i % (SUB // 2)
        pick = pick[j * rows : (j + 1) * rows, j * tokens : (j + 1) * tokens]
        r, t = slice(i * rows, (i + 1) * rows), slice(i * tokens, (i + 1) * tokens)
        rows_ref[r, :half] = mm(pick, a_ref[t, :], 1, 0).astype(BF16)
        rows_ref[r, half:] = mm(pick, b_ref[t, :], 1, 0).astype(BF16)


def put_rows(picks, rows, units, weight_ref, cut, out_ref):
    n, tokens = picks[0].shape
    for i, pick in enumerate(picks):
        t = slice(i * tokens, (i + 1) * tokens)
        left = jnp.concatenate([pick.T, units[t, :]], axis=1)
        right = jnp.concatenate([rows[i * n : (i + 1) * n, cut], weight_ref[:, cut]], axis=0)
        out_ref[t, :] = mm(left, right, 1, 0).astype(BF16)


def store(source, target, sem):
    n = source.shape[0]
    at = pl.multiple_of(pl.program_id(0) * n, n)
    copy = pltpu.make_async_copy(source, target.at[pl.ds(at, n)], sem)
    copy.start()
    return copy


def fetch(sources, targets, sems):
    copies = [
        pltpu.make_async_copy(src.at[0], dst, sems.at[i])
        for i, (src, dst) in enumerate(zip(sources, targets))
    ]

    @pl.when(pl.program_id(0) == 0)
    def _():
        for copy in copies:
            copy.start()

    def ready(*which):
        @pl.when(pl.program_id(0) == 0)
        def _():
            for i in which:
                copies[i].wait()

    return ready


def forward_kernel(
    place_ref, gate_ref, xa_ref, xb_ref, wg_hbm, wu_hbm, wd_hbm, sgu_ref, sd_ref,
    oa_hbm, ob_hbm, xr_hbm, gp_hbm, up_hbm, hid_hbm, spre_ref, shid_ref,
    wg_ref, wu_ref, wd_ref, sems, oa_ref, ob_ref, xr_ref, gp_ref, up_ref, hid_ref, out_sems,
):
    ready = fetch((wg_hbm, wu_hbm, wd_hbm), (wg_ref, wu_ref, wd_ref), sems)
    hits, picks, gate = picks_of(place_ref, gate_ref, xr_ref.shape[0])
    half = xa_ref.shape[1]
    unit = sd_ref.shape[0]
    take_rows(picks, xa_ref, xb_ref, xr_ref)
    stores = [store(xr_ref, xr_hbm, out_sems.at[0])]
    spre = mm(xa_ref[...], sgu_ref[:, :half], 1, 1) + mm(xb_ref[...], sgu_ref[:, half:], 1, 1)
    spre_ref[...] = spre
    sgp, sup = spre[:, :unit], spre[:, unit:]
    shid = (sgp * jax.nn.sigmoid(sgp) * sup).astype(BF16)
    shid_ref[...] = shid
    xr = xr_ref[...]
    ready(0, 1)
    gp = mm(xr, wg_ref[...], 1, 1)
    gp_ref[...] = gp
    stores.append(store(gp_ref, gp_hbm, out_sems.at[1]))
    up = mm(xr, wu_ref[...], 1, 1)
    up_ref[...] = up
    stores.append(store(up_ref, up_hbm, out_sems.at[2]))
    hid = (gp * jax.nn.sigmoid(gp) * up).astype(BF16)
    hid_ref[...] = hid
    stores.append(store(hid_ref, hid_hbm, out_sems.at[3]))
    ready(2)
    rows = (mm(hid, wd_ref[...], 1, 0) * gate).astype(BF16)
    put_rows(picks, rows, shid, sd_ref, slice(0, half), oa_ref)
    stores.append(store(oa_ref, oa_hbm, out_sems.at[4]))
    put_rows(picks, rows, shid, sd_ref, slice(half, 2 * half), ob_ref)
    stores.append(store(ob_ref, ob_hbm, out_sems.at[5]))
    for copy in stores:
        copy.wait()


def shared_back(spre_ref, ca_ref, cb_ref, sd_ref):
    unit, half = sd_ref.shape[0], ca_ref.shape[1]
    sgp, sup = spre_ref[:, :unit], spre_ref[:, unit:]
    ssig = jax.nn.sigmoid(sgp)
    sgrad = mm(ca_ref[...], sd_ref[:, :half], 1, 1) + mm(cb_ref[...], sd_ref[:, half:], 1, 1)
    sgg = (sgrad * sup * ssig * (1.0 + sgp * (1.0 - ssig))).astype(BF16)
    sug = (sgrad * sgp * ssig).astype(BF16)
    return jnp.concatenate([sgg, sug], axis=1)


def shared_back_kernel(ca_ref, cb_ref, spre_ref, sd_ref, out_ref):
    out_ref[...] = shared_back(spre_ref, ca_ref, cb_ref, sd_ref)


def shared_back_half(parts, spre, sd):
    rows, half = parts[0].shape
    tile = min(512, rows)
    out_shape = jax.ShapeDtypeStruct(spre.shape, BF16)
    args = (*parts, spre, sd)
    return pl.pallas_call(
        shared_back_kernel,
        grid=(rows // tile,),
        in_specs=[spec_rows(tile, half)] * 2 + [spec_rows(tile, spre.shape[1]), spec_whole(sd)],
        out_specs=spec_rows(tile, spre.shape[1]),
        out_shape=out_shape,
        compiler_params=params(),
        cost_estimate=cost(16 * rows * half * sd.shape[0], list(args) + [out_shape]),
        name="shared_back",
    )(*args)


def backward_kernel(
    given, place_ref, gate_ref, ca_ref, cb_ref, wg_hbm, wu_hbm, wd_hbm, sgu_ref, sd_ref,
    gp_ref, up_ref, spre_ref,
    oa_hbm, ob_hbm, cs_hbm, ggp_hbm, ugp_hbm, sgrad_ref, score_ref,
    wg_ref, wu_ref, wd_ref, sems, oa_ref, ob_ref, cs_ref, ggp_ref, ugp_ref, cr_ref, out_sems,
):
    ready = fetch((wg_hbm, wu_hbm, wd_hbm), (wg_ref, wu_ref, wd_ref), sems)
    hits, picks, gate = picks_of(place_ref, gate_ref, cr_ref.shape[0])
    half = ca_ref.shape[1]
    take_rows(picks, ca_ref, cb_ref, cr_ref)
    both = spre_ref[...] if given else shared_back(spre_ref, ca_ref, cb_ref, sd_ref)
    sgrad_ref[...] = both
    cr = cr_ref[...]
    cs_ref[...] = (cr.astype(F32) * gate).astype(BF16)
    stores = [store(cs_ref, cs_hbm, out_sems.at[0])]
    ready(2)
    raw = mm(cr, wd_ref[...], 1, 1)
    gp, up = gp_ref[...], up_ref[...]
    sig = jax.nn.sigmoid(gp)
    silu = gp * sig
    score = jnp.sum(raw * (silu * up).astype(BF16).astype(F32), axis=1, keepdims=True)
    n, tokens = hits[0].shape
    for i, hit in enumerate(hits):
        part = jnp.where(hit, score[i * n : (i + 1) * n, :], 0.0)
        score_ref[0, :, i * tokens : (i + 1) * tokens] = jnp.sum(part, axis=0, keepdims=True)
    grad = raw * gate
    ggp = (grad * up * sig * (1.0 + gp * (1.0 - sig))).astype(BF16)
    ugp = (grad * silu).astype(BF16)
    ggp_ref[...] = ggp
    stores.append(store(ggp_ref, ggp_hbm, out_sems.at[1]))
    ugp_ref[...] = ugp
    stores.append(store(ugp_ref, ugp_hbm, out_sems.at[2]))
    ready(0, 1)
    rows = (mm(ggp, wg_ref[...], 1, 0) + mm(ugp, wu_ref[...], 1, 0)).astype(BF16)
    put_rows(picks, rows, both, sgu_ref, slice(0, half), oa_ref)
    stores.append(store(oa_ref, oa_hbm, out_sems.at[3]))
    put_rows(picks, rows, both, sgu_ref, slice(half, 2 * half), ob_ref)
    stores.append(store(ob_ref, ob_hbm, out_sems.at[4]))
    for copy in stores:
        copy.wait()


def spec_rows(rows, width):
    return pl.BlockSpec((rows, width), lambda i: (i, 0))


def spec_info(tok):
    return pl.BlockSpec((1, 1, tok), lambda i: (i, 0, 0))


def spec_whole(array):
    return pl.BlockSpec(array.shape, lambda i: (0,) * array.ndim, pipeline_mode=pl.Buffered(1))


def cost(flops, arrays):
    return pl.CostEstimate(
        flops=int(flops),
        bytes_accessed=int(sum(np.prod(a.shape) * a.dtype.itemsize for a in arrays)),
        transcendentals=0,
    )


def params():
    return pltpu.CompilerParams(
        dimension_semantics=("arbitrary",), vmem_limit_bytes=VMEM_LIMIT
    )


def half_call(name, kernel, place, gate, parts, weights, more, outs, own, scratch):
    groups, _, tokens = place.shape
    half = parts[1].shape[1]
    ff = weights[0].shape[1]
    hbm = pl.BlockSpec(memory_space=pl.ANY)
    once = dict(pipeline_mode=pl.Buffered(1)) if groups == 1 else {}
    by_group = lambda n: pl.BlockSpec((n.shape[0] // groups, n.shape[1]), lambda i: (i, 0), **once)
    args = (place, gate, *parts, *weights, *more)
    rows = outs[2].shape[0]
    unit = weights[4].shape[0]
    flops = 6 * rows * ff * 2 * half + 6 * groups * tokens * unit * 2 * half
    flops += 4 * rows * tokens * half
    return pl.pallas_call(
        kernel,
        grid=(groups,),
        in_specs=[spec_info(tokens)] * 2
        + [pl.BlockSpec((tokens, half), lambda i: (i, 0), **once)] * 2
        + [hbm] * 3
        + [spec_whole(w) for w in weights[3:]]
        + [by_group(m) for m in more],
        out_specs=[hbm] * own
        + [by_group(o) if len(o.shape) == 2 else spec_info(tokens) for o in outs[own:]],
        out_shape=outs,
        scratch_shapes=[pltpu.VMEM(w.shape[1:], BF16) for w in weights[:3]]
        + [pltpu.SemaphoreType.DMA((3,))]
        + [pltpu.VMEM((o.shape[0] // groups, o.shape[1]), o.dtype) for o in outs[:own]]
        + scratch
        + [pltpu.SemaphoreType.DMA((own,))],
        compiler_params=params(),
        cost_estimate=cost(4 * flops, list(args) + outs),
        name=name,
    )(*args)


def forward_half(place, gate, parts, weights, rows):
    tokens, half = parts[1].shape
    ff, unit = weights[0].shape[1], weights[4].shape[0]
    shape = jax.ShapeDtypeStruct
    outs = [
        shape((tokens, half), BF16),
        shape((tokens, half), BF16),
        shape((rows, 2 * half), BF16),
        shape((rows, ff), F32),
        shape((rows, ff), F32),
        shape((rows, ff), BF16),
        shape((tokens, 2 * unit), F32),
        shape((tokens, unit), BF16),
    ]
    return half_call("forward_half", forward_kernel, place, gate, parts, weights, (), outs, 6, [])


def backward_half(place, gate, parts, weights, ahead, rows, both=None):
    tokens, half = parts[1].shape
    ff, unit = weights[0].shape[1], weights[4].shape[0]
    shape = jax.ShapeDtypeStruct
    outs = [
        shape((tokens, half), BF16),
        shape((tokens, half), BF16),
        shape((rows, 2 * half), BF16),
        shape((rows, ff), BF16),
        shape((rows, ff), BF16),
        shape((tokens, 2 * unit), BF16),
        shape(place.shape, F32),
    ]
    more = (ahead[3], ahead[4], ahead[6] if both is None else both)
    kernel = functools.partial(backward_kernel, both is not None)
    scratch = [pltpu.VMEM((rows // place.shape[0], 2 * half), BF16)]
    return half_call(
        "backward_half", kernel, place, gate, parts, weights, more, outs, 5, scratch
    )


def shared_grads_kernel(
    g0_ref, g1_ref, h0_ref, h1_ref, xa0, xa1, xb0, xb1, ca0, ca1, cb0, cb1,
    ga_ref, gb_ref, da_ref, db_ref, gt_ref, ht_ref,
):
    rows = g0_ref.shape[0]

    @pl.when(pl.program_id(0) == 0)
    def _():
        gt_ref[:, :rows] = g0_ref[...].T
        gt_ref[:, rows:] = g1_ref[...].T
        ht_ref[:, :rows] = h0_ref[...].T
        ht_ref[:, rows:] = h1_ref[...].T

    for out, t_ref, one, two in (
        (ga_ref, gt_ref, xa0, xa1),
        (gb_ref, gt_ref, xb0, xb1),
        (da_ref, ht_ref, ca0, ca1),
        (db_ref, ht_ref, cb0, cb1),
    ):
        part = mm(t_ref[:, :rows], one[...], 1, 0) + mm(t_ref[:, rows:], two[...], 1, 0)
        out[...] = part.astype(BF16)


def shared_grads(grads, hiddens, xs, cs):
    rows, half = xs[2].shape
    unit2, unit = grads[0].shape[1], hiddens[0].shape[1]
    tile = min(256, half)
    col = pl.BlockSpec((rows, tile), lambda i: (0, i))
    args = (*grads, *hiddens, *xs, *cs)
    out_shape = [jax.ShapeDtypeStruct((n, half), BF16) for n in (unit2, unit2, unit, unit)]
    return pl.pallas_call(
        shared_grads_kernel,
        grid=(half // tile,),
        in_specs=[spec_whole(a) for a in (*grads, *hiddens)] + [col] * 8,
        out_specs=[pl.BlockSpec((o.shape[0], tile), lambda i: (0, i)) for o in out_shape],
        out_shape=out_shape,
        scratch_shapes=[pltpu.VMEM((unit2, 2 * rows), BF16), pltpu.VMEM((unit, 2 * rows), BF16)],
        compiler_params=params(),
        cost_estimate=cost(8 * rows * half * (unit2 + unit), list(args) + out_shape),
        name="shared_grads",
    )(*args)


def expert_grads_kernel(
    x0_ref, x1_ref, c0_ref, c1_ref, g0_ref, g1_ref, u0_ref, u1_ref, h0_ref, h1_ref,
    wg_ref, wu_ref, wd_ref, gt_ref, ut_ref, ht_ref,
):
    rows = x0_ref.shape[0]

    @pl.when(pl.program_id(0) == 0)
    def _():
        for t_ref, one, two in (
            (gt_ref, g0_ref, g1_ref), (ut_ref, u0_ref, u1_ref), (ht_ref, h0_ref, h1_ref)
        ):
            t_ref[:, :rows] = one[...].T
            t_ref[:, rows:] = two[...].T

    x = jnp.concatenate([x0_ref[...], x1_ref[...]], axis=0)
    c = jnp.concatenate([c0_ref[...], c1_ref[...]], axis=0)
    wg_ref[0] = mm(gt_ref[...], x, 1, 0).astype(BF16)
    wu_ref[0] = mm(ut_ref[...], x, 1, 0).astype(BF16)
    wd_ref[0] = mm(ht_ref[...], c, 1, 0).astype(BF16)


def expert_grads(xr, cs, ggp, ugp, hid):
    rows, width = xr[0].shape
    ff = ggp[0].shape[1]
    tile = min(256, width)
    col = pl.BlockSpec((rows, tile), lambda i: (0, i))
    args = (*xr, *cs, *ggp, *ugp, *hid)
    out_shape = [jax.ShapeDtypeStruct((1, ff, width), BF16)] * 3
    return pl.pallas_call(
        expert_grads_kernel,
        grid=(width // tile,),
        in_specs=[col] * 4 + [spec_whole(a) for a in (*ggp, *ugp, *hid)],
        out_specs=[pl.BlockSpec((1, ff, tile), lambda i: (0, 0, i))] * 3,
        out_shape=out_shape,
        scratch_shapes=[pltpu.VMEM((ff, 2 * rows), BF16)] * 3,
        compiler_params=params(),
        cost_estimate=cost(24 * rows * width * ff, list(args) + out_shape),
        name="expert_grads",
    )(*args)


def local(tokens, expert_ids, gates, w_gate, w_up, w_down, s_gate, s_up, s_down, cotangent):
    tok, width = tokens.shape
    top = expert_ids.shape[1]
    experts, dp = lax.axis_size("expert"), lax.axis_size("dp")
    me, my_dp = lax.axis_index("expert"), lax.axis_index("dp")
    capacity = min(tok, 5 * tok * top // (4 * experts))
    slots = -(-capacity // 16) * 16
    units = s_gate.shape[1] // experts
    share, half = tok // dp, width // 2
    sizes = split_of(experts, dp)
    shares_at = my_dp ^ jnp.arange(dp, dtype=jnp.int32)
    turns = ((3, 1), (1, 3))
    shape = (1,) + sizes[1:] + (share, half)
    flat = lambda parts: [p.reshape(-1, p.shape[5]) for p in parts]
    full = lambda parts: [p.reshape(shape) for p in parts]

    def mine(rows):
        rows = lax.dynamic_slice_in_dim(rows, my_dp * share, share, 0)
        return [rows[:, i * half : (i + 1) * half].reshape(1, 1, 1, 1, share, half) for i in range(2)]

    halves = lambda rows: [rows[..., i * half : (i + 1) * half] for i in range(2)]
    mine = lambda rows: lax.dynamic_slice_in_dim(rows, my_dp * share, share, 0)[None, None, None, None]
    high = lax.reduce_precision(gates, 8, 7)
    facts = jnp.concatenate([expert_ids.astype(F32), high, gates - high], axis=1).astype(BF16)
    facts = jnp.pad(facts, ((0, 0), (0, FACTS - facts.shape[1])))
    x0 = mine(jnp.concatenate([tokens[:, :half], facts, tokens[:, half:]], axis=1))
    x1 = spread(x0, sizes, 2)
    x1 = (x1[..., : half + FACTS], x1[..., half + FACTS :])
    x2 = [spread(p, sizes, turn[0]) for p, turn in zip(x1, turns)]
    c1 = spread(after(mine(cotangent), x1), sizes, 2, x2)
    x3 = [spread(p, sizes, turn[1]) for p, turn in zip(x2, turns)]
    own_x = flat(x3)
    other_x = [partner(p, sizes, 0, 1) for p in own_x]

    before = jnp.triu(jnp.ones((tok, tok), BF16), 1)
    start = slots * (jnp.arange(experts // 2, dtype=jnp.int32) % GROUP)

    def routing(part):
        known = part[:, half : half + 3 * top].astype(F32).T.reshape(3, top, experts // 2, tok)
        hit = known[0] == me.astype(F32)
        taken = jnp.any(hit, axis=0)
        gate = jnp.sum(jnp.where(hit, known[1] + known[2], 0.0), axis=0)
        place = mm(taken.astype(BF16), before, 1, 0).astype(jnp.int32) + start[:, None]
        place = jnp.where(taken, place, -1)
        return place.reshape(-1, 1, GROUP * tok), gate.reshape(-1, 1, GROUP * tok)

    place, gate = zip(routing(own_x[0]), routing(other_x[0]))

    pad = -units % 128
    first = after(me * units, x1)
    widen = lambda m: jnp.pad(m, ((0, pad), (0, 0)))
    columns = lambda m: widen(lax.dynamic_slice_in_dim(m, first, units, 1).T)
    sgu = jnp.concatenate([columns(s_gate), columns(s_up)], axis=0)
    sd = widen(lax.dynamic_slice_in_dim(s_down, first, units, 0))
    weights = (w_gate.swapaxes(1, 2), w_up.swapaxes(1, 2), w_down, sgu, sd)

    rows = experts // 2 * slots
    ahead0 = forward_half(place[0], gate[0], own_x, weights, rows)
    c2 = [spread(p, sizes, turn[0], ahead0[0]) for p, turn in zip(after(halves(c1), x3), turns)]
    ahead1 = forward_half(after(place[1], c2), gate[1], after(other_x, ahead0[0]), weights, rows)
    c3 = [spread(p, sizes, turn[1], ahead1[0]) for p, turn in zip(c2, turns)]
    own_c = flat(c3)
    back0 = backward_half(place[0], gate[0], own_c, weights, ahead0, rows)
    out_came = after([partner(p, sizes, 0, 1) for p in full(ahead1[:2])], back0[0])
    out = [list(t) for t in zip(full(ahead0[:2]), out_came)]
    out = [parts_for(t, sizes, turn[1]) for t, turn in zip(out, turns)]
    other_c = after([partner(p, sizes, 0, 1) for p in own_c], back0[0])

    both1 = shared_back_half(after(other_c, [sent for sent, _ in out]), ahead1[6], sd)
    ga, gb, da, db = shared_grads(
        [back0[5], both1],
        [ahead0[7], ahead1[7]],
        [own_x[0], other_x[0], own_x[1], other_x[1]],
        [own_c[0], other_c[0], own_c[1], other_c[1]],
    )
    out = [fold(*t, sizes, turn[1], ga) for t, turn in zip(out, turns)]
    out = [parts_for(t, sizes, turn[0]) for t, turn in zip(out, turns)]
    unit = units + pad
    both = jnp.concatenate([ga, gb], axis=1)
    grads = jnp.concatenate(
        [both[:units], both[unit : unit + units], jnp.concatenate([da, db], axis=1)[:units]], axis=0
    )
    send = grads.reshape(3 * units, experts, width // experts).transpose(1, 0, 2)
    got = lax.all_to_all(send, "expert", split_axis=0, concat_axis=0, tiled=True)
    back1 = backward_half(
        after(place[1], send, [sent for sent, _ in out]), gate[1], other_c, weights, ahead1, rows, both1
    )

    out = [fold(*t, sizes, turn[0], back1[0]) for t, turn in zip(out, turns)]
    back1_out, got = after((back1[:2], got), [t[-1] for t in out])
    dx_came = [partner(p, sizes, 0, 1) for p in full(after(back1_out, got))]
    out = [jnp.concatenate(p, axis=5) for p in zip(*out)]
    out = parts_for(out, sizes, 2)
    dx = [list(t) for t in zip(full(back0[:2]), after(dx_came, out[0]))]
    dx = [parts_for(t, sizes, turn[1]) for t, turn in zip(dx, turns)]
    dx_sent = [sent for sent, _ in dx]

    index = np.arange(experts).reshape(sizes[2], sizes[1], 2).transpose(2, 1, 0).reshape(-1)
    where = jnp.asarray(np.argsort(index), jnp.int32)[me ^ jnp.arange(experts, dtype=jnp.int32)]
    score = jnp.stack(after([back0[6], back1[6]], dx_sent)).reshape(experts, dp, share)
    score = score[where][:, shares_at].reshape(experts, tok)
    scores = lax.all_to_all(score, "expert", split_axis=0, concat_axis=0, tiled=True).T
    named = expert_ids[:, :, None] == jnp.arange(experts, dtype=jnp.int32)[None, None, :]
    gate_part = jnp.sum(jnp.where(named, scores[:, None, :], 0.0), axis=2)
    gate_grads = gate_part
    for k in range(1, dp):
        gate_grads = gate_grads + partner(gate_part, sizes, 3, k)

    got = after(got, dx_sent)
    grad_sg = got[:, :units].reshape(experts * units, -1).T
    grad_su = got[:, units : 2 * units].reshape(experts * units, -1).T
    grad_sd = got[:, 2 * units :].reshape(experts * units, -1)
    out = fold(*out, sizes, 2, dx_sent)
    dx = [fold(*t, sizes, turn[1], out[1:], grad_sd) for t, turn in zip(dx, turns)]
    dx = [parts_for(t, sizes, turn[0]) for t, turn in zip(dx, turns)]
    dx_sent = [sent for sent, _ in dx]
    moe_out = both_halves(total(after(out, dx_sent)).reshape(share, width), sizes)
    dx = [fold(*t, sizes, turn[0]) for t, turn in zip(dx, turns)]
    dx = [jnp.concatenate(p, axis=5) for p in zip(*dx)]
    dx = parts_for(dx, sizes, 2)
    grad_wg, grad_wu, grad_wd = expert_grads(
        [ahead0[2], ahead1[2]],
        after([back0[2], back1[2]], dx[0]),
        [back0[3], back1[3]],
        [back0[4], back1[4]],
        [ahead0[5], ahead1[5]],
    )
    token_grads = both_halves(total(fold(*dx, sizes, 2, grad_wg)).reshape(share, width), sizes)
    grad_wg, grad_wu = grad_wg.swapaxes(1, 2), grad_wu.swapaxes(1, 2)
    return (moe_out, token_grads, gate_grads, grad_wg, grad_wu, grad_wd, grad_sg, grad_su, grad_sd)


def solution(mesh):
    row = P("expert", None)
    cols = P("expert", None, "dp")
    return jax.shard_map(
        local,
        mesh=mesh,
        in_specs=(
            row, row, row, cols, cols, P("expert", "dp", None),
            P(None, "dp"), P(None, "dp"), P("dp", None), row,
        ),
        out_specs=(
            row, row, row, cols, cols, P("expert", "dp", None),
            P("expert", "dp"), P("expert", "dp"), P("dp", "expert"),
        ),
        check_vma=False,
    )
```

```python
import functools

import jax
import jax.numpy as jnp
import numpy as np
from jax import lax
from jax.experimental import pallas as pl
from jax.experimental.pallas import tpu as pltpu
from jax.sharding import PartitionSpec as P

F32 = jnp.float32
BF16 = jnp.bfloat16
GROUP = 8
SUB = 4
FACTS = 128
VMEM_LIMIT = 56 * 1024 * 1024


def mm(left, right, left_dim, right_dim):
    return lax.dot_general(
        left, right, (((left_dim,), (right_dim,)), ((), ())), preferred_element_type=F32
    )


def split_of(experts, dp):
    bits = experts.bit_length() - 1
    middle = (bits - 1) // 2
    return (2, 1 << middle, 1 << (bits - 1 - middle), dp)


def partner(array, sizes, dim, k):
    if dim == 3:
        axis, mask = "dp", k
    else:
        axis, mask = "expert", k * (1, 2, 2 * sizes[1])[dim]
    return lax.ppermute(array, axis, [(i, i ^ mask) for i in range(lax.axis_size(axis))])


def after(arrays, *earlier):
    return lax.optimization_barrier((arrays, earlier))[0]


def spread(out, sizes, dim, *earlier):
    came = [partner(out, sizes, dim, k) for k in range(1, sizes[dim])]
    return jnp.concatenate([out] + after(came, *earlier), axis=dim)


def total(terms):
    out = terms[0].astype(F32)
    for term in terms[1:]:
        out = out + term.astype(F32)
    return out.astype(BF16)


def parts_for(terms, sizes, dim):
    cut = lambda k: total([lax.slice_in_dim(t, k, k + 1, axis=dim) for t in terms])
    return [cut(k) for k in range(1, sizes[dim])], [cut(0)]


def fold(sent, stays, sizes, dim, *earlier):
    return stays + after([partner(part, sizes, dim, k + 1) for k, part in enumerate(sent)], *earlier)


def both_halves(rows, sizes):
    out = [rows] + [partner(rows, sizes, 3, k) for k in range(1, sizes[3])]
    out = jnp.stack(out)
    order = jnp.arange(sizes[3]) ^ lax.axis_index("dp")
    return out[order].reshape(-1, rows.shape[1])


def picks_of(place_ref, gate_ref, rows):
    parts = GROUP // SUB
    tokens = place_ref.shape[2] // parts
    hits, gates = [], []
    for i in range(parts):
        cut = slice(i * tokens, (i + 1) * tokens)
        place = place_ref[0, :, cut] - i * (rows // parts)
        hit = lax.broadcasted_iota(jnp.int32, (rows // parts, tokens), 0) == place
        hits.append(hit)
        gates.append(jnp.sum(jnp.where(hit, gate_ref[0, :, cut], 0.0), axis=1, keepdims=True))
    return hits, [hit.astype(BF16) for hit in hits], jnp.concatenate(gates, axis=0)


def take_rows(picks, a_ref, b_ref, rows_ref):
    half = a_ref.shape[1]
    rows, tokens = 2 * picks[0].shape[0] // SUB, 2 * picks[0].shape[1] // SUB
    for i in range(GROUP // 2):
        pick, j = picks[2 * i // SUB], i % (SUB // 2)
        pick = pick[j * rows : (j + 1) * rows, j * tokens : (j + 1) * tokens]
        r, t = slice(i * rows, (i + 1) * rows), slice(i * tokens, (i + 1) * tokens)
        rows_ref[r, :half] = mm(pick, a_ref[t, :], 1, 0).astype(BF16)
        rows_ref[r, half:] = mm(pick, b_ref[t, :], 1, 0).astype(BF16)


def put_rows(picks, rows, units, weight_ref, cut, out_ref):
    n, tokens = picks[0].shape
    for i, pick in enumerate(picks):
        t = slice(i * tokens, (i + 1) * tokens)
        left = jnp.concatenate([pick.T, units[t, :]], axis=1)
        right = jnp.concatenate([rows[i * n : (i + 1) * n, cut], weight_ref[:, cut]], axis=0)
        out_ref[t, :] = mm(left, right, 1, 0).astype(BF16)


def store(source, target, sem):
    n = source.shape[0]
    at = pl.multiple_of(pl.program_id(0) * n, n)
    copy = pltpu.make_async_copy(source, target.at[pl.ds(at, n)], sem)
    copy.start()
    return copy


def fetch(sources, targets, sems):
    copies = [
        pltpu.make_async_copy(src.at[0], dst, sems.at[i])
        for i, (src, dst) in enumerate(zip(sources, targets))
    ]

    @pl.when(pl.program_id(0) == 0)
    def _():
        for copy in copies:
            copy.start()

    def ready(*which):
        @pl.when(pl.program_id(0) == 0)
        def _():
            for i in which:
                copies[i].wait()

    return ready


def forward_kernel(
    place_ref, gate_ref, xa_ref, xb_ref, wg_hbm, wu_hbm, wd_hbm, sgu_ref, sd_ref,
    oa_hbm, ob_hbm, xr_hbm, gp_hbm, up_hbm, hid_hbm, spre_ref, shid_ref,
    wg_ref, wu_ref, wd_ref, sems, oa_ref, ob_ref, xr_ref, gp_ref, up_ref, hid_ref, out_sems,
):
    ready = fetch((wg_hbm, wu_hbm, wd_hbm), (wg_ref, wu_ref, wd_ref), sems)
    hits, picks, gate = picks_of(place_ref, gate_ref, xr_ref.shape[0])
    half = xa_ref.shape[1]
    unit = sd_ref.shape[0]
    take_rows(picks, xa_ref, xb_ref, xr_ref)
    stores = [store(xr_ref, xr_hbm, out_sems.at[0])]
    spre = mm(xa_ref[...], sgu_ref[:, :half], 1, 1) + mm(xb_ref[...], sgu_ref[:, half:], 1, 1)
    spre_ref[...] = spre
    sgp, sup = spre[:, :unit], spre[:, unit:]
    shid = (sgp * jax.nn.sigmoid(sgp) * sup).astype(BF16)
    shid_ref[...] = shid
    xr = xr_ref[...]
    ready(0, 1)
    gp = mm(xr, wg_ref[...], 1, 1)
    gp_ref[...] = gp
    stores.append(store(gp_ref, gp_hbm, out_sems.at[1]))
    up = mm(xr, wu_ref[...], 1, 1)
    up_ref[...] = up
    stores.append(store(up_ref, up_hbm, out_sems.at[2]))
    hid = (gp * jax.nn.sigmoid(gp) * up).astype(BF16)
    hid_ref[...] = hid
    stores.append(store(hid_ref, hid_hbm, out_sems.at[3]))
    ready(2)
    rows = (mm(hid, wd_ref[...], 1, 0) * gate).astype(BF16)
    put_rows(picks, rows, shid, sd_ref, slice(0, half), oa_ref)
    stores.append(store(oa_ref, oa_hbm, out_sems.at[4]))
    put_rows(picks, rows, shid, sd_ref, slice(half, 2 * half), ob_ref)
    stores.append(store(ob_ref, ob_hbm, out_sems.at[5]))
    for copy in stores:
        copy.wait()


def shared_back(spre_ref, ca_ref, cb_ref, sd_ref):
    unit, half = sd_ref.shape[0], ca_ref.shape[1]
    sgp, sup = spre_ref[:, :unit], spre_ref[:, unit:]
    ssig = jax.nn.sigmoid(sgp)
    sgrad = mm(ca_ref[...], sd_ref[:, :half], 1, 1) + mm(cb_ref[...], sd_ref[:, half:], 1, 1)
    sgg = (sgrad * sup * ssig * (1.0 + sgp * (1.0 - ssig))).astype(BF16)
    sug = (sgrad * sgp * ssig).astype(BF16)
    return jnp.concatenate([sgg, sug], axis=1)


def shared_back_kernel(ca_ref, cb_ref, spre_ref, sd_ref, out_ref):
    out_ref[...] = shared_back(spre_ref, ca_ref, cb_ref, sd_ref)


def shared_back_half(parts, spre, sd):
    rows, half = parts[0].shape
    tile = min(512, rows)
    out_shape = jax.ShapeDtypeStruct(spre.shape, BF16)
    args = (*parts, spre, sd)
    return pl.pallas_call(
        shared_back_kernel,
        grid=(rows // tile,),
        in_specs=[spec_rows(tile, half)] * 2 + [spec_rows(tile, spre.shape[1]), spec_whole(sd)],
        out_specs=spec_rows(tile, spre.shape[1]),
        out_shape=out_shape,
        compiler_params=params(),
        cost_estimate=cost(16 * rows * half * sd.shape[0], list(args) + [out_shape]),
        name="shared_back",
    )(*args)


def backward_kernel(
    given, place_ref, gate_ref, ca_ref, cb_ref, wg_hbm, wu_hbm, wd_hbm, sgu_ref, sd_ref,
    gp_ref, up_ref, spre_ref,
    oa_hbm, ob_hbm, cs_hbm, ggp_hbm, ugp_hbm, sgrad_ref, score_ref,
    wg_ref, wu_ref, wd_ref, sems, oa_ref, ob_ref, cs_ref, ggp_ref, ugp_ref, cr_ref, out_sems,
):
    ready = fetch((wg_hbm, wu_hbm, wd_hbm), (wg_ref, wu_ref, wd_ref), sems)
    hits, picks, gate = picks_of(place_ref, gate_ref, cr_ref.shape[0])
    half = ca_ref.shape[1]
    take_rows(picks, ca_ref, cb_ref, cr_ref)
    both = spre_ref[...] if given else shared_back(spre_ref, ca_ref, cb_ref, sd_ref)
    sgrad_ref[...] = both
    cr = cr_ref[...]
    cs_ref[...] = (cr.astype(F32) * gate).astype(BF16)
    stores = [store(cs_ref, cs_hbm, out_sems.at[0])]
    ready(2)
    raw = mm(cr, wd_ref[...], 1, 1)
    gp, up = gp_ref[...], up_ref[...]
    sig = jax.nn.sigmoid(gp)
    silu = gp * sig
    score = jnp.sum(raw * (silu * up).astype(BF16).astype(F32), axis=1, keepdims=True)
    n, tokens = hits[0].shape
    for i, hit in enumerate(hits):
        part = jnp.where(hit, score[i * n : (i + 1) * n, :], 0.0)
        score_ref[0, :, i * tokens : (i + 1) * tokens] = jnp.sum(part, axis=0, keepdims=True)
    grad = raw * gate
    ggp = (grad * up * sig * (1.0 + gp * (1.0 - sig))).astype(BF16)
    ugp = (grad * silu).astype(BF16)
    ggp_ref[...] = ggp
    stores.append(store(ggp_ref, ggp_hbm, out_sems.at[1]))
    ugp_ref[...] = ugp
    stores.append(store(ugp_ref, ugp_hbm, out_sems.at[2]))
    ready(0, 1)
    rows = (mm(ggp, wg_ref[...], 1, 0) + mm(ugp, wu_ref[...], 1, 0)).astype(BF16)
    put_rows(picks, rows, both, sgu_ref, slice(0, half), oa_ref)
    stores.append(store(oa_ref, oa_hbm, out_sems.at[3]))
    put_rows(picks, rows, both, sgu_ref, slice(half, 2 * half), ob_ref)
    stores.append(store(ob_ref, ob_hbm, out_sems.at[4]))
    for copy in stores:
        copy.wait()


def spec_rows(rows, width):
    return pl.BlockSpec((rows, width), lambda i: (i, 0))


def spec_info(tok):
    return pl.BlockSpec((1, 1, tok), lambda i: (i, 0, 0))


def spec_whole(array):
    return pl.BlockSpec(array.shape, lambda i: (0,) * array.ndim, pipeline_mode=pl.Buffered(1))


def cost(flops, arrays):
    return pl.CostEstimate(
        flops=int(flops),
        bytes_accessed=int(sum(np.prod(a.shape) * a.dtype.itemsize for a in arrays)),
        transcendentals=0,
    )


def params():
    return pltpu.CompilerParams(
        dimension_semantics=("arbitrary",), vmem_limit_bytes=VMEM_LIMIT
    )


def half_call(name, kernel, place, gate, parts, weights, more, outs, own, scratch):
    groups, _, tokens = place.shape
    half = parts[1].shape[1]
    ff = weights[0].shape[1]
    hbm = pl.BlockSpec(memory_space=pl.ANY)
    once = dict(pipeline_mode=pl.Buffered(1)) if groups == 1 else {}
    by_group = lambda n: pl.BlockSpec((n.shape[0] // groups, n.shape[1]), lambda i: (i, 0), **once)
    args = (place, gate, *parts, *weights, *more)
    rows = outs[2].shape[0]
    unit = weights[4].shape[0]
    flops = 6 * rows * ff * 2 * half + 6 * groups * tokens * unit * 2 * half
    flops += 4 * rows * tokens * half
    return pl.pallas_call(
        kernel,
        grid=(groups,),
        in_specs=[spec_info(tokens)] * 2
        + [pl.BlockSpec((tokens, half), lambda i: (i, 0), **once)] * 2
        + [hbm] * 3
        + [spec_whole(w) for w in weights[3:]]
        + [by_group(m) for m in more],
        out_specs=[hbm] * own
        + [by_group(o) if len(o.shape) == 2 else spec_info(tokens) for o in outs[own:]],
        out_shape=outs,
        scratch_shapes=[pltpu.VMEM(w.shape[1:], BF16) for w in weights[:3]]
        + [pltpu.SemaphoreType.DMA((3,))]
        + [pltpu.VMEM((o.shape[0] // groups, o.shape[1]), o.dtype) for o in outs[:own]]
        + scratch
        + [pltpu.SemaphoreType.DMA((own,))],
        compiler_params=params(),
        cost_estimate=cost(4 * flops, list(args) + outs),
        name=name,
    )(*args)


def forward_half(place, gate, parts, weights, rows):
    tokens, half = parts[1].shape
    ff, unit = weights[0].shape[1], weights[4].shape[0]
    shape = jax.ShapeDtypeStruct
    outs = [
        shape((tokens, half), BF16),
        shape((tokens, half), BF16),
        shape((rows, 2 * half), BF16),
        shape((rows, ff), F32),
        shape((rows, ff), F32),
        shape((rows, ff), BF16),
        shape((tokens, 2 * unit), F32),
        shape((tokens, unit), BF16),
    ]
    return half_call("forward_half", forward_kernel, place, gate, parts, weights, (), outs, 6, [])


def backward_half(place, gate, parts, weights, ahead, rows, both=None):
    tokens, half = parts[1].shape
    ff, unit = weights[0].shape[1], weights[4].shape[0]
    shape = jax.ShapeDtypeStruct
    outs = [
        shape((tokens, half), BF16),
        shape((tokens, half), BF16),
        shape((rows, 2 * half), BF16),
        shape((rows, ff), BF16),
        shape((rows, ff), BF16),
        shape((tokens, 2 * unit), BF16),
        shape(place.shape, F32),
    ]
    more = (ahead[3], ahead[4], ahead[6] if both is None else both)
    kernel = functools.partial(backward_kernel, both is not None)
    scratch = [pltpu.VMEM((rows // place.shape[0], 2 * half), BF16)]
    return half_call(
        "backward_half", kernel, place, gate, parts, weights, more, outs, 5, scratch
    )


def shared_grads_kernel(
    g0_ref, g1_ref, h0_ref, h1_ref, xa0, xa1, xb0, xb1, ca0, ca1, cb0, cb1,
    ga_ref, gb_ref, da_ref, db_ref, gt_ref, ht_ref,
):
    rows = g0_ref.shape[0]

    @pl.when(pl.program_id(0) == 0)
    def _():
        gt_ref[:, :rows] = g0_ref[...].T
        gt_ref[:, rows:] = g1_ref[...].T
        ht_ref[:, :rows] = h0_ref[...].T
        ht_ref[:, rows:] = h1_ref[...].T

    for out, t_ref, one, two in (
        (ga_ref, gt_ref, xa0, xa1),
        (gb_ref, gt_ref, xb0, xb1),
        (da_ref, ht_ref, ca0, ca1),
        (db_ref, ht_ref, cb0, cb1),
    ):
        part = mm(t_ref[:, :rows], one[...], 1, 0) + mm(t_ref[:, rows:], two[...], 1, 0)
        out[...] = part.astype(BF16)


def shared_grads(grads, hiddens, xs, cs):
    rows, half = xs[2].shape
    unit2, unit = grads[0].shape[1], hiddens[0].shape[1]
    tile = min(256, half)
    col = pl.BlockSpec((rows, tile), lambda i: (0, i))
    args = (*grads, *hiddens, *xs, *cs)
    out_shape = [jax.ShapeDtypeStruct((n, half), BF16) for n in (unit2, unit2, unit, unit)]
    return pl.pallas_call(
        shared_grads_kernel,
        grid=(half // tile,),
        in_specs=[spec_whole(a) for a in (*grads, *hiddens)] + [col] * 8,
        out_specs=[pl.BlockSpec((o.shape[0], tile), lambda i: (0, i)) for o in out_shape],
        out_shape=out_shape,
        scratch_shapes=[pltpu.VMEM((unit2, 2 * rows), BF16), pltpu.VMEM((unit, 2 * rows), BF16)],
        compiler_params=params(),
        cost_estimate=cost(8 * rows * half * (unit2 + unit), list(args) + out_shape),
        name="shared_grads",
    )(*args)


def expert_grads_kernel(
    x0_ref, x1_ref, c0_ref, c1_ref, g0_ref, g1_ref, u0_ref, u1_ref, h0_ref, h1_ref,
    wg_ref, wu_ref, wd_ref, gt_ref, ut_ref, ht_ref,
):
    rows = x0_ref.shape[0]

    @pl.when(pl.program_id(0) == 0)
    def _():
        for t_ref, one, two in (
            (gt_ref, g0_ref, g1_ref), (ut_ref, u0_ref, u1_ref), (ht_ref, h0_ref, h1_ref)
        ):
            t_ref[:, :rows] = one[...].T
            t_ref[:, rows:] = two[...].T

    x = jnp.concatenate([x0_ref[...], x1_ref[...]], axis=0)
    c = jnp.concatenate([c0_ref[...], c1_ref[...]], axis=0)
    wg_ref[0] = mm(gt_ref[...], x, 1, 0).astype(BF16)
    wu_ref[0] = mm(ut_ref[...], x, 1, 0).astype(BF16)
    wd_ref[0] = mm(ht_ref[...], c, 1, 0).astype(BF16)


def expert_grads(xr, cs, ggp, ugp, hid):
    rows, width = xr[0].shape
    ff = ggp[0].shape[1]
    tile = min(256, width)
    col = pl.BlockSpec((rows, tile), lambda i: (0, i))
    args = (*xr, *cs, *ggp, *ugp, *hid)
    out_shape = [jax.ShapeDtypeStruct((1, ff, width), BF16)] * 3
    return pl.pallas_call(
        expert_grads_kernel,
        grid=(width // tile,),
        in_specs=[col] * 4 + [spec_whole(a) for a in (*ggp, *ugp, *hid)],
        out_specs=[pl.BlockSpec((1, ff, tile), lambda i: (0, 0, i))] * 3,
        out_shape=out_shape,
        scratch_shapes=[pltpu.VMEM((ff, 2 * rows), BF16)] * 3,
        compiler_params=params(),
        cost_estimate=cost(24 * rows * width * ff, list(args) + out_shape),
        name="expert_grads",
    )(*args)


def local(tokens, expert_ids, gates, w_gate, w_up, w_down, s_gate, s_up, s_down, cotangent):
    tok, width = tokens.shape
    top = expert_ids.shape[1]
    experts, dp = lax.axis_size("expert"), lax.axis_size("dp")
    me, my_dp = lax.axis_index("expert"), lax.axis_index("dp")
    capacity = min(tok, 5 * tok * top // (4 * experts))
    slots = -(-capacity // 16) * 16
    units = s_gate.shape[1] // experts
    share, half = tok // dp, width // 2
    sizes = split_of(experts, dp)
    shares_at = my_dp ^ jnp.arange(dp, dtype=jnp.int32)
    turns = ((3, 1), (1, 3))
    shape = (1,) + sizes[1:] + (share, half)
    flat = lambda parts: [p.reshape(-1, p.shape[5]) for p in parts]
    full = lambda parts: [p.reshape(shape) for p in parts]

    def mine(rows):
        rows = lax.dynamic_slice_in_dim(rows, my_dp * share, share, 0)
        return [rows[:, i * half : (i + 1) * half].reshape(1, 1, 1, 1, share, half) for i in range(2)]

    halves = lambda rows: [rows[..., i * half : (i + 1) * half] for i in range(2)]
    mine = lambda rows: lax.dynamic_slice_in_dim(rows, my_dp * share, share, 0)[None, None, None, None]
    high = lax.reduce_precision(gates, 8, 7)
    facts = jnp.concatenate([expert_ids.astype(F32), high, gates - high], axis=1).astype(BF16)
    facts = jnp.pad(facts, ((0, 0), (0, FACTS - facts.shape[1])))
    x0 = mine(jnp.concatenate([tokens[:, :half], facts, tokens[:, half:]], axis=1))
    x1 = spread(x0, sizes, 2)
    x1 = (x1[..., : half + FACTS], x1[..., half + FACTS :])
    x2 = [spread(p, sizes, turn[0]) for p, turn in zip(x1, turns)]
    x3 = [spread(p, sizes, turn[1]) for p, turn in zip(x2, turns)]
    c1 = spread(after(mine(cotangent), x2), sizes, 2, x3)
    own_x = flat(x3)
    other_x = [partner(p, sizes, 0, 1) for p in own_x]

    before = jnp.triu(jnp.ones((tok, tok), BF16), 1)
    start = slots * (jnp.arange(experts // 2, dtype=jnp.int32) % GROUP)

    def routing(part):
        known = part[:, half : half + 3 * top].astype(F32).T.reshape(3, top, experts // 2, tok)
        hit = known[0] == me.astype(F32)
        taken = jnp.any(hit, axis=0)
        gate = jnp.sum(jnp.where(hit, known[1] + known[2], 0.0), axis=0)
        place = mm(taken.astype(BF16), before, 1, 0).astype(jnp.int32) + start[:, None]
        place = jnp.where(taken, place, -1)
        return place.reshape(-1, 1, GROUP * tok), gate.reshape(-1, 1, GROUP * tok)

    place, gate = zip(routing(own_x[0]), routing(other_x[0]))

    pad = -units % 128
    first = after(me * units, x2)
    widen = lambda m: jnp.pad(m, ((0, pad), (0, 0)))
    columns = lambda m: widen(lax.dynamic_slice_in_dim(m, first, units, 1).T)
    sgu = jnp.concatenate([columns(s_gate), columns(s_up)], axis=0)
    sd = widen(lax.dynamic_slice_in_dim(s_down, first, units, 0))
    weights = (w_gate.swapaxes(1, 2), w_up.swapaxes(1, 2), w_down, sgu, sd)

    rows = experts // 2 * slots
    ahead0 = forward_half(place[0], gate[0], own_x, weights, rows)
    c2 = [spread(p, sizes, turn[0], ahead0[0]) for p, turn in zip(halves(c1), turns)]
    ahead1 = forward_half(after(place[1], c2), gate[1], after(other_x, ahead0[0]), weights, rows)
    c3 = [spread(p, sizes, turn[1], ahead1[0]) for p, turn in zip(c2, turns)]
    own_c = flat(c3)
    back0 = backward_half(place[0], gate[0], own_c, weights, ahead0, rows)
    out_came = after([partner(p, sizes, 0, 1) for p in full(ahead1[:2])], back0[0])
    out = [list(t) for t in zip(full(ahead0[:2]), out_came)]
    out = [parts_for(t, sizes, turn[1]) for t, turn in zip(out, turns)]
    other_c = after([partner(p, sizes, 0, 1) for p in own_c], back0[0])

    both1 = shared_back_half(after(other_c, [sent for sent, _ in out]), ahead1[6], sd)
    ga, gb, da, db = shared_grads(
        [back0[5], both1],
        [ahead0[7], ahead1[7]],
        [own_x[0], other_x[0], own_x[1], other_x[1]],
        [own_c[0], other_c[0], own_c[1], other_c[1]],
    )
    out = [fold(*t, sizes, turn[1], ga) for t, turn in zip(out, turns)]
    out = [parts_for(t, sizes, turn[0]) for t, turn in zip(out, turns)]
    unit = units + pad
    both = jnp.concatenate([ga, gb], axis=1)
    grads = jnp.concatenate(
        [both[:units], both[unit : unit + units], jnp.concatenate([da, db], axis=1)[:units]], axis=0
    )
    send = grads.reshape(3 * units, experts, width // experts).transpose(1, 0, 2)
    got = lax.all_to_all(send, "expert", split_axis=0, concat_axis=0, tiled=True)
    back1 = backward_half(
        after(place[1], send, [sent for sent, _ in out]), gate[1], other_c, weights, ahead1, rows, both1
    )

    out = [fold(*t, sizes, turn[0], back1[0]) for t, turn in zip(out, turns)]
    back1_out, got = after((back1[:2], got), [t[-1] for t in out])
    dx_came = [partner(p, sizes, 0, 1) for p in full(after(back1_out, got))]
    out = [jnp.concatenate(p, axis=5) for p in zip(*out)]
    out = parts_for(out, sizes, 2)
    dx = [list(t) for t in zip(full(back0[:2]), after(dx_came, out[0]))]
    dx = [parts_for(t, sizes, turn[1]) for t, turn in zip(dx, turns)]
    dx_sent = [sent for sent, _ in dx]

    index = np.arange(experts).reshape(sizes[2], sizes[1], 2).transpose(2, 1, 0).reshape(-1)
    where = jnp.asarray(np.argsort(index), jnp.int32)[me ^ jnp.arange(experts, dtype=jnp.int32)]
    score = jnp.stack(after([back0[6], back1[6]], dx_sent)).reshape(experts, dp, share)
    score = score[where][:, shares_at].reshape(experts, tok)
    scores = lax.all_to_all(score, "expert", split_axis=0, concat_axis=0, tiled=True).T
    named = expert_ids[:, :, None] == jnp.arange(experts, dtype=jnp.int32)[None, None, :]
    gate_part = jnp.sum(jnp.where(named, scores[:, None, :], 0.0), axis=2)
    gate_grads = gate_part
    for k in range(1, dp):
        gate_grads = gate_grads + partner(gate_part, sizes, 3, k)

    got = after(got, dx_sent)
    grad_sg = got[:, :units].reshape(experts * units, -1).T
    grad_su = got[:, units : 2 * units].reshape(experts * units, -1).T
    grad_sd = got[:, 2 * units :].reshape(experts * units, -1)
    out = fold(*out, sizes, 2, dx_sent)
    dx = [fold(*t, sizes, turn[1], out[1:], grad_sd) for t, turn in zip(dx, turns)]
    dx = [parts_for(t, sizes, turn[0]) for t, turn in zip(dx, turns)]
    dx_sent = [sent for sent, _ in dx]
    moe_out = both_halves(total(after(out, dx_sent)).reshape(share, width), sizes)
    dx = [fold(*t, sizes, turn[0]) for t, turn in zip(dx, turns)]
    dx = [jnp.concatenate(p, axis=5) for p in zip(*dx)]
    dx = parts_for(dx, sizes, 2)
    grad_wg, grad_wu, grad_wd = expert_grads(
        [ahead0[2], ahead1[2]],
        after([back0[2], back1[2]], dx[0]),
        [back0[3], back1[3]],
        [back0[4], back1[4]],
        [ahead0[5], ahead1[5]],
    )
    token_grads = both_halves(total(fold(*dx, sizes, 2, grad_wg)).reshape(share, width), sizes)
    grad_wg, grad_wu = grad_wg.swapaxes(1, 2), grad_wu.swapaxes(1, 2)
    return (moe_out, token_grads, gate_grads, grad_wg, grad_wu, grad_wd, grad_sg, grad_su, grad_sd)


def solution(mesh):
    row = P("expert", None)
    cols = P("expert", None, "dp")
    return jax.shard_map(
        local,
        mesh=mesh,
        in_specs=(
            row, row, row, cols, cols, P("expert", "dp", None),
            P(None, "dp"), P(None, "dp"), P("dp", None), row,
        ),
        out_specs=(
            row, row, row, cols, cols, P("expert", "dp", None),
            P("expert", "dp"), P("expert", "dp"), P("dp", "expert"),
        ),
        check_vma=False,
    )
```

```python
import functools

import jax
import jax.numpy as jnp
import numpy as np
from jax import lax
from jax.experimental import pallas as pl
from jax.experimental.pallas import tpu as pltpu
from jax.sharding import PartitionSpec as P

F32 = jnp.float32
BF16 = jnp.bfloat16
GROUP = 8
SUB = 4
FACTS = 128
VMEM_LIMIT = 56 * 1024 * 1024


def mm(left, right, left_dim, right_dim):
    return lax.dot_general(
        left, right, (((left_dim,), (right_dim,)), ((), ())), preferred_element_type=F32
    )


def split_of(experts, dp):
    bits = experts.bit_length() - 1
    middle = (bits - 1) // 2
    return (2, 1 << middle, 1 << (bits - 1 - middle), dp)


def partner(array, sizes, dim, k):
    if dim == 3:
        axis, mask = "dp", k
    else:
        axis, mask = "expert", k * (1, 2, 2 * sizes[1])[dim]
    return lax.ppermute(array, axis, [(i, i ^ mask) for i in range(lax.axis_size(axis))])


def after(arrays, *earlier):
    return lax.optimization_barrier((arrays, earlier))[0]


def spread(out, sizes, dim, *earlier):
    came = [partner(out, sizes, dim, k) for k in range(1, sizes[dim])]
    return jnp.concatenate([out] + after(came, *earlier), axis=dim)


def total(terms):
    out = terms[0].astype(F32)
    for term in terms[1:]:
        out = out + term.astype(F32)
    return out.astype(BF16)


def parts_for(terms, sizes, dim):
    cut = lambda k: total([lax.slice_in_dim(t, k, k + 1, axis=dim) for t in terms])
    return [cut(k) for k in range(1, sizes[dim])], [cut(0)]


def fold(sent, stays, sizes, dim, *earlier):
    return stays + after([partner(part, sizes, dim, k + 1) for k, part in enumerate(sent)], *earlier)


def both_halves(rows, sizes):
    out = [rows] + [partner(rows, sizes, 3, k) for k in range(1, sizes[3])]
    out = jnp.stack(out)
    order = jnp.arange(sizes[3]) ^ lax.axis_index("dp")
    return out[order].reshape(-1, rows.shape[1])


def picks_of(place_ref, gate_ref, rows):
    parts = GROUP // SUB
    tokens = place_ref.shape[2] // parts
    hits, gates = [], []
    for i in range(parts):
        cut = slice(i * tokens, (i + 1) * tokens)
        place = place_ref[0, :, cut] - i * (rows // parts)
        hit = lax.broadcasted_iota(jnp.int32, (rows // parts, tokens), 0) == place
        hits.append(hit)
        gates.append(jnp.sum(jnp.where(hit, gate_ref[0, :, cut], 0.0), axis=1, keepdims=True))
    return hits, [hit.astype(BF16) for hit in hits], jnp.concatenate(gates, axis=0)


def take_rows(picks, a_ref, b_ref, rows_ref):
    half = a_ref.shape[1]
    rows, tokens = 2 * picks[0].shape[0] // SUB, 2 * picks[0].shape[1] // SUB
    for i in range(GROUP // 2):
        pick, j = picks[2 * i // SUB], i % (SUB // 2)
        pick = pick[j * rows : (j + 1) * rows, j * tokens : (j + 1) * tokens]
        r, t = slice(i * rows, (i + 1) * rows), slice(i * tokens, (i + 1) * tokens)
        rows_ref[r, :half] = mm(pick, a_ref[t, :], 1, 0).astype(BF16)
        rows_ref[r, half:] = mm(pick, b_ref[t, :], 1, 0).astype(BF16)


def put_rows(picks, rows, units, weight_ref, cut, out_ref):
    n, tokens = picks[0].shape
    for i, pick in enumerate(picks):
        t = slice(i * tokens, (i + 1) * tokens)
        left = jnp.concatenate([pick.T, units[t, :]], axis=1)
        right = jnp.concatenate([rows[i * n : (i + 1) * n, cut], weight_ref[:, cut]], axis=0)
        out_ref[t, :] = mm(left, right, 1, 0).astype(BF16)


def store(source, target, sem):
    n = source.shape[0]
    at = pl.multiple_of(pl.program_id(0) * n, n)
    copy = pltpu.make_async_copy(source, target.at[pl.ds(at, n)], sem)
    copy.start()
    return copy


def fetch(sources, targets, sems):
    copies = [
        pltpu.make_async_copy(src.at[0], dst, sems.at[i])
        for i, (src, dst) in enumerate(zip(sources, targets))
    ]

    @pl.when(pl.program_id(0) == 0)
    def _():
        for copy in copies:
            copy.start()

    def ready(*which):
        @pl.when(pl.program_id(0) == 0)
        def _():
            for i in which:
                copies[i].wait()

    return ready


def forward_kernel(
    place_ref, gate_ref, xa_ref, xb_ref, wg_hbm, wu_hbm, wd_hbm, sgu_ref, sd_ref,
    oa_hbm, ob_hbm, xr_hbm, gp_hbm, up_hbm, hid_hbm, spre_ref, shid_ref,
    wg_ref, wu_ref, wd_ref, sems, oa_ref, ob_ref, xr_ref, gp_ref, up_ref, hid_ref, out_sems,
):
    ready = fetch((wg_hbm, wu_hbm, wd_hbm), (wg_ref, wu_ref, wd_ref), sems)
    hits, picks, gate = picks_of(place_ref, gate_ref, xr_ref.shape[0])
    half = xa_ref.shape[1]
    unit = sd_ref.shape[0]
    take_rows(picks, xa_ref, xb_ref, xr_ref)
    stores = [store(xr_ref, xr_hbm, out_sems.at[0])]
    spre = mm(xa_ref[...], sgu_ref[:, :half], 1, 1) + mm(xb_ref[...], sgu_ref[:, half:], 1, 1)
    spre_ref[...] = spre
    sgp, sup = spre[:, :unit], spre[:, unit:]
    shid = (sgp * jax.nn.sigmoid(sgp) * sup).astype(BF16)
    shid_ref[...] = shid
    xr = xr_ref[...]
    ready(0, 1)
    gp = mm(xr, wg_ref[...], 1, 1)
    gp_ref[...] = gp
    stores.append(store(gp_ref, gp_hbm, out_sems.at[1]))
    up = mm(xr, wu_ref[...], 1, 1)
    up_ref[...] = up
    stores.append(store(up_ref, up_hbm, out_sems.at[2]))
    hid = (gp * jax.nn.sigmoid(gp) * up).astype(BF16)
    hid_ref[...] = hid
    stores.append(store(hid_ref, hid_hbm, out_sems.at[3]))
    ready(2)
    rows = (mm(hid, wd_ref[...], 1, 0) * gate).astype(BF16)
    put_rows(picks, rows, shid, sd_ref, slice(0, half), oa_ref)
    stores.append(store(oa_ref, oa_hbm, out_sems.at[4]))
    put_rows(picks, rows, shid, sd_ref, slice(half, 2 * half), ob_ref)
    stores.append(store(ob_ref, ob_hbm, out_sems.at[5]))
    for copy in stores:
        copy.wait()


def shared_back(spre_ref, ca_ref, cb_ref, sd_ref):
    unit, half = sd_ref.shape[0], ca_ref.shape[1]
    sgp, sup = spre_ref[:, :unit], spre_ref[:, unit:]
    ssig = jax.nn.sigmoid(sgp)
    sgrad = mm(ca_ref[...], sd_ref[:, :half], 1, 1) + mm(cb_ref[...], sd_ref[:, half:], 1, 1)
    sgg = (sgrad * sup * ssig * (1.0 + sgp * (1.0 - ssig))).astype(BF16)
    sug = (sgrad * sgp * ssig).astype(BF16)
    return jnp.concatenate([sgg, sug], axis=1)


def shared_back_kernel(ca_ref, cb_ref, spre_ref, sd_ref, out_ref):
    out_ref[...] = shared_back(spre_ref, ca_ref, cb_ref, sd_ref)


def shared_back_half(parts, spre, sd):
    rows, half = parts[0].shape
    tile = min(512, rows)
    out_shape = jax.ShapeDtypeStruct(spre.shape, BF16)
    args = (*parts, spre, sd)
    return pl.pallas_call(
        shared_back_kernel,
        grid=(rows // tile,),
        in_specs=[spec_rows(tile, half)] * 2 + [spec_rows(tile, spre.shape[1]), spec_whole(sd)],
        out_specs=spec_rows(tile, spre.shape[1]),
        out_shape=out_shape,
        compiler_params=params(),
        cost_estimate=cost(16 * rows * half * sd.shape[0], list(args) + [out_shape]),
        name="shared_back",
    )(*args)


def backward_kernel(
    given, place_ref, gate_ref, ca_ref, cb_ref, wg_hbm, wu_hbm, wd_hbm, sgu_ref, sd_ref,
    gp_ref, up_ref, spre_ref,
    oa_hbm, ob_hbm, cs_hbm, ggp_hbm, ugp_hbm, sgrad_ref, score_ref,
    wg_ref, wu_ref, wd_ref, sems, oa_ref, ob_ref, cs_ref, ggp_ref, ugp_ref, cr_ref, out_sems,
):
    ready = fetch((wg_hbm, wu_hbm, wd_hbm), (wg_ref, wu_ref, wd_ref), sems)
    hits, picks, gate = picks_of(place_ref, gate_ref, cr_ref.shape[0])
    half = ca_ref.shape[1]
    take_rows(picks, ca_ref, cb_ref, cr_ref)
    both = spre_ref[...] if given else shared_back(spre_ref, ca_ref, cb_ref, sd_ref)
    sgrad_ref[...] = both
    cr = cr_ref[...]
    cs_ref[...] = (cr.astype(F32) * gate).astype(BF16)
    stores = [store(cs_ref, cs_hbm, out_sems.at[0])]
    ready(2)
    raw = mm(cr, wd_ref[...], 1, 1)
    gp, up = gp_ref[...], up_ref[...]
    sig = jax.nn.sigmoid(gp)
    silu = gp * sig
    score = jnp.sum(raw * (silu * up).astype(BF16).astype(F32), axis=1, keepdims=True)
    n, tokens = hits[0].shape
    for i, hit in enumerate(hits):
        part = jnp.where(hit, score[i * n : (i + 1) * n, :], 0.0)
        score_ref[0, :, i * tokens : (i + 1) * tokens] = jnp.sum(part, axis=0, keepdims=True)
    grad = raw * gate
    ggp = (grad * up * sig * (1.0 + gp * (1.0 - sig))).astype(BF16)
    ugp = (grad * silu).astype(BF16)
    ggp_ref[...] = ggp
    stores.append(store(ggp_ref, ggp_hbm, out_sems.at[1]))
    ugp_ref[...] = ugp
    stores.append(store(ugp_ref, ugp_hbm, out_sems.at[2]))
    ready(0, 1)
    rows = (mm(ggp, wg_ref[...], 1, 0) + mm(ugp, wu_ref[...], 1, 0)).astype(BF16)
    put_rows(picks, rows, both, sgu_ref, slice(0, half), oa_ref)
    stores.append(store(oa_ref, oa_hbm, out_sems.at[3]))
    put_rows(picks, rows, both, sgu_ref, slice(half, 2 * half), ob_ref)
    stores.append(store(ob_ref, ob_hbm, out_sems.at[4]))
    for copy in stores:
        copy.wait()


def spec_rows(rows, width):
    return pl.BlockSpec((rows, width), lambda i: (i, 0))


def spec_info(tok):
    return pl.BlockSpec((1, 1, tok), lambda i: (i, 0, 0))


def spec_whole(array):
    return pl.BlockSpec(array.shape, lambda i: (0,) * array.ndim, pipeline_mode=pl.Buffered(1))


def cost(flops, arrays):
    return pl.CostEstimate(
        flops=int(flops),
        bytes_accessed=int(sum(np.prod(a.shape) * a.dtype.itemsize for a in arrays)),
        transcendentals=0,
    )


def params():
    return pltpu.CompilerParams(
        dimension_semantics=("arbitrary",), vmem_limit_bytes=VMEM_LIMIT
    )


def half_call(name, kernel, place, gate, parts, weights, more, outs, own, scratch):
    groups, _, tokens = place.shape
    half = parts[1].shape[1]
    ff = weights[0].shape[1]
    hbm = pl.BlockSpec(memory_space=pl.ANY)
    once = dict(pipeline_mode=pl.Buffered(1)) if groups == 1 else {}
    by_group = lambda n: pl.BlockSpec((n.shape[0] // groups, n.shape[1]), lambda i: (i, 0), **once)
    args = (place, gate, *parts, *weights, *more)
    rows = outs[2].shape[0]
    unit = weights[4].shape[0]
    flops = 6 * rows * ff * 2 * half + 6 * groups * tokens * unit * 2 * half
    flops += 4 * rows * tokens * half
    return pl.pallas_call(
        kernel,
        grid=(groups,),
        in_specs=[spec_info(tokens)] * 2
        + [pl.BlockSpec((tokens, half), lambda i: (i, 0), **once)] * 2
        + [hbm] * 3
        + [spec_whole(w) for w in weights[3:]]
        + [by_group(m) for m in more],
        out_specs=[hbm] * own
        + [by_group(o) if len(o.shape) == 2 else spec_info(tokens) for o in outs[own:]],
        out_shape=outs,
        scratch_shapes=[pltpu.VMEM(w.shape[1:], BF16) for w in weights[:3]]
        + [pltpu.SemaphoreType.DMA((3,))]
        + [pltpu.VMEM((o.shape[0] // groups, o.shape[1]), o.dtype) for o in outs[:own]]
        + scratch
        + [pltpu.SemaphoreType.DMA((own,))],
        compiler_params=params(),
        cost_estimate=cost(4 * flops, list(args) + outs),
        name=name,
    )(*args)


def forward_half(place, gate, parts, weights, rows):
    tokens, half = parts[1].shape
    ff, unit = weights[0].shape[1], weights[4].shape[0]
    shape = jax.ShapeDtypeStruct
    outs = [
        shape((tokens, half), BF16),
        shape((tokens, half), BF16),
        shape((rows, 2 * half), BF16),
        shape((rows, ff), F32),
        shape((rows, ff), F32),
        shape((rows, ff), BF16),
        shape((tokens, 2 * unit), F32),
        shape((tokens, unit), BF16),
    ]
    return half_call("forward_half", forward_kernel, place, gate, parts, weights, (), outs, 6, [])


def backward_half(place, gate, parts, weights, ahead, rows, both=None):
    tokens, half = parts[1].shape
    ff, unit = weights[0].shape[1], weights[4].shape[0]
    shape = jax.ShapeDtypeStruct
    outs = [
        shape((tokens, half), BF16),
        shape((tokens, half), BF16),
        shape((rows, 2 * half), BF16),
        shape((rows, ff), BF16),
        shape((rows, ff), BF16),
        shape((tokens, 2 * unit), BF16),
        shape(place.shape, F32),
    ]
    more = (ahead[3], ahead[4], ahead[6] if both is None else both)
    kernel = functools.partial(backward_kernel, both is not None)
    scratch = [pltpu.VMEM((rows // place.shape[0], 2 * half), BF16)]
    return half_call(
        "backward_half", kernel, place, gate, parts, weights, more, outs, 5, scratch
    )


def shared_grads_kernel(
    g0_ref, g1_ref, h0_ref, h1_ref, xa0, xa1, xb0, xb1, ca0, ca1, cb0, cb1,
    ga_ref, gb_ref, da_ref, db_ref, gt_ref, ht_ref,
):
    rows = g0_ref.shape[0]

    @pl.when(pl.program_id(0) == 0)
    def _():
        gt_ref[:, :rows] = g0_ref[...].T
        gt_ref[:, rows:] = g1_ref[...].T
        ht_ref[:, :rows] = h0_ref[...].T
        ht_ref[:, rows:] = h1_ref[...].T

    for out, t_ref, one, two in (
        (ga_ref, gt_ref, xa0, xa1),
        (gb_ref, gt_ref, xb0, xb1),
        (da_ref, ht_ref, ca0, ca1),
        (db_ref, ht_ref, cb0, cb1),
    ):
        part = mm(t_ref[:, :rows], one[...], 1, 0) + mm(t_ref[:, rows:], two[...], 1, 0)
        out[...] = part.astype(BF16)


def shared_grads(grads, hiddens, xs, cs):
    rows, half = xs[2].shape
    unit2, unit = grads[0].shape[1], hiddens[0].shape[1]
    tile = min(256, half)
    col = pl.BlockSpec((rows, tile), lambda i: (0, i))
    args = (*grads, *hiddens, *xs, *cs)
    out_shape = [jax.ShapeDtypeStruct((n, half), BF16) for n in (unit2, unit2, unit, unit)]
    return pl.pallas_call(
        shared_grads_kernel,
        grid=(half // tile,),
        in_specs=[spec_whole(a) for a in (*grads, *hiddens)] + [col] * 8,
        out_specs=[pl.BlockSpec((o.shape[0], tile), lambda i: (0, i)) for o in out_shape],
        out_shape=out_shape,
        scratch_shapes=[pltpu.VMEM((unit2, 2 * rows), BF16), pltpu.VMEM((unit, 2 * rows), BF16)],
        compiler_params=params(),
        cost_estimate=cost(8 * rows * half * (unit2 + unit), list(args) + out_shape),
        name="shared_grads",
    )(*args)


def expert_grads_kernel(
    x0_ref, x1_ref, c0_ref, c1_ref, g0_ref, g1_ref, u0_ref, u1_ref, h0_ref, h1_ref,
    wg_ref, wu_ref, wd_ref, gt_ref, ut_ref, ht_ref,
):
    rows = x0_ref.shape[0]

    @pl.when(pl.program_id(0) == 0)
    def _():
        for t_ref, one, two in (
            (gt_ref, g0_ref, g1_ref), (ut_ref, u0_ref, u1_ref), (ht_ref, h0_ref, h1_ref)
        ):
            t_ref[:, :rows] = one[...].T
            t_ref[:, rows:] = two[...].T

    x = jnp.concatenate([x0_ref[...], x1_ref[...]], axis=0)
    c = jnp.concatenate([c0_ref[...], c1_ref[...]], axis=0)
    wg_ref[0] = mm(gt_ref[...], x, 1, 0).astype(BF16)
    wu_ref[0] = mm(ut_ref[...], x, 1, 0).astype(BF16)
    wd_ref[0] = mm(ht_ref[...], c, 1, 0).astype(BF16)


def expert_grads(xr, cs, ggp, ugp, hid):
    rows, width = xr[0].shape
    ff = ggp[0].shape[1]
    tile = min(256, width)
    col = pl.BlockSpec((rows, tile), lambda i: (0, i))
    args = (*xr, *cs, *ggp, *ugp, *hid)
    out_shape = [jax.ShapeDtypeStruct((1, ff, width), BF16)] * 3
    return pl.pallas_call(
        expert_grads_kernel,
        grid=(width // tile,),
        in_specs=[col] * 4 + [spec_whole(a) for a in (*ggp, *ugp, *hid)],
        out_specs=[pl.BlockSpec((1, ff, tile), lambda i: (0, 0, i))] * 3,
        out_shape=out_shape,
        scratch_shapes=[pltpu.VMEM((ff, 2 * rows), BF16)] * 3,
        compiler_params=params(),
        cost_estimate=cost(24 * rows * width * ff, list(args) + out_shape),
        name="expert_grads",
    )(*args)


def local(tokens, expert_ids, gates, w_gate, w_up, w_down, s_gate, s_up, s_down, cotangent):
    tok, width = tokens.shape
    top = expert_ids.shape[1]
    experts, dp = lax.axis_size("expert"), lax.axis_size("dp")
    me, my_dp = lax.axis_index("expert"), lax.axis_index("dp")
    capacity = min(tok, 5 * tok * top // (4 * experts))
    slots = -(-capacity // 16) * 16
    units = s_gate.shape[1] // experts
    share, half = tok // dp, width // 2
    sizes = split_of(experts, dp)
    shares_at = my_dp ^ jnp.arange(dp, dtype=jnp.int32)
    turns = ((3, 1), (1, 3))
    shape = (1,) + sizes[1:] + (share, half)
    flat = lambda parts: [p.reshape(-1, p.shape[5]) for p in parts]
    full = lambda parts: [p.reshape(shape) for p in parts]

    def mine(rows):
        rows = lax.dynamic_slice_in_dim(rows, my_dp * share, share, 0)
        return [rows[:, i * half : (i + 1) * half].reshape(1, 1, 1, 1, share, half) for i in range(2)]

    halves = lambda rows: [rows[..., i * half : (i + 1) * half] for i in range(2)]
    mine = lambda rows: lax.dynamic_slice_in_dim(rows, my_dp * share, share, 0)[None, None, None, None]
    high = lax.reduce_precision(gates, 8, 7)
    facts = jnp.concatenate([expert_ids.astype(F32), high, gates - high], axis=1).astype(BF16)
    facts = jnp.pad(facts, ((0, 0), (0, FACTS - facts.shape[1])))
    x0 = mine(jnp.concatenate([tokens[:, :half], facts, tokens[:, half:]], axis=1))
    x1 = spread(x0, sizes, 2)
    x1 = (x1[..., : half + FACTS], x1[..., half + FACTS :])
    x2 = [spread(p, sizes, turn[0]) for p, turn in zip(x1, turns)]
    c1 = spread(after(mine(cotangent), x1), sizes, 2, x2)
    x3 = [spread(p, sizes, turn[1]) for p, turn in zip(x2, turns)]
    own_x = flat(x3)
    other_x = [partner(p, sizes, 0, 1) for p in own_x]

    before = jnp.triu(jnp.ones((tok, tok), BF16), 1)
    start = slots * (jnp.arange(experts // 2, dtype=jnp.int32) % GROUP)

    def routing(part):
        known = part[:, half : half + 3 * top].astype(F32).T.reshape(3, top, experts // 2, tok)
        hit = known[0] == me.astype(F32)
        taken = jnp.any(hit, axis=0)
        gate = jnp.sum(jnp.where(hit, known[1] + known[2], 0.0), axis=0)
        place = mm(taken.astype(BF16), before, 1, 0).astype(jnp.int32) + start[:, None]
        place = jnp.where(taken, place, -1)
        return place.reshape(-1, 1, GROUP * tok), gate.reshape(-1, 1, GROUP * tok)

    place, gate = zip(routing(own_x[0]), routing(other_x[0]))

    pad = -units % 128
    first = after(me * units, x1)
    widen = lambda m: jnp.pad(m, ((0, pad), (0, 0)))
    columns = lambda m: widen(lax.dynamic_slice_in_dim(m, first, units, 1).T)
    sgu = jnp.concatenate([columns(s_gate), columns(s_up)], axis=0)
    sd = widen(lax.dynamic_slice_in_dim(s_down, first, units, 0))
    weights = (w_gate.swapaxes(1, 2), w_up.swapaxes(1, 2), w_down, sgu, sd)

    rows = experts // 2 * slots
    ahead0 = forward_half(place[0], gate[0], own_x, weights, rows)
    c2 = [spread(p, sizes, turn[0], ahead0[0]) for p, turn in zip(after(halves(c1), x3), turns)]
    ahead1 = forward_half(after(place[1], c2), gate[1], after(other_x, ahead0[0]), weights, rows)
    c3 = [spread(p, sizes, turn[1], ahead1[0]) for p, turn in zip(c2, turns)]
    own_c = flat(c3)
    back0 = backward_half(place[0], gate[0], own_c, weights, ahead0, rows)
    out_came = after([partner(p, sizes, 0, 1) for p in full(ahead1[:2])], back0[0])
    out = [list(t) for t in zip(full(ahead0[:2]), out_came)]
    out = [parts_for(t, sizes, turn[1]) for t, turn in zip(out, turns)]
    other_c = after([partner(p, sizes, 0, 1) for p in own_c], back0[0])

    both1 = shared_back_half(after(other_c, [sent for sent, _ in out]), ahead1[6], sd)
    ga, gb, da, db = shared_grads(
        [back0[5], both1],
        [ahead0[7], ahead1[7]],
        [own_x[0], other_x[0], own_x[1], other_x[1]],
        [own_c[0], other_c[0], own_c[1], other_c[1]],
    )
    out = [fold(*t, sizes, turn[1], ga) for t, turn in zip(out, turns)]
    terms = out
    out = [parts_for(t, sizes, turn[0]) for t, turn in zip(out, turns)]
    unit = units + pad
    both = jnp.concatenate([ga, gb], axis=1)
    grads = jnp.concatenate(
        [both[:units], both[unit : unit + units], jnp.concatenate([da, db], axis=1)[:units]], axis=0
    )
    send = grads.reshape(3 * units, experts, width // experts).transpose(1, 0, 2)
    got = lax.all_to_all(send, "expert", split_axis=0, concat_axis=0, tiled=True)
    back1 = backward_half(
        after(place[1], send, [sent for sent, _ in out]), gate[1], other_c, weights, ahead1, rows, both1
    )

    kept = [parts_for(after(t, back1[0]), sizes, turn[0])[1] for t, turn in zip(terms, turns)]
    out = [fold(t[0], k, sizes, turn[0], back1[0]) for t, k, turn in zip(out, kept, turns)]
    back1_out, got = after((back1[:2], got), [t[-1] for t in out])
    dx_came = [partner(p, sizes, 0, 1) for p in full(after(back1_out, got))]
    out = [jnp.concatenate(p, axis=5) for p in zip(*out)]
    out = parts_for(out, sizes, 2)
    dx = [list(t) for t in zip(full(back0[:2]), after(dx_came, out[0]))]
    dx = [parts_for(t, sizes, turn[1]) for t, turn in zip(dx, turns)]
    dx_sent = [sent for sent, _ in dx]

    index = np.arange(experts).reshape(sizes[2], sizes[1], 2).transpose(2, 1, 0).reshape(-1)
    where = jnp.asarray(np.argsort(index), jnp.int32)[me ^ jnp.arange(experts, dtype=jnp.int32)]
    score = jnp.stack(after([back0[6], back1[6]], dx_sent)).reshape(experts, dp, share)
    score = score[where][:, shares_at].reshape(experts, tok)
    scores = lax.all_to_all(score, "expert", split_axis=0, concat_axis=0, tiled=True).T
    named = expert_ids[:, :, None] == jnp.arange(experts, dtype=jnp.int32)[None, None, :]
    gate_part = jnp.sum(jnp.where(named, scores[:, None, :], 0.0), axis=2)
    gate_grads = gate_part
    for k in range(1, dp):
        gate_grads = gate_grads + partner(gate_part, sizes, 3, k)

    got = after(got, dx_sent)
    grad_sg = got[:, :units].reshape(experts * units, -1).T
    grad_su = got[:, units : 2 * units].reshape(experts * units, -1).T
    grad_sd = got[:, 2 * units :].reshape(experts * units, -1)
    out = fold(*out, sizes, 2, dx_sent)
    dx = [fold(*t, sizes, turn[1], out[1:], grad_sd) for t, turn in zip(dx, turns)]
    dx = [parts_for(t, sizes, turn[0]) for t, turn in zip(dx, turns)]
    dx_sent = [sent for sent, _ in dx]
    moe_out = both_halves(total(after(out, dx_sent)).reshape(share, width), sizes)
    dx = [fold(*t, sizes, turn[0]) for t, turn in zip(dx, turns)]
    dx = [jnp.concatenate(p, axis=5) for p in zip(*dx)]
    dx = parts_for(dx, sizes, 2)
    grad_wg, grad_wu, grad_wd = expert_grads(
        [ahead0[2], ahead1[2]],
        after([back0[2], back1[2]], dx[0]),
        [back0[3], back1[3]],
        [back0[4], back1[4]],
        [ahead0[5], ahead1[5]],
    )
    token_grads = both_halves(total(fold(*dx, sizes, 2, grad_wg)).reshape(share, width), sizes)
    grad_wg, grad_wu = grad_wg.swapaxes(1, 2), grad_wu.swapaxes(1, 2)
    return (moe_out, token_grads, gate_grads, grad_wg, grad_wu, grad_wd, grad_sg, grad_su, grad_sd)


def solution(mesh):
    row = P("expert", None)
    cols = P("expert", None, "dp")
    return jax.shard_map(
        local,
        mesh=mesh,
        in_specs=(
            row, row, row, cols, cols, P("expert", "dp", None),
            P(None, "dp"), P(None, "dp"), P("dp", None), row,
        ),
        out_specs=(
            row, row, row, cols, cols, P("expert", "dp", None),
            P("expert", "dp"), P("expert", "dp"), P("dp", "expert"),
        ),
        check_vma=False,
    )
```
